512 devices in a mesh: seq: 8 (over x, core), row: 8 (over z_lo), col: 8 (over y, z_hi).
Axes of the slice: x: 4, y: 4, z: 16 (z_hi: 2, z_lo: 8; z = z_hi * 8 + z_lo), core: 2. Of those that a mesh axis runs over, the one named last changes fastest.
Arguments:
- homolog_activations: bfloat16 [256, 512, 64], P(('seq', 'col'), 'row'), may hold values from -6 to 6
- alignment_token_ids: int32 [256, 512], P(('seq', 'col'), 'row'), may hold values from 0 to 79
- symbol_lookup_matrix: bfloat16 [80, 64], replicated, may hold values from -6 to 6
- homolog_rescale_vector: float32 [64], replicated, may hold values from 0.1 to 1.9
- first_operand_projection: bfloat16 [64, 32], replicated, may hold values from -0.75 to 0.75
- second_operand_projection: bfloat16 [64, 32], replicated, may hold values from -0.75 to 0.75
- outer_output_weight: bfloat16 [1024, 128], replicated, may hold values from -0.75 to 0.75
- outer_bias: float32 [128], replicated, may hold values from -3 to 3
- pair: bfloat16 [512, 512, 128], P('row', ('seq', 'col')), may hold values from -6 to 6
- pair_norm_gain: float32 [128], replicated, may hold values from 0.1 to 1.9
- pair_query_weight: bfloat16 [128, 128], replicated, as said below
- pair_key_weight: bfloat16 [128, 128], replicated, as said below
- pair_value_weight: bfloat16 [128, 128], replicated, may hold values from -0.5 to 0.5
- pair_gate_weight: bfloat16 [128, 128], replicated, may hold values from -0.5 to 0.5
- pair_output_weight: bfloat16 [128, 128], replicated, may hold values from -0.5 to 0.5
- nodes: bfloat16 [512, 64], P(('seq', 'col')), may hold values from -6 to 6
- coords: float32 [3, 512], P(None, ('seq', 'col')), may hold values from -18 to 18
- neighbour_index: int32 [512, 64], P(('seq', 'col')), may hold values from 0 to 511
- neighbour_count: int32 [512], P(('seq', 'col')), may hold values from 1 to 64, 20480 in all
- node_norm_gain: float32 [64], replicated, may hold values from 0.1 to 1.9
- node_query_weight: bfloat16 [64, 64], replicated, as said below
- node_key_weight: bfloat16 [64, 64], replicated, as said below
- node_value_weight: bfloat16 [64, 64], replicated, may hold values from -0.75 to 0.75
- node_output_weight: bfloat16 [64, 64], replicated, may hold values from -0.75 to 0.75
- distance_penalty: float32 [4], replicated, may hold values from 0.02 to 0.5
- coordinate_step: float32 [4], replicated, may hold values from -0.5 to 0.5
Outputs:
- pair_out: bfloat16 [512, 512, 128], P('row', ('seq', 'col'))
- nodes_out: bfloat16 [512, 64], P(('seq', 'col'))
- coords_out: float32 [3, 512], P(None, ('seq', 'col'))
The draws below stay inside these ranges and needn't reach their ends.
Inputs may be any that keep to these rules, and one draw needn't show every extreme that they name: `neighbour_index`: indices of residues; only the first neighbour_count[i] entries of row i are used. `pair_query_weight`: a projection matrix. `pair_key_weight`: a projection matrix. `node_query_weight`: a projection matrix. `node_key_weight`: a projection matrix.
All inputs are finite; a program needn't handle non-finite values. No bound on the sum of `neighbour_count` on one device may be relied on, other than what follows from the above.
Results may differ from the reference program's by a relative error of at most 0.02.
Values may be sent and summed in bfloat16 or wider, within the bound.
No kernel may reach another device: no remote copies, remote signals or barrier semaphores. Data moves between devices by JAX's collectives and lax.ppermute only.
A program may use at most 64 MiB of HBM per device.

```python
import math
from functools import partial
import jax
import jax.numpy as jnp
import numpy as np
from jax import lax

HOMOLOG_TOTAL = 256
CHAIN_LENGTH = 512
ROW_FEATURE_DIM = 64
AMINO_VOCABULARY = 80
PRODUCT_WIDTH = 32
C_PAIR = 128
PAIR_HEADS = 4
C_NODE = 64
NODE_HEADS = 4
K = 64


def draw_pair_query_weight(key, part):
    key = jax.random.fold_in(key, 11)
    return (jax.random.normal(key, (C_PAIR, C_PAIR), jnp.float32) * C_PAIR ** (-0.5)).astype(jnp.bfloat16)


def draw_pair_key_weight(key, part):
    key = jax.random.fold_in(key, 12)
    return (jax.random.normal(key, (C_PAIR, C_PAIR), jnp.float32) * C_PAIR ** (-0.5)).astype(jnp.bfloat16)


def draw_node_query_weight(key, part):
    key = jax.random.fold_in(key, 13)
    return (jax.random.normal(key, (C_NODE, C_NODE), jnp.float32) * C_NODE ** (-0.5)).astype(jnp.bfloat16)


def draw_node_key_weight(key, part):
    key = jax.random.fold_in(key, 14)
    return (jax.random.normal(key, (C_NODE, C_NODE), jnp.float32) * C_NODE ** (-0.5)).astype(jnp.bfloat16)


def plant(entries, own_key, low, high):
    longest = entries.shape.index(max(entries.shape))
    spots = []
    for shift in (0, 1):
        where = [jax.random.randint(jax.random.fold_in(own_key, axis), (), 0, length) for axis, length in enumerate(entries.shape)]
        where[longest] = (where[longest] + shift) % entries.shape[longest]
        spots.append(tuple(where))
    return entries.at[spots[0]].set(low).at[spots[1]].set(high)


def block_scale(stream_key, dims, split, least, largest):
    def one(dim, blocks):
        heights = jax.random.uniform(jax.random.fold_in(jax.random.fold_in(stream_key, 6), dim), (blocks,), jnp.float32, least / len(split), largest / len(split))
        return jnp.repeat(jnp.exp(heights), dims[dim] // blocks).reshape((-1,) + (1,) * (len(dims) - dim - 1))

    gain = one(*split[0])
    for cut in split[1:]:
        gain = gain * one(*cut)
    return gain


def split_up(number_of, total, most, lean):
    loads = [(1 << 20) // math.isqrt(grade ** lean) + 1 for grade in range(2, number_of + 1)]
    surplus, counts = total - most - (number_of - 1), [1] * (number_of - 1)
    while surplus > 0:
        free = [i for i in range(number_of - 1) if counts[i] < most]
        mass, remaining = sum([loads[i] for i in free]), surplus
        for i in free:
            extra = min(most - counts[i], max(1, remaining * loads[i] // mass), surplus)
            counts[i] = counts[i] + extra
            surplus = surplus - extra
    return np.array([most] + counts)


def ragged(key, number_of, total, most, skew):
    if number_of == 2:
        one = jax.random.randint(key, (), max(1, total - most), min(most, total - 1) + 1)
        return jnp.stack([one, total - one])
    sizes = jnp.asarray(split_up(number_of, total, most, skew), jnp.int32)
    pairs = (number_of - 1) // 2
    source_of, taker = sizes[1:1 + 2 * pairs:2], sizes[2:2 + 2 * pairs:2]
    slack = jnp.minimum(source_of - 1, most - taker)
    shifted = jax.random.randint(jax.random.fold_in(key, 1), (pairs,), 0, 1 << 20) % (slack + 1)
    sizes = sizes.at[1:1 + 2 * pairs:2].set(source_of - shifted).at[2:2 + 2 * pairs:2].set(taker + shifted)
    return sizes[jax.random.permutation(jax.random.fold_in(key, 2), number_of)]


def scatter_about(own_key, dims, deviation, bound, split=(), kind=jnp.bfloat16):
    drawn = deviation * jax.random.normal(own_key, dims, jnp.float32)
    if split:
        drawn = drawn * block_scale(own_key, dims, split, -0.22, 0.18)
    return jnp.clip(drawn, -bound, bound).astype(kind)


def setup_inputs(seed: int = 0) -> dict:
    arg_keys = jax.random.split(jax.random.key(seed), 27)
    homolog_activations = scatter_about(arg_keys[0], (HOMOLOG_TOTAL, CHAIN_LENGTH, ROW_FEATURE_DIM), 1.0, 6.0, ((0, 64), (1, 8)))
    alignment_token_ids = plant(jax.random.randint(arg_keys[1], (HOMOLOG_TOTAL, CHAIN_LENGTH), 0, AMINO_VOCABULARY), jax.random.fold_in(arg_keys[1], 1), 0, AMINO_VOCABULARY - 1).astype(jnp.int32)
    symbol_lookup_matrix = scatter_about(arg_keys[2], (AMINO_VOCABULARY, ROW_FEATURE_DIM), 1.0, 6.0)
    homolog_rescale_vector = jnp.clip(1.0 + 0.18 * jax.random.normal(arg_keys[3], (ROW_FEATURE_DIM,), jnp.float32), 0.1, 1.9)
    first_operand_projection = scatter_about(arg_keys[4], (ROW_FEATURE_DIM, PRODUCT_WIDTH), ROW_FEATURE_DIM ** -0.5, 0.75)
    second_operand_projection = scatter_about(arg_keys[5], (ROW_FEATURE_DIM, PRODUCT_WIDTH), ROW_FEATURE_DIM ** -0.5, 0.75)
    outer_output_weight = scatter_about(arg_keys[6], (PRODUCT_WIDTH * PRODUCT_WIDTH, C_PAIR), (2 * PRODUCT_WIDTH) ** -0.5, 0.75)
    outer_bias = scatter_about(arg_keys[7], (C_PAIR,), 0.5, 3.0, (), jnp.float32)
    pair = scatter_about(arg_keys[8], (CHAIN_LENGTH, CHAIN_LENGTH, C_PAIR), 1.0, 6.0, ((0, 8), (1, 64)))
    pair_norm_gain = jnp.clip(1.0 + 0.18 * jax.random.normal(arg_keys[9], (C_PAIR,), jnp.float32), 0.1, 1.9)
    pair_query_weight = draw_pair_query_weight(jax.random.fold_in(arg_keys[26], 71), 0)
    pair_key_weight = draw_pair_key_weight(jax.random.fold_in(arg_keys[26], 71), 0)
    pair_value_weight = scatter_about(arg_keys[12], (C_PAIR, C_PAIR), C_PAIR ** -0.5, 0.5)
    pair_gate_weight = scatter_about(arg_keys[13], (C_PAIR, C_PAIR), C_PAIR ** -0.5, 0.5)
    pair_output_weight = scatter_about(arg_keys[14], (C_PAIR, C_PAIR), C_PAIR ** -0.5, 0.5)
    nodes = scatter_about(arg_keys[15], (CHAIN_LENGTH, C_NODE), 1.0, 6.0, ((0, 64),))
    coords = scatter_about(arg_keys[16], (3, CHAIN_LENGTH), 3.0, 18.0, ((1, 64),), jnp.float32)
    neighbour_index = plant(jax.random.randint(arg_keys[17], (CHAIN_LENGTH, K), 0, CHAIN_LENGTH), jax.random.fold_in(arg_keys[17], 1), 0, CHAIN_LENGTH - 1).astype(jnp.int32)
    neighbour_count = ragged(arg_keys[18], CHAIN_LENGTH, CHAIN_LENGTH * K * 5 // 8, K, 2).astype(jnp.int32)
    node_norm_gain = jnp.clip(1.0 + 0.18 * jax.random.normal(arg_keys[19], (C_NODE,), jnp.float32), 0.1, 1.9)
    node_query_weight = draw_node_query_weight(jax.random.fold_in(arg_keys[26], 71), 0)
    node_key_weight = draw_node_key_weight(jax.random.fold_in(arg_keys[26], 71), 0)
    node_value_weight = scatter_about(arg_keys[22], (C_NODE, C_NODE), C_NODE ** -0.5, 0.75)
    node_output_weight = scatter_about(arg_keys[23], (C_NODE, C_NODE), C_NODE ** -0.5, 0.75)
    distance_penalty = jnp.clip(jnp.exp(jax.random.uniform(arg_keys[24], (NODE_HEADS,), jnp.float32, math.log(0.02), math.log(0.5))), 0.02, 0.5)
    coordinate_step = jnp.clip(jax.random.uniform(arg_keys[25], (NODE_HEADS,), jnp.float32, -0.5, 0.5), -0.5, 0.5)
    return {"homolog_activations": homolog_activations, "alignment_token_ids": alignment_token_ids, "symbol_lookup_matrix": symbol_lookup_matrix, "homolog_rescale_vector": homolog_rescale_vector, "first_operand_projection": first_operand_projection, "second_operand_projection": second_operand_projection, "outer_output_weight": outer_output_weight, "outer_bias": outer_bias, "pair": pair, "pair_norm_gain": pair_norm_gain, "pair_query_weight": pair_query_weight, "pair_key_weight": pair_key_weight, "pair_value_weight": pair_value_weight, "pair_gate_weight": pair_gate_weight, "pair_output_weight": pair_output_weight, "nodes": nodes, "coords": coords, "neighbour_index": neighbour_index, "neighbour_count": neighbour_count, "node_norm_gain": node_norm_gain, "node_query_weight": node_query_weight, "node_key_weight": node_key_weight, "node_value_weight": node_value_weight, "node_output_weight": node_output_weight, "distance_penalty": distance_penalty, "coordinate_step": coordinate_step}


def layer_normalize(values_in, gain_vec):
    average = lax.optimization_barrier(jnp.mean(values_in, -1, keepdims=True))
    centred = values_in - average
    variance = lax.optimization_barrier(jnp.mean(centred * centred, -1, keepdims=True))
    return centred * lax.rsqrt(variance + 1e-05) * gain_vec.astype(jnp.float32)

def attend_row(row_in, gain_vec, w_query, w_key, w_value, w_gate, w_out):
    length, channels = row_in.shape
    head_dim = channels // PAIR_HEADS
    normed = layer_normalize(row_in.astype(jnp.float32), gain_vec).astype(jnp.bfloat16)
    queries = jnp.dot(normed, w_query, preferred_element_type=jnp.float32).astype(jnp.bfloat16)
    keys_row = jnp.dot(normed, w_key, preferred_element_type=jnp.float32).astype(jnp.bfloat16)
    values_row = jnp.dot(normed, w_value, preferred_element_type=jnp.float32).astype(jnp.bfloat16)
    gates = jnp.dot(normed, w_gate, preferred_element_type=jnp.float32)
    queries = queries.reshape(length, PAIR_HEADS, head_dim).astype(jnp.float32)
    keys_row = keys_row.reshape(length, PAIR_HEADS, head_dim).astype(jnp.float32)
    values_row = values_row.reshape(length, PAIR_HEADS, head_dim).astype(jnp.float32)
    scores = jnp.einsum('qhd,khd->hqk', queries, keys_row) * head_dim ** (-0.5)
    weights = jax.nn.softmax(scores, axis=-1).astype(jnp.bfloat16)
    attended = jnp.einsum('hqk,khd->qhd', weights.astype(jnp.float32), values_row).reshape(length, channels)
    attended = (attended * jax.nn.sigmoid(gates)).astype(jnp.bfloat16)
    update = jnp.dot(attended, w_out, preferred_element_type=jnp.float32)
    return (row_in.astype(jnp.float32) + update).astype(jnp.bfloat16)

def reference(homolog_activations, alignment_token_ids, symbol_lookup_matrix, homolog_rescale_vector, first_operand_projection, second_operand_projection, outer_output_weight, outer_bias, pair, pair_norm_gain, pair_query_weight, pair_key_weight, pair_value_weight, pair_gate_weight, pair_output_weight, nodes, coords, neighbour_index, neighbour_count, node_norm_gain, node_query_weight, node_key_weight, node_value_weight, node_output_weight, distance_penalty, coordinate_step):
    alignment_input = homolog_activations.astype(jnp.float32) + symbol_lookup_matrix[alignment_token_ids].astype(jnp.float32)
    alignment_normed = layer_normalize(alignment_input, homolog_rescale_vector)
    left_factor = jnp.dot(alignment_normed, first_operand_projection, preferred_element_type=jnp.float32).astype(jnp.bfloat16)
    right_factor = jnp.dot(alignment_normed, second_operand_projection, preferred_element_type=jnp.float32).astype(jnp.bfloat16)
    block_rows = 16

    def outer_block(first_row):
        left_rows = lax.dynamic_slice_in_dim(left_factor, first_row, block_rows, 1).astype(jnp.float32)
        summed = jnp.einsum('sic,sjd->ijcd', left_rows, right_factor.astype(jnp.float32))
        outer = (summed / HOMOLOG_TOTAL).reshape(block_rows, CHAIN_LENGTH, PRODUCT_WIDTH * PRODUCT_WIDTH).astype(jnp.bfloat16)
        update = jnp.dot(outer, outer_output_weight, preferred_element_type=jnp.float32) + outer_bias
        pair_rows = lax.dynamic_slice_in_dim(pair, first_row, block_rows, 0).astype(jnp.float32)
        return (pair_rows + update).astype(jnp.bfloat16)
    starts = (jnp.arange(CHAIN_LENGTH // block_rows) * block_rows).astype(jnp.int32)
    pair_mid = lax.map(outer_block, starts).reshape(CHAIN_LENGTH, CHAIN_LENGTH, C_PAIR)
    pair_out = lax.map(partial(attend_row, gain_vec=pair_norm_gain, w_query=pair_query_weight, w_key=pair_key_weight, w_value=pair_value_weight, w_gate=pair_gate_weight, w_out=pair_output_weight), pair_mid)
    node_dim = C_NODE // NODE_HEADS
    node_norm = layer_normalize(nodes.astype(jnp.float32), node_norm_gain).astype(jnp.bfloat16)
    node_query = jnp.dot(node_norm, node_query_weight, preferred_element_type=jnp.float32).astype(jnp.bfloat16)
    node_key = jnp.dot(node_norm, node_key_weight, preferred_element_type=jnp.float32).astype(jnp.bfloat16)
    node_value = jnp.dot(node_norm, node_value_weight, preferred_element_type=jnp.float32).astype(jnp.bfloat16)
    near_key = node_key[neighbour_index].reshape(CHAIN_LENGTH, K, NODE_HEADS, node_dim).astype(jnp.float32)
    near_value = node_value[neighbour_index].reshape(CHAIN_LENGTH, K, NODE_HEADS, node_dim).astype(jnp.float32)
    near_pos = coords[:, neighbour_index]
    offsets = near_pos - coords[:, :, None]
    dist2 = lax.optimization_barrier(jnp.sum(offsets * offsets, 0))
    queries = node_query.reshape(CHAIN_LENGTH, NODE_HEADS, node_dim).astype(jnp.float32)
    logits = jnp.einsum('ihd,ikhd->ihk', queries, near_key) * node_dim ** (-0.5)
    logits = logits - distance_penalty[None, :, None] * dist2[:, None, :]
    is_valid = jnp.arange(K, dtype=jnp.int32)[None, :] < neighbour_count[:, None]
    logits = jnp.where(is_valid[:, None, :], logits, -1e+30)
    node_weight = jax.nn.softmax(logits, axis=-1)
    node_weight = jnp.where(is_valid[:, None, :], node_weight, 0.0)
    weight_low = node_weight.astype(jnp.bfloat16).astype(jnp.float32)
    node_mix = jnp.einsum('ihk,ikhd->ihd', weight_low, near_value).reshape(CHAIN_LENGTH, C_NODE).astype(jnp.bfloat16)
    nodes_out = (nodes.astype(jnp.float32) + jnp.dot(node_mix, node_output_weight, preferred_element_type=jnp.float32)).astype(jnp.bfloat16)
    coord_pull = lax.optimization_barrier(jnp.sum(node_weight * coordinate_step[None, :, None], 1))
    coords_out = coords + lax.optimization_barrier(jnp.sum(offsets * coord_pull[None], -1))
    return (pair_out, nodes_out, coords_out)
```

```python
import math

import jax
import jax.numpy as jnp
from jax import lax
from jax.experimental import pallas as pl
from jax.experimental.pallas import tpu as pltpu
from jax.sharding import Mesh, PartitionSpec as P

F32 = jnp.float32
BF16 = jnp.bfloat16
PAIR_HEADS = 4
NODE_HEADS = 4
PLANE = ("x", "core", "y")
GROUP = ("x", "core", "y", "zh")
VMEM_LIMIT = 48 * 1024 * 1024


def dot(a, b, ca=1, cb=0):
    return lax.dot_general(a, b, (((ca,), (cb,)), ((), ())), preferred_element_type=F32)


def iota(shape, dim):
    return lax.broadcasted_iota(jnp.int32, shape, dim)


def one_where(mask):
    return jnp.where(mask, 1.0, 0.0).astype(BF16)


def layer_normalize(values_in, gain):
    average = jnp.mean(values_in, -1, keepdims=True)
    centred = values_in - average
    variance = jnp.mean(centred * centred, -1, keepdims=True)
    return centred * lax.rsqrt(variance + 1e-05) * gain


def msa_kernel(
    act_ref, tok_ref, emb_ref, gain_ref, wl_ref, wr_ref, left_ref, right_ref
):
    seqs, length, _ = act_ref.shape
    kinds = emb_ref.shape[0]
    emb = emb_ref[...]
    rows = []
    for s in range(seqs):
        picked = one_where(iota((kinds, length), 0) == tok_ref[s : s + 1, :])
        rows.append(act_ref[s].astype(F32) + dot(picked, emb, 0, 0))
    normed = layer_normalize(jnp.concatenate(rows, 0), gain_ref[...]).astype(BF16)

    left = dot(wl_ref[...], normed, 0, 1).astype(BF16).astype(F32)
    low = iota((16, 128), 1) < 64
    parts = []
    for p in range(2):
        a0 = left[0:16, p * 128 : (p + 1) * 128]
        a1 = left[16:32, p * 128 : (p + 1) * 128]
        parts.append(jnp.where(low, a0, pltpu.roll(a1, 64, 1)))
        parts.append(jnp.where(low, pltpu.roll(a0, 64, 1), a1))
    block = jnp.concatenate(parts, 0).astype(BF16)
    left_ref[...] = jnp.broadcast_to(block[None], left_ref.shape)

    out_row, source = iota((256, 256), 0), iota((256, 256), 1)
    wanted = (out_row % 4) * 64 + ((out_row % 64) // 4) * 4 + out_row // 64
    moved = dot(one_where(source == wanted), normed).astype(BF16)
    right = jnp.zeros((64, 128), F32)
    for j in range(4):
        place = one_where(iota((32, 128), 1) == iota((32, 128), 0) + 32 * j)
        widened = dot(wr_ref[...], place).astype(BF16)
        right = right + dot(moved[j * 64 : (j + 1) * 64], widened)
    right = right.astype(BF16).reshape(4, 16, 128)
    for a in range(8):
        right_ref[a * 4 : (a + 1) * 4] = right


def node_project_kernel(nodes_ref, coords_ref, gain_ref, wq_ref, wk_ref, wv_ref, slot_ref, query_ref):
    normed = layer_normalize(nodes_ref[...].astype(F32), gain_ref[...]).astype(BF16)
    query_ref[...] = dot(wq_ref[...], normed, 0, 1).astype(BF16).astype(F32)
    width = wk_ref.shape[1]
    row, lane = iota((width, 128), 0), iota((width, 128), 1)
    kv = dot(normed, dot(wk_ref[...], one_where(lane == row)).astype(BF16))
    kv = kv + dot(normed, dot(wv_ref[...], one_where(lane == row + width)).astype(BF16))
    rest = coords_ref[...]
    placed = jnp.zeros((8, 128), F32)
    for part in range(3):
        piece = rest.astype(BF16)
        rest = rest - piece.astype(F32)
        spot = one_where(iota((3, 128), 1) == iota((3, 128), 0) * 3 + part)
        placed = placed + dot(piece, spot, 0, 0)
    slot_ref[...] = jnp.concatenate([kv, placed], 0).astype(BF16)


def outer_kernel(
    half_ref, left_in, right_in, pair_ref, weight_ref, bias_ref, slot_ref, out_ref, left, right, joined, update
):
    turn = one_where(
        iota((256, 256), 1) == (iota((256, 256), 0) % 16) * 16 + iota((256, 256), 0) // 16
    )
    for g in range(8):
        part = dot(turn, left_in[g * 4 : (g + 1) * 4].reshape(256, 128)).astype(BF16)
        for q in range(16):
            left[g * 16 : (g + 1) * 16, q * 128 : (q + 1) * 128] = part[q * 16 : (q + 1) * 16]
    row = iota((256, 256), 0)
    turn = one_where(
        iota((256, 256), 1) == ((row % 64) // 4) * 16 + (row // 64) * 4 + row % 4
    )
    for g in range(2):
        part = dot(turn, right_in[g * 16 : (g + 1) * 16].reshape(256, 128)).astype(BF16)
        for q in range(4):
            right[g * 64 : (g + 1) * 64, q * 128 : (q + 1) * 128] = part[q * 64 : (q + 1) * 64]

    lane = iota((128, 128), 1)
    low, even = lane < 64, (lane // 32) % 2 == 0
    scale = 1.0 / 256.0
    for e in range(4):
        products = [
            dot(left[:, (4 * e + k) * 128 : (4 * e + k + 1) * 128], right[...], 0, 0) * scale
            for k in range(4)
        ]
        for jq in range(4):
            v0, v1, v2, v3 = [p[:, jq * 128 : (jq + 1) * 128] for p in products]
            t0 = jnp.where(low, v0, pltpu.roll(v2, 64, 1))
            t2 = jnp.where(low, pltpu.roll(v0, 64, 1), v2)
            t1 = jnp.where(low, v1, pltpu.roll(v3, 64, 1))
            t3 = jnp.where(low, pltpu.roll(v1, 64, 1), v3)
            a = [
                jnp.where(even, t0, pltpu.roll(t1, 32, 1)),
                jnp.where(even, pltpu.roll(t0, 96, 1), t1),
                jnp.where(even, t2, pltpu.roll(t3, 32, 1)),
                jnp.where(even, pltpu.roll(t2, 96, 1), t3),
            ]
            for j in range(4):
                block = a[j].astype(BF16)
                at = (jq * 4 + j) * 64
                joined[at : at + 64, e * 128 : (e + 1) * 128] = block[:64]
                joined[at : at + 64, (4 + e) * 128 : (5 + e) * 128] = block[64:]
    for j in range(16):
        update[:, j, :] = dot(joined[j * 64 : (j + 1) * 64], weight_ref[...])
    own = pl.multiple_of(half_ref[0] * 8, 8)
    update[:, pl.ds(own, 8), :] += pair_ref[...].astype(F32) + bias_ref[...].reshape(1, 1, 128)
    out_ref[:, 0:16, :] = update[...].astype(BF16)
    out_ref[:, 16:32, :] = jnp.broadcast_to(slot_ref[...][None], (64, 16, 128))


def attend_kernel(got_ref, gain_ref, wq_ref, wk_ref, wv_ref, wg_ref, wo_ref, out_ref, q_s, k_s, v_s, mid_s, gate_s):
    both = got_ref[:, 0:16, :].astype(F32).reshape(32, 2, 16, 128)
    pair_mid = (both[:, 0] + both[:, 1]).reshape(512, 128).astype(BF16).astype(F32)
    mid_s[...] = pair_mid
    normed = layer_normalize(pair_mid, gain_ref[...]).astype(BF16)
    q_s[...] = dot(normed, wq_ref[...]).astype(BF16)
    k_s[...] = dot(normed, wk_ref[...]).astype(BF16)
    v_s[...] = dot(normed, wv_ref[...]).astype(BF16)
    gate_s[...] = dot(normed, wg_ref[...])
    factor = 32 ** (-0.5) * math.log2(math.e)
    head_of = iota((512, 128), 1) // 32
    keys, values = k_s[...], v_s[...]
    zero, one = jnp.zeros((512, 128), BF16), jnp.ones((512, 128), BF16)
    head_keys = [jnp.where(head_of == h, keys, zero) for h in range(PAIR_HEADS)]
    head_values = [
        jnp.concatenate(
            [jnp.where(head_of == h, values, zero), jnp.where(head_of == h, one, zero)], 1
        )
        for h in range(PAIR_HEADS)
    ]
    for c in range(4):
        at = slice(c * 128, (c + 1) * 128)
        queries = q_s[at, :]
        total = jnp.zeros((128, 256), F32)
        for h in range(PAIR_HEADS):
            scores = dot(queries, head_keys[h], 1, 1)
            top = jnp.max(scores, -1, keepdims=True)
            weights = jnp.exp2((scores - top) * factor).astype(BF16)
            total = total + dot(weights, head_values[h])
        attended = total[:, :128] / total[:, 128:] * jax.nn.sigmoid(gate_s[at, :])
        result = mid_s[at, :] + dot(attended.astype(BF16), wo_ref[...])
        out_ref[c * 16 : (c + 1) * 16] = result.astype(BF16).reshape(16, 8, 128)


def node_kernel(
    count_ref, got_ref, index_ref, query_ref, nodes_ref, coords_ref, wo_ref, penalty_ref, step_ref, nodes_out, coords_out
):
    table = got_ref[:, 16:32, :].reshape(64, 2, 8, 128)
    kv_table = table[:, 0].reshape(512, 128)
    place_table = table[:, 1].reshape(512, 128)
    local, slots = index_ref.shape
    width, dim = nodes_ref.shape[1], nodes_ref.shape[1] // NODE_HEADS
    lane = iota((1, slots), 1)
    spot = iota((1, local), 1)
    mixed = jnp.zeros((width, local), F32)
    moved = jnp.zeros((3, local), F32)
    for i in range(local):
        picked = one_where(iota((512, slots), 0) == index_ref[i : i + 1, :])
        near = dot(kv_table, picked, 0, 0)
        where = dot(place_table, picked, 0, 0)
        position = [
            where[3 * c : 3 * c + 1] + where[3 * c + 1 : 3 * c + 2] + where[3 * c + 2 : 3 * c + 3]
            for c in range(3)
        ]
        offsets = jnp.concatenate(position, 0) - coords_ref[:, i : i + 1]
        dist2 = jnp.sum(offsets * offsets, 0, keepdims=True)
        products = near[:width] * query_ref[:, i : i + 1]
        logits = jnp.sum(products.reshape(NODE_HEADS, dim, slots), 1) * dim ** (-0.5)
        logits = logits - penalty_ref[...] * dist2
        valid = lane < count_ref[i]
        logits = jnp.where(valid, logits, -1e30)
        powers = jnp.exp(logits - jnp.max(logits, -1, keepdims=True))
        weight = powers / jnp.sum(powers, -1, keepdims=True)
        weight = jnp.where(valid, weight, 0.0)
        low = weight.astype(BF16).astype(F32)
        spread = jnp.broadcast_to(low[:, None, :], (NODE_HEADS, dim, slots)).reshape(width, slots)
        column = jnp.sum(near[width:] * spread, -1, keepdims=True)
        mixed = mixed + jnp.where(spot == i, column, 0.0)
        pull = jnp.sum(weight * step_ref[...], 0, keepdims=True)
        moved = moved + jnp.where(spot == i, jnp.sum(offsets * pull, -1, keepdims=True), 0.0)
    out = nodes_ref[...].astype(F32) + dot(mixed.astype(BF16), wo_ref[...], 0, 0)
    nodes_out[...] = out.astype(BF16)
    coords_out[...] = coords_ref[...] + moved


def call(body, out_shape, args, scratch=(), scalars=0, cost=None):
    spaces = [pltpu.SMEM] * scalars + [pltpu.VMEM] * (len(args) - scalars)
    out_specs = jax.tree.map(lambda _: pl.BlockSpec(memory_space=pltpu.VMEM), out_shape)
    return pl.pallas_call(
        body,
        out_shape=out_shape,
        in_specs=[pl.BlockSpec(memory_space=s) for s in spaces],
        out_specs=out_specs,
        scratch_shapes=list(scratch),
        compiler_params=pltpu.CompilerParams(vmem_limit_bytes=VMEM_LIMIT),
        cost_estimate=cost,
    )(*args)


def shape(dims, kind=BF16):
    return jax.ShapeDtypeStruct(dims, kind)


def on_device(
    homolog_activations,
    alignment_token_ids,
    symbol_lookup_matrix,
    homolog_rescale_vector,
    first_operand_projection,
    second_operand_projection,
    outer_output_weight,
    outer_bias,
    pair,
    pair_norm_gain,
    pair_query_weight,
    pair_key_weight,
    pair_value_weight,
    pair_gate_weight,
    pair_output_weight,
    nodes,
    coords,
    neighbour_index,
    neighbour_count,
    node_norm_gain,
    node_query_weight,
    node_key_weight,
    node_value_weight,
    node_output_weight,
    distance_penalty,
    coordinate_step,
):
    left, right = call(
        msa_kernel,
        (shape((32, 64, 128)), shape((32, 16, 128))),
        (
            homolog_activations,
            alignment_token_ids,
            symbol_lookup_matrix,
            homolog_rescale_vector.reshape(1, -1),
            first_operand_projection,
            second_operand_projection,
        ),
    )
    right = lax.all_to_all(right, PLANE, split_axis=0, concat_axis=0, tiled=True)
    left, right = lax.optimization_barrier((left, right))
    across = [(a * 8 + r, r * 8 + a) for a in range(8) for r in range(8)]
    right = lax.ppermute(right, ("x", "core", "row"), across)
    left = lax.all_to_all(left, PLANE, split_axis=0, concat_axis=0, tiled=True)
    slot, node_query = call(
        node_project_kernel,
        (shape((16, 128)), shape((64, 8), F32)),
        (
            nodes,
            coords,
            node_norm_gain.reshape(1, -1),
            node_query_weight,
            node_key_weight,
            node_value_weight,
        ),
    )
    partial_rows = call(
        outer_kernel,
        shape((64, 32, 128)),
        (
            lax.axis_index("zh").reshape(1).astype(jnp.int32),
            left,
            right,
            pair,
            outer_output_weight,
            outer_bias.reshape(1, -1),
            slot,
        ),
        scratch=(
            pltpu.VMEM((128, 2048), BF16),
            pltpu.VMEM((128, 512), BF16),
            pltpu.VMEM((1024, 1024), BF16),
            pltpu.VMEM((64, 16, 128), F32),
        ),
        scalars=1,
    )
    got = lax.all_to_all(partial_rows, GROUP, split_axis=0, concat_axis=0, tiled=True)
    row = call(
        attend_kernel,
        shape((64, 8, 128)),
        (
            got,
            pair_norm_gain.reshape(1, -1),
            pair_query_weight,
            pair_key_weight,
            pair_value_weight,
            pair_gate_weight,
            pair_output_weight,
        ),
        scratch=(
            pltpu.VMEM((512, 128), BF16),
            pltpu.VMEM((512, 128), BF16),
            pltpu.VMEM((512, 128), BF16),
            pltpu.VMEM((512, 128), F32),
            pltpu.VMEM((512, 128), F32),
        ),
    )
    pair_out = lax.all_to_all(row, GROUP, split_axis=0, concat_axis=0, tiled=True)
    nodes_out, coords_out = call(
        node_kernel,
        (shape(nodes.shape), shape(coords.shape, F32)),
        (
            neighbour_count,
            got,
            neighbour_index,
            node_query,
            nodes,
            coords,
            node_output_weight,
            distance_penalty.reshape(-1, 1),
            coordinate_step.reshape(-1, 1),
        ),
        scalars=1,
    )
    return (pair_out, nodes_out, coords_out)


def solution(mesh):
    fine = Mesh(mesh.devices.reshape(4, 2, 8, 4, 2), ("x", "core", "row", "y", "zh"))
    placed = (
        P(GROUP, "row", None),
        P(GROUP, "row"),
        P(),
        P(),
        P(),
        P(),
        P(),
        P(),
        P("row", GROUP, None),
        P(),
        P(),
        P(),
        P(),
        P(),
        P(),
        P(GROUP, None),
        P(None, GROUP),
        P(GROUP, None),
        P(GROUP),
        P(),
        P(),
        P(),
        P(),
        P(),
        P(),
        P(),
    )
    return jax.shard_map(
        on_device,
        mesh=fine,
        in_specs=placed,
        out_specs=(
            P("row", GROUP, None),
            P(GROUP, None),
            P(None, GROUP),
        ),
        check_vma=False,
    )
```

```python
import math

import jax
import jax.numpy as jnp
from jax import lax
from jax.experimental import pallas as pl
from jax.experimental.pallas import tpu as pltpu
from jax.sharding import Mesh, PartitionSpec as P

F32 = jnp.float32
BF16 = jnp.bfloat16
PAIR_HEADS = 4
NODE_HEADS = 4
PLANE = ("x", "core", "y")
GROUP = ("x", "core", "y", "zh")
VMEM_LIMIT = 48 * 1024 * 1024


def dot(a, b, ca=1, cb=0):
    return lax.dot_general(a, b, (((ca,), (cb,)), ((), ())), preferred_element_type=F32)


def iota(shape, dim):
    return lax.broadcasted_iota(jnp.int32, shape, dim)


def one_where(mask):
    return jnp.where(mask, 1.0, 0.0).astype(BF16)


def layer_normalize(values_in, gain):
    average = jnp.mean(values_in, -1, keepdims=True)
    centred = values_in - average
    variance = jnp.mean(centred * centred, -1, keepdims=True)
    return centred * lax.rsqrt(variance + 1e-05) * gain


def swap_lane_groups(v, low, even):
    t0 = jnp.where(low, v[0], pltpu.roll(v[2], 64, 1))
    t2 = jnp.where(low, pltpu.roll(v[0], 64, 1), v[2])
    t1 = jnp.where(low, v[1], pltpu.roll(v[3], 64, 1))
    t3 = jnp.where(low, pltpu.roll(v[1], 64, 1), v[3])
    return (
        jnp.where(even, t0, pltpu.roll(t1, 32, 1)),
        jnp.where(even, pltpu.roll(t0, 96, 1), t1),
        jnp.where(even, t2, pltpu.roll(t3, 32, 1)),
        jnp.where(even, pltpu.roll(t2, 96, 1), t3),
    )


def lane_masks(rows):
    lane = iota((rows, 128), 1)
    return lane < 64, (lane // 32) % 2 == 0


def first_kernel(
    half_ref,
    act_ref,
    tok_ref,
    emb_ref,
    gain_ref,
    pair_ref,
    nodes_ref,
    coords_ref,
    node_gain_ref,
    wq_ref,
    wk_ref,
    wv_ref,
    swap_ref,
    normed_ref,
    slot_ref,
    query_ref,
):
    seqs, length, _ = act_ref.shape
    kinds = emb_ref.shape[0]
    emb = emb_ref[...]
    rows = []
    for s in range(seqs):
        picked = one_where(iota((kinds, length), 0) == tok_ref[s : s + 1, :])
        rows.append(act_ref[s].astype(F32) + dot(picked, emb, 0, 0))
    normed = layer_normalize(jnp.concatenate(rows, 0), gain_ref[...]).astype(BF16)
    normed_ref[...] = normed
    row, lane = iota((64, 128), 0), iota((64, 128), 1)
    packed = dot(normed[:128], one_where(lane == row)) + dot(normed[128:], one_where(lane == row + 64))
    swap_ref[0:128] = packed.astype(BF16)
    swap_ref[128:384] = pair_ref[:, 1 - half_ref[0]].reshape(256, 128)

    normed = layer_normalize(nodes_ref[...].astype(F32), node_gain_ref[...]).astype(BF16)
    query_ref[...] = dot(wq_ref[...], normed, 0, 1).astype(BF16).astype(F32)
    kv = dot(normed, dot(wk_ref[...], one_where(lane == row)).astype(BF16))
    kv = kv + dot(normed, dot(wv_ref[...], one_where(lane == row + 64)).astype(BF16))
    rest = coords_ref[...]
    placed = jnp.zeros((8, 128), F32)
    for part in range(3):
        piece = rest.astype(BF16)
        rest = rest - piece.astype(F32)
        spot = one_where(iota((3, 128), 1) == iota((3, 128), 0) * 3 + part)
        placed = placed + dot(piece, spot, 0, 0)
    slot = jnp.concatenate([kv, placed], 0).astype(BF16)
    slot_ref[...] = slot
    swap_ref[384:400] = slot


def spread_kernel(half_ref, normed_ref, slot_ref, pair_ref, got_ref, wl_ref, wr_ref, out_ref):
    half = half_ref[0]
    mine = half == 0
    row, lane = iota((128, 64), 0), iota((128, 64), 1)
    packed = got_ref[0:128]
    theirs = jnp.concatenate(
        [dot(packed, one_where(row == lane)), dot(packed, one_where(row == lane + 64))], 0
    )
    own = normed_ref[...].astype(F32)
    planes = [
        jnp.where(mine, own, theirs).astype(BF16),
        jnp.where(mine, theirs, own).astype(BF16),
    ]

    row, source = iota((128, 256), 0), iota((128, 256), 1)
    pick = one_where(source == (row // 32) * 64 + (row % 32) * 2 + half)
    low, even = lane_masks(8)
    parts = []
    for p in range(2):
        rows = dot(pick, planes[p]).astype(BF16)
        left = dot(wl_ref[...], rows, 0, 1).astype(BF16).astype(F32)
        parts += swap_lane_groups([left[k * 8 : (k + 1) * 8] for k in range(4)], low, even)
    block = jnp.concatenate(parts, 0).astype(BF16)
    out_ref[:, 0:64] = jnp.broadcast_to(block[None], (32, 64, 128))

    first = iota((32, 16, 128), 1) // 8 == half
    kept = pair_ref[:, half].astype(F32)
    came = got_ref[128:384].reshape(32, 8, 128).astype(F32)
    kept = jnp.concatenate([kept, kept], 1)
    came = jnp.concatenate([came, came], 1)
    out_ref[:, 64:80] = jnp.where(first, kept, came).astype(BF16)

    own, theirs = slot_ref[...].astype(F32), got_ref[384:400].astype(F32)
    one = jnp.where(mine, own, theirs)
    two = jnp.where(mine, theirs, own)
    kv = jnp.concatenate([one[:8], two[:8]], 0).astype(BF16)
    out_ref[:, 80:96] = jnp.broadcast_to(kv[None], (32, 16, 128))

    place = jnp.concatenate([one[8:], two[8:]], 0)
    widened = dot(wr_ref[...], one_where(iota((32, 128), 1) == iota((32, 128), 0) + 32)).astype(BF16)
    both = jnp.concatenate(planes, 0)
    for g in range(4):
        row, source = iota((128, 512), 0) + g * 128, iota((128, 512), 1)
        wanted = ((row // 8) % 2) * 256 + ((row // 2) % 4) * 64 + (row // 16) * 2 + row % 2
        moved = dot(one_where(source == wanted), both).astype(BF16)
        right = dot(moved, widened).reshape(8, 16, 128) + place[None]
        out_ref[g * 8 : (g + 1) * 8, 96:112] = right.astype(BF16)


def right_kernel(got_ref, out_ref):
    rows = got_ref[:, 96:112].reshape(512, 128)
    row, source = iota((128, 512), 0), iota((128, 512), 1)
    start = (row // 4) * 16 + (row % 4) * 2
    at, lane = iota((128, 128), 0), iota((128, 128), 1)
    total = jnp.zeros((128, 128), F32)
    for plane in range(2):
        for column in range(2):
            picked = dot(one_where(source == start + plane * 8 + column), rows).astype(BF16)
            shift = (plane * 2 + column) * 32
            keep = (lane >= shift) & (lane < shift + 32)
            total = total + dot(picked, one_where((at + shift == lane + 32) & keep))
    out_ref[...] = jnp.broadcast_to(total.astype(BF16)[None], out_ref.shape)


def outer_kernel(got_ref, right_in, weight_ref, out_ref, left, right, joined, weight, update):
    row = iota((256, 256), 0)
    wanted = ((row // 4) % 4) * 64 + ((row // 16) % 2) * 32 + (row % 4) * 8 + row // 32
    turn = one_where(iota((256, 256), 1) == wanted)
    for g in range(8):
        part = dot(turn, got_ref[g * 4 : (g + 1) * 4, 0:64].reshape(256, 128)).astype(BF16)
        for q in range(8):
            for p in range(2):
                at = p * 128 + g * 16
                left[at : at + 16, q * 128 : (q + 1) * 128] = part[q * 32 + p * 16 : q * 32 + p * 16 + 16]
    low, even = lane_masks(128)
    for t in range(4):
        a, b = right_in[2 * t].astype(F32), right_in[2 * t + 1].astype(F32)
        right[0:128, t * 128 : (t + 1) * 128] = jnp.where(low, a, pltpu.roll(b, 64, 1)).astype(BF16)
        right[128:256, t * 128 : (t + 1) * 128] = jnp.where(low, pltpu.roll(a, 64, 1), b).astype(BF16)
    for q in range(8):
        for k in range(4):
            at = (k * 8 + q) * 32
            weight[q * 128 + k * 32 : q * 128 + k * 32 + 32] = weight_ref[at : at + 32]

    low, even = lane_masks(32)
    scale = 1.0 / 256.0
    for q in range(8):
        product = dot(left[:, q * 128 : (q + 1) * 128], right[...], 0, 0) * scale
        for t in range(4):
            tile = product[:, t * 128 : (t + 1) * 128]
            blocks = swap_lane_groups([tile[k * 32 : (k + 1) * 32] for k in range(4)], low, even)
            for j in range(4):
                at = (t * 4 + j) * 32
                joined[at : at + 32, q * 128 : (q + 1) * 128] = blocks[j].astype(BF16)
    for j in range(0, 16, 4):
        rows = dot(joined[j * 32 : (j + 4) * 32], weight[...])
        for k in range(4):
            update[:, j + k, :] = rows[k * 32 : (k + 1) * 32]
    out_ref[...] = update[...].astype(BF16)


def attend_kernel(
    update_ref, got_ref, bias_ref, gain_ref, wq_ref, wk_ref, wv_ref, wg_ref, wo_ref, out_ref, q_s, k_s, v_s, mid_s, gate_s
):
    row = iota((512, 512), 0)
    wanted = ((row // 2) % 32) * 16 + (row // 64) * 2 + row % 2
    turn = one_where(iota((512, 512), 1) == wanted)
    pair_mid = dot(turn, update_ref[...].reshape(512, 128))
    pair_mid = pair_mid + got_ref[:, 64:80].reshape(512, 128).astype(F32) + bias_ref[...]
    pair_mid = pair_mid.astype(BF16).astype(F32)
    mid_s[...] = pair_mid
    normed = layer_normalize(pair_mid, gain_ref[...]).astype(BF16)
    q_s[...] = dot(normed, wq_ref[...]).astype(BF16)
    k_s[...] = dot(normed, wk_ref[...]).astype(BF16)
    v_s[...] = dot(normed, wv_ref[...]).astype(BF16)
    gate_s[...] = dot(normed, wg_ref[...])
    factor = 32 ** (-0.5) * math.log2(math.e)
    head_of = iota((512, 128), 1) // 32
    keys, values = k_s[...], v_s[...]
    zero, one = jnp.zeros((512, 128), BF16), jnp.ones((512, 128), BF16)
    head_keys = [jnp.where(head_of == h, keys, zero) for h in range(PAIR_HEADS)]
    head_values = [
        jnp.concatenate(
            [jnp.where(head_of == h, values, zero), jnp.where(head_of == h, one, zero)], 1
        )
        for h in range(PAIR_HEADS)
    ]
    for c in range(4):
        at = slice(c * 128, (c + 1) * 128)
        queries = q_s[at, :]
        total = jnp.zeros((128, 256), F32)
        for h in range(PAIR_HEADS):
            scores = dot(queries, head_keys[h], 1, 1)
            top = jnp.max(scores, -1, keepdims=True)
            weights = jnp.exp2((scores - top) * factor).astype(BF16)
            total = total + dot(weights, head_values[h])
        attended = total[:, :128] / total[:, 128:] * jax.nn.sigmoid(gate_s[at, :])
        result = mid_s[at, :] + dot(attended.astype(BF16), wo_ref[...])
        out_ref[c * 16 : (c + 1) * 16] = result.astype(BF16).reshape(16, 8, 128)


def node_kernel(
    count_ref, got_ref, index_ref, query_ref, nodes_ref, coords_ref, wo_ref, penalty_ref, step_ref, nodes_out, coords_out
):
    kv_table = got_ref[:, 80:96].reshape(512, 128)
    place_table = got_ref[:, 96:112].reshape(512, 128)
    local, slots = index_ref.shape
    width, dim = nodes_ref.shape[1], nodes_ref.shape[1] // NODE_HEADS
    lane = iota((1, slots), 1)
    spot = iota((1, local), 1)
    mixed = jnp.zeros((width, local), F32)
    moved = jnp.zeros((3, local), F32)
    for i in range(local):
        picked = one_where(iota((512, slots), 0) == index_ref[i : i + 1, :])
        near = dot(kv_table, picked, 0, 0)
        where = dot(place_table, picked, 0, 0)
        position = [
            where[3 * c : 3 * c + 1] + where[3 * c + 1 : 3 * c + 2] + where[3 * c + 2 : 3 * c + 3]
            for c in range(3)
        ]
        offsets = jnp.concatenate(position, 0) - coords_ref[:, i : i + 1]
        dist2 = jnp.sum(offsets * offsets, 0, keepdims=True)
        products = near[:width] * query_ref[:, i : i + 1]
        logits = jnp.sum(products.reshape(NODE_HEADS, dim, slots), 1) * dim ** (-0.5)
        logits = logits - penalty_ref[...] * dist2
        valid = lane < count_ref[i]
        logits = jnp.where(valid, logits, -1e30)
        powers = jnp.exp(logits - jnp.max(logits, -1, keepdims=True))
        weight = powers / jnp.sum(powers, -1, keepdims=True)
        weight = jnp.where(valid, weight, 0.0)
        low = weight.astype(BF16).astype(F32)
        spread = jnp.broadcast_to(low[:, None, :], (NODE_HEADS, dim, slots)).reshape(width, slots)
        column = jnp.sum(near[width:] * spread, -1, keepdims=True)
        mixed = mixed + jnp.where(spot == i, column, 0.0)
        pull = jnp.sum(weight * step_ref[...], 0, keepdims=True)
        moved = moved + jnp.where(spot == i, jnp.sum(offsets * pull, -1, keepdims=True), 0.0)
    out = nodes_ref[...].astype(F32) + dot(mixed.astype(BF16), wo_ref[...], 0, 0)
    nodes_out[...] = out.astype(BF16)
    coords_out[...] = coords_ref[...] + moved


def call(body, out_shape, args, scratch=(), scalars=0, cost=None):
    spaces = [pltpu.SMEM] * scalars + [pltpu.VMEM] * (len(args) - scalars)
    out_specs = jax.tree.map(lambda _: pl.BlockSpec(memory_space=pltpu.VMEM), out_shape)
    return pl.pallas_call(
        body,
        out_shape=out_shape,
        in_specs=[pl.BlockSpec(memory_space=s) for s in spaces],
        out_specs=out_specs,
        scratch_shapes=list(scratch),
        compiler_params=pltpu.CompilerParams(vmem_limit_bytes=VMEM_LIMIT),
        cost_estimate=cost,
    )(*args)


def shape(dims, kind=BF16):
    return jax.ShapeDtypeStruct(dims, kind)


def on_device(
    homolog_activations,
    alignment_token_ids,
    symbol_lookup_matrix,
    homolog_rescale_vector,
    first_operand_projection,
    second_operand_projection,
    outer_output_weight,
    outer_bias,
    pair,
    pair_norm_gain,
    pair_query_weight,
    pair_key_weight,
    pair_value_weight,
    pair_gate_weight,
    pair_output_weight,
    nodes,
    coords,
    neighbour_index,
    neighbour_count,
    node_norm_gain,
    node_query_weight,
    node_key_weight,
    node_value_weight,
    node_output_weight,
    distance_penalty,
    coordinate_step,
):
    half = lax.axis_index("zh").reshape(1).astype(jnp.int32)
    by_parity = pair.reshape(32, 2, 8, 128)
    swap, normed, slot, node_query = call(
        first_kernel,
        (shape((400, 128)), shape((256, 64)), shape((16, 128)), shape((64, 8), F32)),
        (
            half,
            homolog_activations,
            alignment_token_ids,
            symbol_lookup_matrix,
            homolog_rescale_vector.reshape(1, -1),
            by_parity,
            nodes,
            coords,
            node_norm_gain.reshape(1, -1),
            node_query_weight,
            node_key_weight,
            node_value_weight,
        ),
        scalars=1,
    )
    swapped = lax.ppermute(swap, "zh", [(0, 1), (1, 0)])
    spread = call(
        spread_kernel,
        shape((32, 112, 128)),
        (
            half,
            normed,
            slot,
            by_parity,
            swapped,
            first_operand_projection,
            second_operand_projection,
        ),
        scalars=1,
    )
    got = lax.all_to_all(spread, PLANE, split_axis=0, concat_axis=0, tiled=True)
    right = call(right_kernel, shape((8, 128, 128)), (got,))
    right = lax.all_to_all(right, "row", split_axis=0, concat_axis=0, tiled=True)
    update = call(
        outer_kernel,
        shape((32, 16, 128)),
        (got, right, outer_output_weight),
        scratch=(
            pltpu.VMEM((256, 1024), BF16),
            pltpu.VMEM((256, 512), BF16),
            pltpu.VMEM((512, 1024), BF16),
            pltpu.VMEM((1024, 128), BF16),
            pltpu.VMEM((32, 16, 128), F32),
        ),
    )
    update = lax.all_to_all(update, PLANE, split_axis=0, concat_axis=0, tiled=True)
    row = call(
        attend_kernel,
        shape((64, 8, 128)),
        (
            update,
            got,
            outer_bias.reshape(1, -1),
            pair_norm_gain.reshape(1, -1),
            pair_query_weight,
            pair_key_weight,
            pair_value_weight,
            pair_gate_weight,
            pair_output_weight,
        ),
        scratch=(
            pltpu.VMEM((512, 128), BF16),
            pltpu.VMEM((512, 128), BF16),
            pltpu.VMEM((512, 128), BF16),
            pltpu.VMEM((512, 128), F32),
            pltpu.VMEM((512, 128), F32),
        ),
    )
    pair_out = lax.all_to_all(row, GROUP, split_axis=0, concat_axis=0, tiled=True)
    nodes_out, coords_out = call(
        node_kernel,
        (shape(nodes.shape), shape(coords.shape, F32)),
        (
            neighbour_count,
            got,
            neighbour_index,
            node_query,
            nodes,
            coords,
            node_output_weight,
            distance_penalty.reshape(-1, 1),
            coordinate_step.reshape(-1, 1),
        ),
        scalars=1,
    )
    return (pair_out, nodes_out, coords_out)


def solution(mesh):
    fine = Mesh(mesh.devices.reshape(4, 2, 8, 4, 2), ("x", "core", "row", "y", "zh"))
    placed = (
        P(GROUP, "row", None),
        P(GROUP, "row"),
        P(),
        P(),
        P(),
        P(),
        P(),
        P(),
        P("row", GROUP, None),
        P(),
        P(),
        P(),
        P(),
        P(),
        P(),
        P(GROUP, None),
        P(None, GROUP),
        P(GROUP, None),
        P(GROUP),
        P(),
        P(),
        P(),
        P(),
        P(),
        P(),
        P(),
    )
    return jax.shard_map(
        on_device,
        mesh=fine,
        in_specs=placed,
        out_specs=(
            P("row", GROUP, None),
            P(GROUP, None),
            P(None, GROUP),
        ),
        check_vma=False,
    )
```

```python
import math

import jax
import jax.numpy as jnp
from jax import lax
from jax.experimental import pallas as pl
from jax.experimental.pallas import tpu as pltpu
from jax.sharding import Mesh, PartitionSpec as P

F32 = jnp.float32
BF16 = jnp.bfloat16
PAIR_HEADS = 4
NODE_HEADS = 4
PLANE = ("x", "core", "y")
GROUP = ("x", "core", "y", "zh")
VMEM_LIMIT = 48 * 1024 * 1024
FETCH_LIMIT = 56 * 1024 * 1024


def dot(a, b, ca=1, cb=0):
    return lax.dot_general(a, b, (((ca,), (cb,)), ((), ())), preferred_element_type=F32)


def iota(shape, dim):
    return lax.broadcasted_iota(jnp.int32, shape, dim)


def one_where(mask):
    return jnp.where(mask, 1.0, 0.0).astype(BF16)


def layer_normalize(values_in, gain):
    average = jnp.mean(values_in, -1, keepdims=True)
    centred = values_in - average
    variance = jnp.mean(centred * centred, -1, keepdims=True)
    return centred * lax.rsqrt(variance + 1e-05) * gain


def swap_lane_groups(v, low, even):
    t0 = jnp.where(low, v[0], pltpu.roll(v[2], 64, 1))
    t2 = jnp.where(low, pltpu.roll(v[0], 64, 1), v[2])
    t1 = jnp.where(low, v[1], pltpu.roll(v[3], 64, 1))
    t3 = jnp.where(low, pltpu.roll(v[1], 64, 1), v[3])
    return (
        jnp.where(even, t0, pltpu.roll(t1, 32, 1)),
        jnp.where(even, pltpu.roll(t0, 96, 1), t1),
        jnp.where(even, t2, pltpu.roll(t3, 32, 1)),
        jnp.where(even, pltpu.roll(t2, 96, 1), t3),
    )


def lane_masks(rows):
    lane = iota((rows, 128), 1)
    return lane < 64, (lane // 32) % 2 == 0


def first_kernel(
    act_ref,
    tok_ref,
    emb_ref,
    gain_ref,
    wl_ref,
    wr_ref,
    out_ref,
):
    seqs, length, _ = act_ref.shape
    kinds = emb_ref.shape[1]
    emb = emb_ref[...]
    rows = []
    for s in range(seqs):
        picked = one_where(iota((kinds, length), 0) == tok_ref[s : s + 1, :])
        rows.append(act_ref[s].astype(F32) + dot(picked, emb, 0, 1))
    normed = layer_normalize(jnp.concatenate(rows, 0), gain_ref[...]).astype(BF16)

    left = dot(wl_ref[...], normed, 1, 1).astype(BF16).astype(F32)
    low = iota((16, 128), 1) < 64
    parts = []
    for p in range(2):
        a0 = left[0:16, p * 128 : (p + 1) * 128]
        a1 = left[16:32, p * 128 : (p + 1) * 128]
        parts.append(jnp.where(low, a0, pltpu.roll(a1, 64, 1)))
        parts.append(jnp.where(low, pltpu.roll(a0, 64, 1), a1))
    block = jnp.concatenate(parts, 0).astype(BF16)
    out_ref[:, 0:64] = jnp.broadcast_to(block[None], (32, 64, 128))

    widened = dot(wr_ref[...], one_where(iota((32, 128), 1) == iota((32, 128), 0)), 0, 0).astype(BF16)
    for g in range(2):
        row, source = iota((256, 256), 0) + g * 256, iota((256, 256), 1)
        wanted = ((row % 8) // 2) * 64 + (row // 16) * 2 + row % 2
        moved = dot(one_where((source == wanted) & (row % 16 < 8)), normed).astype(BF16)
        right = dot(moved, widened).astype(BF16)
        out_ref[g * 16 : (g + 1) * 16, 64:80] = right.reshape(16, 16, 128)


def node_project_kernel(nodes_ref, coords_ref, node_gain_ref, wq_ref, wk_ref, wv_ref, slot_ref, query_ref):
    row, lane = iota((64, 128), 0), iota((64, 128), 1)
    normed = layer_normalize(nodes_ref[...].astype(F32), node_gain_ref[...]).astype(BF16)
    query_ref[...] = dot(wq_ref[...], normed, 0, 1).astype(BF16).astype(F32)
    kv = dot(normed, dot(wk_ref[...], one_where(lane == row)).astype(BF16))
    kv = kv + dot(normed, dot(wv_ref[...], one_where(lane == row + 64)).astype(BF16))
    rest = coords_ref[...]
    placed = jnp.zeros((8, 128), F32)
    for part in range(3):
        piece = rest.astype(BF16)
        rest = rest - piece.astype(F32)
        spot = one_where(iota((3, 128), 1) == iota((3, 128), 0) * 3 + part)
        placed = placed + dot(piece, spot, 0, 0)
    slot_ref[...] = jnp.concatenate([kv, placed], 0).astype(BF16)


def right_kernel(got_ref, out_ref):
    rows = got_ref[:, 64:80].reshape(512, 128)
    row, source = iota((64, 512), 0), iota((64, 512), 1)
    start = (row // 4) * 16 + (row % 4) * 2
    at, lane = iota((128, 128), 0), iota((128, 128), 1)
    total = jnp.zeros((64, 128), F32)
    for hi in range(2):
        for column in range(2):
            picked = dot(one_where(source == start + hi * 256 + column), rows).astype(BF16)
            shift = (hi * 2 + column) * 32
            total = total + dot(picked, one_where((lane == at + shift) & (at < 32)))
    out_ref[...] = jnp.broadcast_to(total.astype(BF16)[None], out_ref.shape)


def outer_kernel(
    got_ref, right_in, pair_ref, weight_ref, slot_ref, out_ref, left, right, joined, update
):
    turn = one_where(
        iota((256, 256), 1) == (iota((256, 256), 0) % 16) * 16 + iota((256, 256), 0) // 16
    )
    for g in range(8):
        part = dot(turn, got_ref[g * 4 : (g + 1) * 4, 0:64].reshape(256, 128)).astype(BF16)
        for q in range(16):
            left[g * 16 : (g + 1) * 16, q * 128 : (q + 1) * 128] = part[q * 16 : (q + 1) * 16]
    low, even = lane_masks(64)
    for t in range(4):
        a, b = right_in[2 * t].astype(F32), right_in[2 * t + 1].astype(F32)
        right[0:64, t * 128 : (t + 1) * 128] = jnp.where(low, a, pltpu.roll(b, 64, 1)).astype(BF16)
        right[64:128, t * 128 : (t + 1) * 128] = jnp.where(low, pltpu.roll(a, 64, 1), b).astype(BF16)

    low, even = lane_masks(128)
    scale = 1.0 / 256.0
    for e in range(4):
        products = [
            dot(left[:, (4 * e + k) * 128 : (4 * e + k + 1) * 128], right[...], 0, 0) * scale
            for k in range(4)
        ]
        for t in range(4):
            blocks = swap_lane_groups([p[:, t * 128 : (t + 1) * 128] for p in products], low, even)
            for j in range(4):
                block = blocks[j].astype(BF16)
                at = (t * 4 + j) * 64
                joined[at : at + 64, e * 128 : (e + 1) * 128] = block[:64]
                joined[at : at + 64, (4 + e) * 128 : (5 + e) * 128] = block[64:]
    for j in range(0, 16, 4):
        rows = dot(joined[j * 64 : (j + 4) * 64], weight_ref[...])
        for k in range(4):
            update[:, j + k, :] = rows[k * 64 : (k + 1) * 64]
    out_ref[:, 0:16] = update[...].astype(BF16)
    slot = slot_ref[...].astype(F32)
    kv = jnp.broadcast_to(slot[None, 0:8], (64, 8, 128))
    out_ref[:, 16:32] = jnp.concatenate([pair_ref[...].astype(F32), kv], 1).astype(BF16)
    out_ref[:, 32:40] = jnp.broadcast_to(slot[None, 8:16], (64, 8, 128)).astype(BF16)


def attend_kernel(
    got_ref, bias_ref, gain_ref, wq_ref, wk_ref, wv_ref, wg_ref, wo_ref, out_ref, q_s, k_s, v_s, mid_s, gate_s
):
    row = iota((512, 512), 0)
    wanted = ((row // 2) % 32) * 16 + (row // 64) * 2 + row % 2
    turn = one_where(iota((512, 512), 1) == wanted)
    shares = got_ref[:, 0:16].reshape(32, 2, 16, 128)
    pair_mid = dot(turn, shares[:, 0].reshape(512, 128)) + dot(turn, shares[:, 1].reshape(512, 128))
    pair = got_ref[:, 16:32].reshape(64, 2, 8, 128)[:, 0].reshape(512, 128)
    pair_mid = pair_mid + pair.astype(F32) + bias_ref[...]
    pair_mid = pair_mid.astype(BF16).astype(F32)
    mid_s[...] = pair_mid
    normed = layer_normalize(pair_mid, gain_ref[...]).astype(BF16)
    q_s[...] = dot(normed, wq_ref[...]).astype(BF16)
    k_s[...] = dot(normed, wk_ref[...]).astype(BF16)
    v_s[...] = dot(normed, wv_ref[...]).astype(BF16)
    gate_s[...] = dot(normed, wg_ref[...])
    factor = 32 ** (-0.5) * math.log2(math.e)
    head_of = iota((512, 128), 1) // 32
    keys, values = k_s[...], v_s[...]
    zero, one = jnp.zeros((512, 128), BF16), jnp.ones((512, 128), BF16)
    head_keys = [jnp.where(head_of == h, keys, zero) for h in range(PAIR_HEADS)]
    head_values = [
        jnp.concatenate(
            [jnp.where(head_of == h, values, zero), jnp.where(head_of == h, one, zero)], 1
        )
        for h in range(PAIR_HEADS)
    ]
    for c in range(4):
        at = slice(c * 128, (c + 1) * 128)
        queries = q_s[at, :]
        total = jnp.zeros((128, 256), F32)
        for h in range(PAIR_HEADS):
            scores = dot(queries, head_keys[h], 1, 1)
            top = jnp.max(scores, -1, keepdims=True)
            weights = jnp.exp2((scores - top) * factor).astype(BF16)
            total = total + dot(weights, head_values[h])
        attended = total[:, :128] / total[:, 128:] * jax.nn.sigmoid(gate_s[at, :])
        result = mid_s[at, :] + dot(attended.astype(BF16), wo_ref[...])
        out_ref[c * 16 : (c + 1) * 16] = result.astype(BF16).reshape(16, 8, 128)


def node_kernel(
    count_ref, got_ref, index_ref, query_ref, nodes_ref, coords_ref, wo_ref, penalty_ref, step_ref, nodes_out, coords_out
):
    kv_table = got_ref[:, 16:32].reshape(64, 2, 8, 128)[:, 1].reshape(512, 128)
    place_table = got_ref[:, 32:40].reshape(512, 128)
    local, slots = index_ref.shape
    width, dim = nodes_ref.shape[1], nodes_ref.shape[1] // NODE_HEADS
    lane = iota((1, slots), 1)
    spot = iota((1, local), 1)
    mixed = jnp.zeros((width, local), F32)
    moved = jnp.zeros((3, local), F32)
    for i in range(local):
        picked = one_where(iota((512, slots), 0) == index_ref[i : i + 1, :])
        near = dot(kv_table, picked, 0, 0)
        where = dot(place_table, picked, 0, 0)
        position = [
            where[3 * c : 3 * c + 1] + where[3 * c + 1 : 3 * c + 2] + where[3 * c + 2 : 3 * c + 3]
            for c in range(3)
        ]
        offsets = jnp.concatenate(position, 0) - coords_ref[:, i : i + 1]
        dist2 = jnp.sum(offsets * offsets, 0, keepdims=True)
        products = near[:width] * query_ref[:, i : i + 1]
        logits = jnp.sum(products.reshape(NODE_HEADS, dim, slots), 1) * dim ** (-0.5)
        logits = logits - penalty_ref[...] * dist2
        valid = lane < count_ref[i]
        logits = jnp.where(valid, logits, -1e30)
        powers = jnp.exp(logits - jnp.max(logits, -1, keepdims=True))
        weight = powers / jnp.sum(powers, -1, keepdims=True)
        weight = jnp.where(valid, weight, 0.0)
        low = weight.astype(BF16).astype(F32)
        spread = jnp.broadcast_to(low[:, None, :], (NODE_HEADS, dim, slots)).reshape(width, slots)
        column = jnp.sum(near[width:] * spread, -1, keepdims=True)
        mixed = mixed + jnp.where(spot == i, column, 0.0)
        pull = jnp.sum(weight * step_ref[...], 0, keepdims=True)
        moved = moved + jnp.where(spot == i, jnp.sum(offsets * pull, -1, keepdims=True), 0.0)
    out = nodes_ref[...].astype(F32) + dot(mixed.astype(BF16), wo_ref[...], 0, 0)
    nodes_out[...] = out.astype(BF16)
    coords_out[...] = coords_ref[...] + moved


def with_fetch(body, count):
    def kernel(*refs):
        sources, held, sems = refs[:count], refs[-count - 1 : -1], refs[-1]
        copies = [pltpu.make_async_copy(sources[i], held[i], sems.at[i]) for i in range(count)]
        for copy in copies:
            copy.start()
        for copy in copies:
            copy.wait()
        body(*held, *refs[count : -count - 1])

    return kernel


def call(body, out_shape, args, scratch=(), fetch=False):
    scratch = list(scratch)
    if fetch:
        body = with_fetch(body, len(args))
        scratch += [pltpu.VMEM(a.shape, a.dtype) for a in args] + [pltpu.SemaphoreType.DMA((len(args),))]
    space = pltpu.HBM if fetch else pltpu.VMEM
    return pl.pallas_call(
        body,
        out_shape=out_shape,
        in_specs=[pl.BlockSpec(memory_space=pltpu.SMEM if a.ndim == 1 else space) for a in args],
        out_specs=jax.tree.map(lambda _: pl.BlockSpec(memory_space=pltpu.VMEM), out_shape),
        scratch_shapes=scratch,
        compiler_params=pltpu.CompilerParams(vmem_limit_bytes=FETCH_LIMIT if fetch else VMEM_LIMIT),
    )(*args)


def shape(dims, kind=BF16):
    return jax.ShapeDtypeStruct(dims, kind)


def on_device(
    homolog_activations,
    alignment_token_ids,
    symbol_lookup_matrix,
    homolog_rescale_vector,
    first_operand_projection,
    second_operand_projection,
    outer_output_weight,
    outer_bias,
    pair,
    pair_norm_gain,
    pair_query_weight,
    pair_key_weight,
    pair_value_weight,
    pair_gate_weight,
    pair_output_weight,
    nodes,
    coords,
    neighbour_index,
    neighbour_count,
    node_norm_gain,
    node_query_weight,
    node_key_weight,
    node_value_weight,
    node_output_weight,
    distance_penalty,
    coordinate_step,
):
    spread = call(
        first_kernel,
        shape((32, 80, 128)),
        (
            homolog_activations,
            alignment_token_ids,
            symbol_lookup_matrix.T,
            homolog_rescale_vector.reshape(1, -1),
            first_operand_projection.T,
            second_operand_projection.T,
        ),
        fetch=True,
    )
    got = lax.all_to_all(spread, PLANE, split_axis=0, concat_axis=0, tiled=True)
    slot, node_query = call(
        node_project_kernel,
        (shape((16, 128)), shape((64, 8), F32)),
        (
            nodes,
            coords,
            node_norm_gain.reshape(1, -1),
            node_query_weight,
            node_key_weight,
            node_value_weight,
        ),
    )
    right = call(right_kernel, shape((8, 64, 128)), (got,))
    right = lax.all_to_all(right, "row", split_axis=0, concat_axis=0, tiled=True)
    shares = call(
        outer_kernel,
        shape((64, 40, 128)),
        (got, right, pair, outer_output_weight, slot),
        scratch=(
            pltpu.VMEM((128, 2048), BF16),
            pltpu.VMEM((128, 512), BF16),
            pltpu.VMEM((1024, 1024), BF16),
            pltpu.VMEM((64, 16, 128), F32),
        ),
    )
    got = lax.all_to_all(shares, GROUP, split_axis=0, concat_axis=0, tiled=True)
    row = call(
        attend_kernel,
        shape((64, 8, 128)),
        (
            got,
            outer_bias.reshape(1, -1),
            pair_norm_gain.reshape(1, -1),
            pair_query_weight,
            pair_key_weight,
            pair_value_weight,
            pair_gate_weight,
            pair_output_weight,
        ),
        scratch=(
            pltpu.VMEM((512, 128), BF16),
            pltpu.VMEM((512, 128), BF16),
            pltpu.VMEM((512, 128), BF16),
            pltpu.VMEM((512, 128), F32),
            pltpu.VMEM((512, 128), F32),
        ),
    )
    pair_out = lax.all_to_all(row, GROUP, split_axis=0, concat_axis=0, tiled=True)
    nodes_out, coords_out = call(
        node_kernel,
        (shape(nodes.shape), shape(coords.shape, F32)),
        (
            neighbour_count,
            got,
            neighbour_index,
            node_query,
            nodes,
            coords,
            node_output_weight,
            distance_penalty.reshape(-1, 1),
            coordinate_step.reshape(-1, 1),
        ),
    )
    return (pair_out, nodes_out, coords_out)


def solution(mesh):
    fine = Mesh(mesh.devices.reshape(4, 2, 8, 4, 2), ("x", "core", "row", "y", "zh"))
    placed = (
        P(GROUP, "row", None),
        P(GROUP, "row"),
        P(),
        P(),
        P(),
        P(),
        P(),
        P(),
        P("row", GROUP, None),
        P(),
        P(),
        P(),
        P(),
        P(),
        P(),
        P(GROUP, None),
        P(None, GROUP),
        P(GROUP, None),
        P(GROUP),
        P(),
        P(),
        P(),
        P(),
        P(),
        P(),
        P(),
    )
    return jax.shard_map(
        on_device,
        mesh=fine,
        in_specs=placed,
        out_specs=(
            P("row", GROUP, None),
            P(GROUP, None),
            P(None, GROUP),
        ),
        check_vma=False,
    )
```

```python
import math

import jax
import jax.numpy as jnp
from jax import lax
from jax.experimental import pallas as pl
from jax.experimental.pallas import tpu as pltpu
from jax.sharding import Mesh, PartitionSpec as P

F32 = jnp.float32
BF16 = jnp.bfloat16
PAIR_HEADS = 4
NODE_HEADS = 4
PLANE = ("x", "core", "y")
GROUP = ("x", "core", "y", "zh")
VMEM_LIMIT = 48 * 1024 * 1024
FETCH_LIMIT = 56 * 1024 * 1024


def dot(a, b, ca=1, cb=0):
    return lax.dot_general(a, b, (((ca,), (cb,)), ((), ())), preferred_element_type=F32)


def iota(shape, dim):
    return lax.broadcasted_iota(jnp.int32, shape, dim)


def one_where(mask):
    return jnp.where(mask, 1.0, 0.0).astype(BF16)


def layer_normalize(values_in, gain):
    average = jnp.mean(values_in, -1, keepdims=True)
    centred = values_in - average
    variance = jnp.mean(centred * centred, -1, keepdims=True)
    return centred * lax.rsqrt(variance + 1e-05) * gain


def swap_lane_groups(v, low, even):
    t0 = jnp.where(low, v[0], pltpu.roll(v[2], 64, 1))
    t2 = jnp.where(low, pltpu.roll(v[0], 64, 1), v[2])
    t1 = jnp.where(low, v[1], pltpu.roll(v[3], 64, 1))
    t3 = jnp.where(low, pltpu.roll(v[1], 64, 1), v[3])
    return (
        jnp.where(even, t0, pltpu.roll(t1, 32, 1)),
        jnp.where(even, pltpu.roll(t0, 96, 1), t1),
        jnp.where(even, t2, pltpu.roll(t3, 32, 1)),
        jnp.where(even, pltpu.roll(t2, 96, 1), t3),
    )


def lane_masks(rows):
    lane = iota((rows, 128), 1)
    return lane < 64, (lane // 32) % 2 == 0


def first_kernel(
    act_ref,
    tok_ref,
    emb_ref,
    gain_ref,
    nodes_ref,
    coords_ref,
    node_gain_ref,
    wq_ref,
    wk_ref,
    wv_ref,
    swap_ref,
    query_ref,
):
    seqs, length, _ = act_ref.shape
    kinds = emb_ref.shape[1]
    emb = emb_ref[...]
    rows = []
    for s in range(seqs):
        picked = one_where(iota((kinds, length), 0) == tok_ref[s : s + 1, :])
        rows.append(act_ref[s].astype(F32) + dot(picked, emb, 0, 1))
    normed = layer_normalize(jnp.concatenate(rows, 0), gain_ref[...]).astype(BF16)
    row, lane = iota((64, 128), 0), iota((64, 128), 1)
    packed = dot(normed[:128], one_where(lane == row)) + dot(normed[128:], one_where(lane == row + 64))
    swap_ref[0:128] = packed.astype(BF16)

    normed = layer_normalize(nodes_ref[...].astype(F32), node_gain_ref[...]).astype(BF16)
    query_ref[...] = dot(wq_ref[...], normed, 0, 1).astype(BF16).astype(F32)
    kv = dot(normed, dot(wk_ref[...], one_where(lane == row)).astype(BF16))
    kv = kv + dot(normed, dot(wv_ref[...], one_where(lane == row + 64)).astype(BF16))
    rest = coords_ref[...]
    placed = jnp.zeros((8, 128), F32)
    for part in range(3):
        piece = rest.astype(BF16)
        rest = rest - piece.astype(F32)
        spot = one_where(iota((3, 128), 1) == iota((3, 128), 0) * 3 + part)
        placed = placed + dot(piece, spot, 0, 0)
    swap_ref[128:144] = jnp.concatenate([kv, placed], 0).astype(BF16)


def spread_kernel(half_ref, own_ref, got_ref, wl_ref, wr_ref, out_ref):
    mine = half_ref[0] == 0
    own, came = own_ref[...].astype(F32), got_ref[...].astype(F32)
    one = jnp.where(mine, own, came)
    two = jnp.where(mine, came, own)
    row, lane = iota((128, 64), 0), iota((128, 64), 1)
    planes = []
    for block in (one, two):
        packed = block[:128].astype(BF16)
        parts = [dot(packed, one_where(row == lane)), dot(packed, one_where(row == lane + 64))]
        planes.append(jnp.concatenate(parts, 0).astype(BF16))

    row, source = iota((128, 256), 0), iota((128, 256), 1)
    low, even = lane_masks(8)
    for core in range(2):
        pick = one_where(source == (row // 32) * 64 + (row % 32) * 2 + core)
        parts = []
        for p in range(2):
            rows = dot(pick, planes[p]).astype(BF16)
            left = dot(wl_ref[...], rows, 1, 1).astype(BF16).astype(F32)
            parts += swap_lane_groups([left[k * 8 : (k + 1) * 8] for k in range(4)], low, even)
        block = jnp.concatenate(parts, 0).astype(BF16)
        for to in range(32):
            if (to // 4) % 2 == core:
                out_ref[to, 0:64] = block

    kv = jnp.concatenate([one[128:136], two[128:136]], 0).astype(BF16)
    out_ref[:, 64:80] = jnp.broadcast_to(kv[None], (32, 16, 128))
    place = jnp.concatenate([one[136:144], two[136:144]], 0)
    widened = dot(wr_ref[...], one_where(iota((32, 128), 1) == iota((32, 128), 0) + 32), 0, 0).astype(BF16)
    both = jnp.concatenate(planes, 0)
    for g in range(4):
        row, source = iota((128, 512), 0) + g * 128, iota((128, 512), 1)
        wanted = ((row // 8) % 2) * 256 + ((row // 2) % 4) * 64 + (row // 16) * 2 + row % 2
        moved = dot(one_where(source == wanted), both).astype(BF16)
        right = dot(moved, widened).reshape(8, 16, 128) + place[None]
        out_ref[g * 8 : (g + 1) * 8, 80:96] = right.astype(BF16)


def right_kernel(got_ref, out_ref):
    rows = got_ref[:, 80:96].reshape(512, 128)
    row, source = iota((128, 512), 0), iota((128, 512), 1)
    start = (row // 4) * 16 + (row % 4) * 2
    at, lane = iota((128, 128), 0), iota((128, 128), 1)
    total = jnp.zeros((128, 128), F32)
    for plane in range(2):
        for column in range(2):
            picked = dot(one_where(source == start + plane * 8 + column), rows).astype(BF16)
            shift = (plane * 2 + column) * 32
            keep = (lane >= shift) & (lane < shift + 32)
            total = total + dot(picked, one_where((at + shift == lane + 32) & keep))
    out_ref[...] = jnp.broadcast_to(total.astype(BF16)[None], out_ref.shape)


def outer_kernel(
    half_ref, got_ref, right_in, other_in, pair_ref, came_ref, weight_ref, out_ref, left, right, joined, weight, update
):
    row = iota((256, 256), 0)
    wanted = ((row // 4) % 4) * 64 + ((row // 16) % 2) * 32 + (row % 4) * 8 + row // 32
    turn = one_where(iota((256, 256), 1) == wanted)
    for g in range(8):
        part = dot(turn, got_ref[g * 4 : (g + 1) * 4, 0:64].reshape(256, 128)).astype(BF16)
        for q in range(8):
            for p in range(2):
                at = p * 128 + g * 16
                left[at : at + 16, q * 128 : (q + 1) * 128] = part[q * 32 + p * 16 : q * 32 + p * 16 + 16]
    low, even = lane_masks(128)
    for t in range(8):
        source = right_in if t < 4 else other_in
        a, b = source[2 * (t % 4)].astype(F32), source[2 * (t % 4) + 1].astype(F32)
        right[0:128, t * 128 : (t + 1) * 128] = jnp.where(low, a, pltpu.roll(b, 64, 1)).astype(BF16)
        right[128:256, t * 128 : (t + 1) * 128] = jnp.where(low, pltpu.roll(a, 64, 1), b).astype(BF16)
    for q in range(8):
        for k in range(4):
            at = (k * 8 + q) * 32
            weight[q * 128 + k * 32 : q * 128 + k * 32 + 32] = weight_ref[at : at + 32]

    low, even = lane_masks(32)
    scale = 1.0 / 256.0
    for q in range(8):
        product = dot(left[:, q * 128 : (q + 1) * 128], right[...], 0, 0) * scale
        for t in range(8):
            tile = product[:, t * 128 : (t + 1) * 128]
            blocks = swap_lane_groups([tile[k * 32 : (k + 1) * 32] for k in range(4)], low, even)
            for j in range(4):
                at = (t * 4 + j) * 32
                joined[at : at + 32, q * 128 : (q + 1) * 128] = blocks[j].astype(BF16)
    for j in range(0, 32, 8):
        rows = dot(joined[j * 32 : (j + 8) * 32], weight[...])
        for k in range(8):
            update[:, j + k, :] = rows[k * 32 : (k + 1) * 32]
    out_ref[:, 0:32] = update[...].astype(BF16)

    first = iota((64, 16, 128), 1) // 8 == half_ref[0]
    kept, came = pair_ref[...].astype(F32), came_ref[...].astype(F32)
    pairs = jnp.where(first, jnp.concatenate([kept, kept], 1), jnp.concatenate([came, came], 1))
    out_ref[:, 32:64] = pairs.reshape(32, 32, 128).astype(BF16)


def attend_kernel(
    half_ref, got_ref, bias_ref, gain_ref, wq_ref, wk_ref, wv_ref, wg_ref, wo_ref, out_ref, q_s, k_s, v_s, mid_s, gate_s, done_s
):
    mine = half_ref[0] == 0
    factor = 32 ** (-0.5) * math.log2(math.e)
    head_of = iota((512, 128), 1) // 32
    zero, one = jnp.zeros((512, 128), BF16), jnp.ones((512, 128), BF16)
    row, source = iota((512, 512), 0), iota((512, 512), 1)
    for p in range(2):
        other = (row // 8) % 2 if p == 0 else 1 - (row // 8) % 2
        wanted = ((row // 16) % 4) * 128 + ((row // 2) % 4) * 32 + other * 16 + (row // 64) * 2 + row % 2
        update = got_ref[:, 0:32].reshape(4, 2, 4, 32, 128)[:, p].reshape(512, 128)
        pair = got_ref[:, 32:64].reshape(32, 2, 16, 128)[:, p].reshape(512, 128)
        pair_mid = dot(one_where(source == wanted), update) + pair.astype(F32) + bias_ref[...]
        pair_mid = pair_mid.astype(BF16).astype(F32)
        normed = layer_normalize(pair_mid, gain_ref[...])
        split = pair_mid.reshape(32, 2, 8, 128)
        mid_s[...] = jnp.where(mine, split[:, 0], split[:, 1]).reshape(256, 128)
        split = normed.reshape(32, 2, 8, 128)
        asking = jnp.where(mine, split[:, 0], split[:, 1]).reshape(256, 128).astype(BF16)
        normed = normed.astype(BF16)
        q_s[...] = dot(asking, wq_ref[...]).astype(BF16)
        gate_s[...] = dot(asking, wg_ref[...])
        k_s[...] = dot(normed, wk_ref[...]).astype(BF16)
        v_s[...] = dot(normed, wv_ref[...]).astype(BF16)
        keys, values = k_s[...], v_s[...]
        head_keys = [jnp.where(head_of == h, keys, zero) for h in range(PAIR_HEADS)]
        head_values = [
            jnp.concatenate(
                [jnp.where(head_of == h, values, zero), jnp.where(head_of == h, one, zero)], 1
            )
            for h in range(PAIR_HEADS)
        ]
        for c in range(2):
            at = slice(c * 128, (c + 1) * 128)
            queries = q_s[at, :]
            total = jnp.zeros((128, 256), F32)
            for h in range(PAIR_HEADS):
                scores = dot(queries, head_keys[h], 1, 1)
                top = jnp.max(scores, -1, keepdims=True)
                weights = jnp.exp2((scores - top) * factor).astype(BF16)
                total = total + dot(weights, head_values[h])
            attended = total[:, :128] / total[:, 128:] * jax.nn.sigmoid(gate_s[at, :])
            result = mid_s[at, :] + dot(attended.astype(BF16), wo_ref[...])
            done_s[c * 16 : (c + 1) * 16, p * 8 : (p + 1) * 8] = result.reshape(16, 8, 128)
    out_ref[...] = done_s[...].astype(BF16)


def node_kernel(
    count_ref, got_ref, index_ref, query_ref, nodes_ref, coords_ref, wo_ref, penalty_ref, step_ref, nodes_out, coords_out
):
    kv_table = got_ref[:, 64:80].reshape(512, 128)
    place_table = got_ref[:, 80:96].reshape(512, 128)
    local, slots = index_ref.shape
    width, dim = nodes_ref.shape[1], nodes_ref.shape[1] // NODE_HEADS
    lane = iota((1, slots), 1)
    spot = iota((1, local), 1)
    mixed = jnp.zeros((width, local), F32)
    moved = jnp.zeros((3, local), F32)
    for i in range(local):
        picked = one_where(iota((512, slots), 0) == index_ref[i : i + 1, :])
        near = dot(kv_table, picked, 0, 0)
        where = dot(place_table, picked, 0, 0)
        position = [
            where[3 * c : 3 * c + 1] + where[3 * c + 1 : 3 * c + 2] + where[3 * c + 2 : 3 * c + 3]
            for c in range(3)
        ]
        offsets = jnp.concatenate(position, 0) - coords_ref[:, i : i + 1]
        dist2 = jnp.sum(offsets * offsets, 0, keepdims=True)
        products = near[:width] * query_ref[:, i : i + 1]
        logits = jnp.sum(products.reshape(NODE_HEADS, dim, slots), 1) * dim ** (-0.5)
        logits = logits - penalty_ref[...] * dist2
        valid = lane < count_ref[i]
        logits = jnp.where(valid, logits, -1e30)
        powers = jnp.exp(logits - jnp.max(logits, -1, keepdims=True))
        weight = powers / jnp.sum(powers, -1, keepdims=True)
        weight = jnp.where(valid, weight, 0.0)
        low = weight.astype(BF16).astype(F32)
        spread = jnp.broadcast_to(low[:, None, :], (NODE_HEADS, dim, slots)).reshape(width, slots)
        column = jnp.sum(near[width:] * spread, -1, keepdims=True)
        mixed = mixed + jnp.where(spot == i, column, 0.0)
        pull = jnp.sum(weight * step_ref[...], 0, keepdims=True)
        moved = moved + jnp.where(spot == i, jnp.sum(offsets * pull, -1, keepdims=True), 0.0)
    out = nodes_ref[...].astype(F32) + dot(mixed.astype(BF16), wo_ref[...], 0, 0)
    nodes_out[...] = out.astype(BF16)
    coords_out[...] = coords_ref[...] + moved


def with_fetch(body, count):
    def kernel(*refs):
        sources, held, sems = refs[:count], refs[-count - 1 : -1], refs[-1]
        copies = [pltpu.make_async_copy(sources[i], held[i], sems.at[i]) for i in range(count)]
        for copy in copies:
            copy.start()
        for copy in copies:
            copy.wait()
        body(*held, *refs[count : -count - 1])

    return kernel


def call(body, out_shape, args, scratch=(), fetch=False):
    scratch = list(scratch)
    if fetch:
        body = with_fetch(body, len(args))
        scratch += [pltpu.VMEM(a.shape, a.dtype) for a in args] + [pltpu.SemaphoreType.DMA((len(args),))]
    space = pltpu.HBM if fetch else pltpu.VMEM
    return pl.pallas_call(
        body,
        out_shape=out_shape,
        in_specs=[pl.BlockSpec(memory_space=pltpu.SMEM if a.ndim == 1 else space) for a in args],
        out_specs=jax.tree.map(lambda _: pl.BlockSpec(memory_space=pltpu.VMEM), out_shape),
        scratch_shapes=scratch,
        compiler_params=pltpu.CompilerParams(vmem_limit_bytes=FETCH_LIMIT if fetch else VMEM_LIMIT),
    )(*args)


def shape(dims, kind=BF16):
    return jax.ShapeDtypeStruct(dims, kind)


def on_device(
    homolog_activations,
    alignment_token_ids,
    symbol_lookup_matrix,
    homolog_rescale_vector,
    first_operand_projection,
    second_operand_projection,
    outer_output_weight,
    outer_bias,
    pair,
    pair_norm_gain,
    pair_query_weight,
    pair_key_weight,
    pair_value_weight,
    pair_gate_weight,
    pair_output_weight,
    nodes,
    coords,
    neighbour_index,
    neighbour_count,
    node_norm_gain,
    node_query_weight,
    node_key_weight,
    node_value_weight,
    node_output_weight,
    distance_penalty,
    coordinate_step,
):
    half = lax.axis_index("zh").reshape(1).astype(jnp.int32)
    swap, node_query = call(
        first_kernel,
        (shape((144, 128)), shape((64, 8), F32)),
        (
            homolog_activations,
            alignment_token_ids,
            symbol_lookup_matrix.T,
            homolog_rescale_vector.reshape(1, -1),
            nodes,
            coords,
            node_norm_gain.reshape(1, -1),
            node_query_weight,
            node_key_weight,
            node_value_weight,
        ),
        fetch=True,
    )
    swapped = lax.ppermute(swap, "zh", [(0, 1), (1, 0)])
    given, _ = lax.optimization_barrier((pair, swap))
    slots = jnp.stack([jnp.where(half[0] == 1, given, 0), jnp.where(half[0] == 0, given, 0)])
    came = lax.psum_scatter(slots, "zh", scatter_dimension=0, tiled=False)
    spread = call(
        spread_kernel,
        shape((32, 96, 128)),
        (half, swap, swapped, first_operand_projection.T, second_operand_projection.T),
    )
    got = lax.all_to_all(spread, PLANE, split_axis=0, concat_axis=0, tiled=True)
    right = call(right_kernel, shape((8, 128, 128)), (got,))
    right = lax.all_to_all(right, "row", split_axis=0, concat_axis=0, tiled=True)
    other = lax.ppermute(right, "core", [(0, 1), (1, 0)])
    rows = call(
        outer_kernel,
        shape((32, 64, 128)),
        (half, got, right, other, pair, came, outer_output_weight),
        scratch=(
            pltpu.VMEM((256, 1024), BF16),
            pltpu.VMEM((256, 1024), BF16),
            pltpu.VMEM((1024, 1024), BF16),
            pltpu.VMEM((1024, 128), BF16),
            pltpu.VMEM((32, 32, 128), F32),
        ),
    )
    rows = lax.all_to_all(rows, PLANE, split_axis=0, concat_axis=0, tiled=True)
    done = call(
        attend_kernel,
        shape((32, 16, 128)),
        (
            half,
            rows,
            outer_bias.reshape(1, -1),
            pair_norm_gain.reshape(1, -1),
            pair_query_weight,
            pair_key_weight,
            pair_value_weight,
            pair_gate_weight,
            pair_output_weight,
        ),
        scratch=(
            pltpu.VMEM((256, 128), BF16),
            pltpu.VMEM((512, 128), BF16),
            pltpu.VMEM((512, 128), BF16),
            pltpu.VMEM((256, 128), F32),
            pltpu.VMEM((256, 128), F32),
            pltpu.VMEM((32, 16, 128), F32),
        ),
    )
    done = lax.all_to_all(done, PLANE, split_axis=0, concat_axis=0, tiled=True)
    pair_out = done.reshape(pair.shape)
    nodes_out, coords_out = call(
        node_kernel,
        (shape(nodes.shape), shape(coords.shape, F32)),
        (
            neighbour_count,
            got,
            neighbour_index,
            node_query,
            nodes,
            coords,
            node_output_weight,
            distance_penalty.reshape(-1, 1),
            coordinate_step.reshape(-1, 1),
        ),
    )
    return (pair_out, nodes_out, coords_out)


def solution(mesh):
    fine = Mesh(mesh.devices.reshape(4, 2, 8, 4, 2), ("x", "core", "row", "y", "zh"))
    placed = (
        P(GROUP, "row", None),
        P(GROUP, "row"),
        P(),
        P(),
        P(),
        P(),
        P(),
        P(),
        P("row", GROUP, None),
        P(),
        P(),
        P(),
        P(),
        P(),
        P(),
        P(GROUP, None),
        P(None, GROUP),
        P(GROUP, None),
        P(GROUP),
        P(),
        P(),
        P(),
        P(),
        P(),
        P(),
        P(),
    )
    return jax.shard_map(
        on_device,
        mesh=fine,
        in_specs=placed,
        out_specs=(
            P("row", GROUP, None),
            P(GROUP, None),
            P(None, GROUP),
        ),
        check_vma=False,
    )
```

```python
import math

import jax
import jax.numpy as jnp
from jax import lax
from jax.experimental import pallas as pl
from jax.experimental.pallas import tpu as pltpu
from jax.sharding import Mesh, PartitionSpec as P

F32 = jnp.float32
BF16 = jnp.bfloat16
PAIR_HEADS = 4
NODE_HEADS = 4
PLANE = ("x", "core", "y")
GROUP = ("x", "core", "y", "zh")
VMEM_LIMIT = 48 * 1024 * 1024


def dot(a, b, ca=1, cb=0):
    return lax.dot_general(a, b, (((ca,), (cb,)), ((), ())), preferred_element_type=F32)


def iota(shape, dim):
    return lax.broadcasted_iota(jnp.int32, shape, dim)


def one_where(mask):
    return jnp.where(mask, 1.0, 0.0).astype(BF16)


def layer_normalize(values_in, gain):
    average = jnp.mean(values_in, -1, keepdims=True)
    centred = values_in - average
    variance = jnp.mean(centred * centred, -1, keepdims=True)
    return centred * lax.rsqrt(variance + 1e-05) * gain


def swap_lane_groups(v, low, even):
    t0 = jnp.where(low, v[0], pltpu.roll(v[2], 64, 1))
    t2 = jnp.where(low, pltpu.roll(v[0], 64, 1), v[2])
    t1 = jnp.where(low, v[1], pltpu.roll(v[3], 64, 1))
    t3 = jnp.where(low, pltpu.roll(v[1], 64, 1), v[3])
    return (
        jnp.where(even, t0, pltpu.roll(t1, 32, 1)),
        jnp.where(even, pltpu.roll(t0, 96, 1), t1),
        jnp.where(even, t2, pltpu.roll(t3, 32, 1)),
        jnp.where(even, pltpu.roll(t2, 96, 1), t3),
    )


def lane_masks(rows):
    lane = iota((rows, 128), 1)
    return lane < 64, (lane // 32) % 2 == 0


def first_kernel(
    act_ref,
    tok_ref,
    emb_ref,
    gain_ref,
    nodes_ref,
    coords_ref,
    node_gain_ref,
    wq_ref,
    wk_ref,
    wv_ref,
    bias_ref,
    pair_gain_ref,
    pair_ref,
    swap_ref,
    query_ref,
    consts_ref,
):
    swap_ref[144:656] = pair_ref[...]
    consts_ref[...] = jnp.where(iota((8, 128), 0) == 0, bias_ref[...], pair_gain_ref[...])
    seqs, length, _ = act_ref.shape
    kinds = emb_ref.shape[1]
    emb = emb_ref[...]
    rows = []
    for s in range(seqs):
        picked = one_where(iota((kinds, length), 0) == tok_ref[s : s + 1, :])
        rows.append(act_ref[s].astype(F32) + dot(picked, emb, 0, 1))
    normed = layer_normalize(jnp.concatenate(rows, 0), gain_ref[...]).astype(BF16)
    row, lane = iota((64, 128), 0), iota((64, 128), 1)
    packed = dot(normed[:128], one_where(lane == row)) + dot(normed[128:], one_where(lane == row + 64))
    swap_ref[0:128] = packed.astype(BF16)

    normed = layer_normalize(nodes_ref[...].astype(F32), node_gain_ref[...]).astype(BF16)
    query_ref[...] = dot(wq_ref[...], normed, 0, 1).astype(BF16).astype(F32)
    kv = dot(normed, dot(wk_ref[...], one_where(lane == row)).astype(BF16))
    kv = kv + dot(normed, dot(wv_ref[...], one_where(lane == row + 64)).astype(BF16))
    rest = coords_ref[...]
    placed = jnp.zeros((8, 128), F32)
    for part in range(3):
        piece = rest.astype(BF16)
        rest = rest - piece.astype(F32)
        spot = one_where(iota((3, 128), 1) == iota((3, 128), 0) * 3 + part)
        placed = placed + dot(piece, spot, 0, 0)
    swap_ref[128:144] = jnp.concatenate([kv, placed], 0).astype(BF16)


def spread_kernel(half_ref, own_ref, got_ref, wl_ref, wr_ref, out_ref):
    mine = half_ref[0] == 0
    own, came = own_ref[0:144].astype(F32), got_ref[0:144].astype(F32)
    one = jnp.where(mine, own, came)
    two = jnp.where(mine, came, own)
    row, lane = iota((128, 64), 0), iota((128, 64), 1)
    planes = []
    for block in (one, two):
        packed = block[:128].astype(BF16)
        parts = [dot(packed, one_where(row == lane)), dot(packed, one_where(row == lane + 64))]
        planes.append(jnp.concatenate(parts, 0).astype(BF16))

    row, source = iota((128, 256), 0), iota((128, 256), 1)
    low, even = lane_masks(8)
    for core in range(2):
        pick = one_where(source == (row // 32) * 64 + (row % 32) * 2 + core)
        parts = []
        for p in range(2):
            rows = dot(pick, planes[p]).astype(BF16)
            left = dot(wl_ref[...], rows, 1, 1).astype(BF16).astype(F32)
            parts += swap_lane_groups([left[k * 8 : (k + 1) * 8] for k in range(4)], low, even)
        block = jnp.concatenate(parts, 0).astype(BF16)
        for to in range(32):
            if (to // 4) % 2 == core:
                out_ref[to, 0:64] = block

    kv = jnp.concatenate([one[128:136], two[128:136]], 0).astype(BF16)
    out_ref[:, 64:80] = jnp.broadcast_to(kv[None], (32, 16, 128))
    place = jnp.concatenate([one[136:144], two[136:144]], 0)
    widened = dot(wr_ref[...], one_where(iota((32, 128), 1) == iota((32, 128), 0) + 32), 0, 0).astype(BF16)
    both = jnp.concatenate(planes, 0)
    for g in range(4):
        row, source = iota((128, 512), 0) + g * 128, iota((128, 512), 1)
        wanted = ((row // 8) % 2) * 256 + ((row // 2) % 4) * 64 + (row // 16) * 2 + row % 2
        moved = dot(one_where(source == wanted), both).astype(BF16)
        right = dot(moved, widened).reshape(8, 16, 128) + place[None]
        out_ref[g * 8 : (g + 1) * 8, 80:96] = right.astype(BF16)


def right_kernel(got_ref, out_ref):
    rows = got_ref[:, 80:96].reshape(512, 128)
    row, source = iota((128, 512), 0), iota((128, 512), 1)
    start = (row // 4) * 16 + (row % 4) * 2
    at, lane = iota((128, 128), 0), iota((128, 128), 1)
    total = jnp.zeros((128, 128), F32)
    for plane in range(2):
        for column in range(2):
            picked = dot(one_where(source == start + plane * 8 + column), rows).astype(BF16)
            shift = (plane * 2 + column) * 32
            keep = (lane >= shift) & (lane < shift + 32)
            total = total + dot(picked, one_where((at + shift == lane + 32) & keep))
    out_ref[...] = jnp.broadcast_to(total.astype(BF16)[None], out_ref.shape)


def outer_kernel(
    half_ref, got_ref, right_in, other_in, pair_ref, came_ref, weight_ref, out_ref, left, right, joined, weight, update
):
    row = iota((256, 256), 0)
    wanted = ((row // 4) % 4) * 64 + ((row // 16) % 2) * 32 + (row % 4) * 8 + row // 32
    turn = one_where(iota((256, 256), 1) == wanted)
    for g in range(8):
        part = dot(turn, got_ref[g * 4 : (g + 1) * 4, 0:64].reshape(256, 128)).astype(BF16)
        for q in range(8):
            for p in range(2):
                at = p * 128 + g * 16
                left[at : at + 16, q * 128 : (q + 1) * 128] = part[q * 32 + p * 16 : q * 32 + p * 16 + 16]
    low, even = lane_masks(128)
    for t in range(8):
        source = right_in if t < 4 else other_in
        a, b = source[2 * (t % 4)].astype(F32), source[2 * (t % 4) + 1].astype(F32)
        right[0:128, t * 128 : (t + 1) * 128] = jnp.where(low, a, pltpu.roll(b, 64, 1)).astype(BF16)
        right[128:256, t * 128 : (t + 1) * 128] = jnp.where(low, pltpu.roll(a, 64, 1), b).astype(BF16)
    for q in range(8):
        for k in range(4):
            at = (k * 8 + q) * 32
            weight[q * 128 + k * 32 : q * 128 + k * 32 + 32] = weight_ref[at : at + 32]

    low, even = lane_masks(32)
    scale = 1.0 / 256.0
    for q in range(8):
        product = dot(left[:, q * 128 : (q + 1) * 128], right[...], 0, 0) * scale
        for t in range(8):
            tile = product[:, t * 128 : (t + 1) * 128]
            blocks = swap_lane_groups([tile[k * 32 : (k + 1) * 32] for k in range(4)], low, even)
            for j in range(4):
                at = (t * 4 + j) * 32
                joined[at : at + 32, q * 128 : (q + 1) * 128] = blocks[j].astype(BF16)
    for j in range(0, 32, 8):
        rows = dot(joined[j * 32 : (j + 8) * 32], weight[...])
        for k in range(8):
            update[:, j + k, :] = rows[k * 32 : (k + 1) * 32]
    out_ref[:, 0:32] = update[...].astype(BF16)

    first = iota((64, 16, 128), 1) // 8 == half_ref[0]
    kept, came = pair_ref[...].astype(F32), came_ref[144:656].reshape(64, 8, 128).astype(F32)
    pairs = jnp.where(first, jnp.concatenate([kept, kept], 1), jnp.concatenate([came, came], 1))
    out_ref[:, 32:64] = pairs.reshape(32, 32, 128).astype(BF16)


def attend_kernel(
    half_ref, got_ref, consts_ref, wq_ref, wk_ref, wv_ref, wg_ref, wo_ref, out_ref, q_s, k_s, v_s, mid_s, gate_s, done_s
):
    mine = half_ref[0] == 0
    factor = 32 ** (-0.5) * math.log2(math.e)
    head_of = iota((512, 128), 1) // 32
    zero, one = jnp.zeros((512, 128), BF16), jnp.ones((512, 128), BF16)
    row, source = iota((512, 512), 0), iota((512, 512), 1)
    for p in range(2):
        other = (row // 8) % 2 if p == 0 else 1 - (row // 8) % 2
        wanted = ((row // 16) % 4) * 128 + ((row // 2) % 4) * 32 + other * 16 + (row // 64) * 2 + row % 2
        update = got_ref[:, 0:32].reshape(4, 2, 4, 32, 128)[:, p].reshape(512, 128)
        pair = got_ref[:, 32:64].reshape(32, 2, 16, 128)[:, p].reshape(512, 128)
        pair_mid = dot(one_where(source == wanted), update) + pair.astype(F32) + consts_ref[0:1]
        pair_mid = pair_mid.astype(BF16).astype(F32)
        normed = layer_normalize(pair_mid, consts_ref[1:2])
        split = pair_mid.reshape(32, 2, 8, 128)
        mid_s[...] = jnp.where(mine, split[:, 0], split[:, 1]).reshape(256, 128)
        split = normed.reshape(32, 2, 8, 128)
        asking = jnp.where(mine, split[:, 0], split[:, 1]).reshape(256, 128).astype(BF16)
        normed = normed.astype(BF16)
        q_s[...] = dot(asking, wq_ref[...]).astype(BF16)
        gate_s[...] = dot(asking, wg_ref[...])
        k_s[...] = dot(normed, wk_ref[...]).astype(BF16)
        v_s[...] = dot(normed, wv_ref[...]).astype(BF16)
        keys, values = k_s[...], v_s[...]
        head_keys = [jnp.where(head_of == h, keys, zero) for h in range(PAIR_HEADS)]
        head_values = [
            jnp.concatenate(
                [jnp.where(head_of == h, values, zero), jnp.where(head_of == h, one, zero)], 1
            )
            for h in range(PAIR_HEADS)
        ]
        for c in range(2):
            at = slice(c * 128, (c + 1) * 128)
            queries = q_s[at, :]
            total = jnp.zeros((128, 256), F32)
            for h in range(PAIR_HEADS):
                scores = dot(queries, head_keys[h], 1, 1)
                top = jnp.max(scores, -1, keepdims=True)
                weights = jnp.exp2((scores - top) * factor).astype(BF16)
                total = total + dot(weights, head_values[h])
            attended = total[:, :128] / total[:, 128:] * jax.nn.sigmoid(gate_s[at, :])
            result = mid_s[at, :] + dot(attended.astype(BF16), wo_ref[...])
            done_s[c * 16 : (c + 1) * 16, p * 8 : (p + 1) * 8] = result.reshape(16, 8, 128)
    out_ref[...] = done_s[...].astype(BF16)


def node_kernel(
    count_ref, got_ref, index_ref, query_ref, nodes_ref, coords_ref, wo_ref, penalty_ref, step_ref, nodes_out, coords_out
):
    kv_table = got_ref[:, 64:80].reshape(512, 128)
    place_table = got_ref[:, 80:96].reshape(512, 128)
    local, slots = index_ref.shape
    width, dim = nodes_ref.shape[1], nodes_ref.shape[1] // NODE_HEADS
    lane = iota((1, slots), 1)
    spot = iota((1, local), 1)
    mixed = jnp.zeros((width, local), F32)
    moved = jnp.zeros((3, local), F32)
    for i in range(local):
        picked = one_where(iota((512, slots), 0) == index_ref[i : i + 1, :])
        near = dot(kv_table, picked, 0, 0)
        where = dot(place_table, picked, 0, 0)
        position = [
            where[3 * c : 3 * c + 1] + where[3 * c + 1 : 3 * c + 2] + where[3 * c + 2 : 3 * c + 3]
            for c in range(3)
        ]
        offsets = jnp.concatenate(position, 0) - coords_ref[:, i : i + 1]
        dist2 = jnp.sum(offsets * offsets, 0, keepdims=True)
        products = near[:width] * query_ref[:, i : i + 1]
        logits = jnp.sum(products.reshape(NODE_HEADS, dim, slots), 1) * dim ** (-0.5)
        logits = logits - penalty_ref[...] * dist2
        valid = lane < count_ref[i]
        logits = jnp.where(valid, logits, -1e30)
        powers = jnp.exp(logits - jnp.max(logits, -1, keepdims=True))
        weight = powers / jnp.sum(powers, -1, keepdims=True)
        weight = jnp.where(valid, weight, 0.0)
        low = weight.astype(BF16).astype(F32)
        spread = jnp.broadcast_to(low[:, None, :], (NODE_HEADS, dim, slots)).reshape(width, slots)
        column = jnp.sum(near[width:] * spread, -1, keepdims=True)
        mixed = mixed + jnp.where(spot == i, column, 0.0)
        pull = jnp.sum(weight * step_ref[...], 0, keepdims=True)
        moved = moved + jnp.where(spot == i, jnp.sum(offsets * pull, -1, keepdims=True), 0.0)
    out = nodes_ref[...].astype(F32) + dot(mixed.astype(BF16), wo_ref[...], 0, 0)
    nodes_out[...] = out.astype(BF16)
    coords_out[...] = coords_ref[...] + moved


def with_fetch(body, count):
    def kernel(*refs):
        sources, held, sems = refs[:count], refs[-count - 1 : -1], refs[-1]
        copies = [pltpu.make_async_copy(sources[i], held[i], sems.at[i]) for i in range(count)]
        for copy in copies:
            copy.start()
        for copy in copies:
            copy.wait()
        body(*held, *refs[count : -count - 1])

    return kernel


def call(body, out_shape, args, scratch=(), fetch=False):
    scratch = list(scratch)
    if fetch:
        body = with_fetch(body, len(args))
        scratch += [pltpu.VMEM(a.shape, a.dtype) for a in args] + [pltpu.SemaphoreType.DMA((len(args),))]
        args = [pltpu.with_memory_space_constraint(a, pltpu.HBM) for a in args]
    space = pltpu.HBM if fetch else pltpu.VMEM
    return pl.pallas_call(
        body,
        out_shape=out_shape,
        in_specs=[pl.BlockSpec(memory_space=pltpu.SMEM if a.ndim == 1 else space) for a in args],
        out_specs=jax.tree.map(lambda _: pl.BlockSpec(memory_space=pltpu.VMEM), out_shape),
        scratch_shapes=scratch,
        compiler_params=pltpu.CompilerParams(vmem_limit_bytes=VMEM_LIMIT),
    )(*args)


def shape(dims, kind=BF16):
    return jax.ShapeDtypeStruct(dims, kind)


def on_device(
    homolog_activations,
    alignment_token_ids,
    symbol_lookup_matrix,
    homolog_rescale_vector,
    first_operand_projection,
    second_operand_projection,
    outer_output_weight,
    outer_bias,
    pair,
    pair_norm_gain,
    pair_query_weight,
    pair_key_weight,
    pair_value_weight,
    pair_gate_weight,
    pair_output_weight,
    nodes,
    coords,
    neighbour_index,
    neighbour_count,
    node_norm_gain,
    node_query_weight,
    node_key_weight,
    node_value_weight,
    node_output_weight,
    distance_penalty,
    coordinate_step,
):
    half = lax.axis_index("zh").reshape(1).astype(jnp.int32)
    swap, node_query, consts = call(
        first_kernel,
        (shape((656, 128)), shape((64, 8), F32), shape((8, 128), F32)),
        (
            homolog_activations,
            alignment_token_ids,
            symbol_lookup_matrix.T,
            homolog_rescale_vector.reshape(1, -1),
            nodes,
            coords,
            node_norm_gain.reshape(1, -1),
            node_query_weight,
            node_key_weight,
            node_value_weight,
            outer_bias.reshape(1, -1),
            pair_norm_gain.reshape(1, -1),
            pair.reshape(512, 128),
        ),
        fetch=True,
    )
    swapped = lax.ppermute(swap, "zh", [(0, 1), (1, 0)])
    spread = call(
        spread_kernel,
        shape((32, 96, 128)),
        (half, swap, swapped, first_operand_projection.T, second_operand_projection.T),
    )
    got = lax.all_to_all(spread, PLANE, split_axis=0, concat_axis=0, tiled=True)
    right = call(right_kernel, shape((8, 128, 128)), (got,))
    right = lax.all_to_all(right, "row", split_axis=0, concat_axis=0, tiled=True)
    other = lax.ppermute(right, "core", [(0, 1), (1, 0)])
    rows = call(
        outer_kernel,
        shape((32, 64, 128)),
        (half, got, right, other, pair, swapped, outer_output_weight),
        scratch=(
            pltpu.VMEM((256, 1024), BF16),
            pltpu.VMEM((256, 1024), BF16),
            pltpu.VMEM((1024, 1024), BF16),
            pltpu.VMEM((1024, 128), BF16),
            pltpu.VMEM((32, 32, 128), F32),
        ),
    )
    rows = lax.all_to_all(rows, PLANE, split_axis=0, concat_axis=0, tiled=True)
    done = call(
        attend_kernel,
        shape((32, 16, 128)),
        (
            half,
            rows,
            consts,
            pair_query_weight,
            pair_key_weight,
            pair_value_weight,
            pair_gate_weight,
            pair_output_weight,
        ),
        scratch=(
            pltpu.VMEM((256, 128), BF16),
            pltpu.VMEM((512, 128), BF16),
            pltpu.VMEM((512, 128), BF16),
            pltpu.VMEM((256, 128), F32),
            pltpu.VMEM((256, 128), F32),
            pltpu.VMEM((32, 16, 128), F32),
        ),
    )
    done = lax.all_to_all(done, PLANE, split_axis=0, concat_axis=0, tiled=True)
    pair_out = done.reshape(pair.shape)
    nodes_out, coords_out = call(
        node_kernel,
        (shape(nodes.shape), shape(coords.shape, F32)),
        (
            neighbour_count,
            got,
            neighbour_index,
            node_query,
            nodes,
            coords,
            node_output_weight,
            distance_penalty.reshape(-1, 1),
            coordinate_step.reshape(-1, 1),
        ),
    )
    return (pair_out, nodes_out, coords_out)


def solution(mesh):
    fine = Mesh(mesh.devices.reshape(4, 2, 8, 4, 2), ("x", "core", "row", "y", "zh"))
    placed = (
        P(GROUP, "row", None),
        P(GROUP, "row"),
        P(),
        P(),
        P(),
        P(),
        P(),
        P(),
        P("row", GROUP, None),
        P(),
        P(),
        P(),
        P(),
        P(),
        P(),
        P(GROUP, None),
        P(None, GROUP),
        P(GROUP, None),
        P(GROUP),
        P(),
        P(),
        P(),
        P(),
        P(),
        P(),
        P(),
    )
    return jax.shard_map(
        on_device,
        mesh=fine,
        in_specs=placed,
        out_specs=(
            P("row", GROUP, None),
            P(GROUP, None),
            P(None, GROUP),
        ),
        check_vma=False,
    )
```

```python
import math

import jax
import jax.numpy as jnp
from jax import lax
from jax.experimental import pallas as pl
from jax.experimental.pallas import tpu as pltpu
from jax.sharding import Mesh, PartitionSpec as P

F32 = jnp.float32
BF16 = jnp.bfloat16
PAIR_HEADS = 4
NODE_HEADS = 4
PLANE = ("x", "core", "y")
GROUP = ("x", "core", "y", "zh")
VMEM_LIMIT = 48 * 1024 * 1024


def dot(a, b, ca=1, cb=0):
    return lax.dot_general(a, b, (((ca,), (cb,)), ((), ())), preferred_element_type=F32)


def iota(shape, dim):
    return lax.broadcasted_iota(jnp.int32, shape, dim)


def one_where(mask):
    return jnp.where(mask, 1.0, 0.0).astype(BF16)


def layer_normalize(values_in, gain):
    average = jnp.mean(values_in, -1, keepdims=True)
    centred = values_in - average
    variance = jnp.mean(centred * centred, -1, keepdims=True)
    return centred * lax.rsqrt(variance + 1e-05) * gain


def swap_lane_groups(v, low, even):
    t0 = jnp.where(low, v[0], pltpu.roll(v[2], 64, 1))
    t2 = jnp.where(low, pltpu.roll(v[0], 64, 1), v[2])
    t1 = jnp.where(low, v[1], pltpu.roll(v[3], 64, 1))
    t3 = jnp.where(low, pltpu.roll(v[1], 64, 1), v[3])
    return (
        jnp.where(even, t0, pltpu.roll(t1, 32, 1)),
        jnp.where(even, pltpu.roll(t0, 96, 1), t1),
        jnp.where(even, t2, pltpu.roll(t3, 32, 1)),
        jnp.where(even, pltpu.roll(t2, 96, 1), t3),
    )


def lane_masks(rows):
    lane = iota((rows, 128), 1)
    return lane < 64, (lane // 32) % 2 == 0


def first_kernel(
    act_ref,
    tok_ref,
    emb_ref,
    gain_ref,
    nodes_ref,
    coords_ref,
    node_gain_ref,
    wq_ref,
    wk_ref,
    wv_ref,
    bias_ref,
    pair_gain_ref,
    pair_ref,
    wl_ref,
    wr_ref,
    swap_ref,
    query_ref,
    consts_ref,
    factor_ref,
):
    swap_ref[144:656] = pair_ref[...]
    factor_ref[0:32] = wl_ref[...]
    factor_ref[32:64] = wr_ref[...]
    consts_ref[...] = jnp.where(iota((8, 128), 0) == 0, bias_ref[...], pair_gain_ref[...])
    seqs, length, _ = act_ref.shape
    kinds = emb_ref.shape[1]
    emb = emb_ref[...]
    rows = []
    for s in range(seqs):
        picked = one_where(iota((kinds, length), 0) == tok_ref[s : s + 1, :])
        rows.append(act_ref[s].astype(F32) + dot(picked, emb, 0, 1))
    normed = layer_normalize(jnp.concatenate(rows, 0), gain_ref[...]).astype(BF16)
    row, lane = iota((64, 128), 0), iota((64, 128), 1)
    packed = dot(normed[:128], one_where(lane == row)) + dot(normed[128:], one_where(lane == row + 64))
    swap_ref[0:128] = packed.astype(BF16)

    normed = layer_normalize(nodes_ref[...].astype(F32), node_gain_ref[...]).astype(BF16)
    query_ref[...] = dot(wq_ref[...], normed, 0, 1).astype(BF16).astype(F32)
    kv = dot(normed, dot(wk_ref[...], one_where(lane == row)).astype(BF16))
    kv = kv + dot(normed, dot(wv_ref[...], one_where(lane == row + 64)).astype(BF16))
    rest = coords_ref[...]
    placed = jnp.zeros((8, 128), F32)
    for part in range(3):
        piece = rest.astype(BF16)
        rest = rest - piece.astype(F32)
        spot = one_where(iota((3, 128), 1) == iota((3, 128), 0) * 3 + part)
        placed = placed + dot(piece, spot, 0, 0)
    swap_ref[128:144] = jnp.concatenate([kv, placed], 0).astype(BF16)


def spread_kernel(half_ref, after_ref, own_ref, got_ref, factor_ref, out_ref):
    mine = half_ref[0] == 0
    own, came = own_ref[0:144].astype(F32), got_ref[0:144].astype(F32)
    one = jnp.where(mine, own, came)
    two = jnp.where(mine, came, own)
    row, lane = iota((128, 64), 0), iota((128, 64), 1)
    planes = []
    for block in (one, two):
        packed = block[:128].astype(BF16)
        parts = [dot(packed, one_where(row == lane)), dot(packed, one_where(row == lane + 64))]
        planes.append(jnp.concatenate(parts, 0).astype(BF16))

    row, source = iota((128, 1), 0), iota((128, 256), 1)
    low, even = lane_masks(8)
    for core in range(2):
        pick = one_where(source == ((row >> 5) << 6) + ((row & 31) << 1) + core)
        parts = []
        for p in range(2):
            rows = dot(pick, planes[p]).astype(BF16)
            left = dot(factor_ref[0:32], rows, 1, 1).astype(BF16).astype(F32)
            parts += swap_lane_groups([left[k * 8 : (k + 1) * 8] for k in range(4)], low, even)
        block = jnp.concatenate(parts, 0).astype(BF16)
        for to in range(32):
            if (to // 4) % 2 == core:
                out_ref[to, 0:64] = block

    kv = jnp.concatenate([one[128:136], two[128:136]], 0).astype(BF16)
    out_ref[:, 64:80] = jnp.broadcast_to(kv[None], (32, 16, 128))
    place = jnp.concatenate([one[136:144], two[136:144]], 0)
    widened = dot(factor_ref[32:64], one_where(iota((32, 128), 1) == iota((32, 128), 0) + 32), 0, 0).astype(BF16)
    both = jnp.concatenate(planes, 0)
    for g in range(4):
        row, source = iota((128, 1), 0) + g * 128, iota((128, 512), 1)
        wanted = (((row >> 3) & 1) << 8) + (((row >> 1) & 3) << 6) + ((row >> 4) << 1) + (row & 1)
        moved = dot(one_where(source == wanted), both).astype(BF16)
        right = dot(moved, widened).reshape(8, 16, 128) + place[None]
        out_ref[g * 8 : (g + 1) * 8, 80:96] = right.astype(BF16)


def right_kernel(got_ref, out_ref):
    rows = got_ref[:, 80:96].reshape(512, 128)
    row, source = iota((128, 1), 0), iota((128, 512), 1)
    start = ((row >> 2) << 4) + ((row & 3) << 1)
    at, lane = iota((128, 128), 0), iota((128, 128), 1)
    total = jnp.zeros((128, 128), F32)
    for plane in range(2):
        for column in range(2):
            picked = dot(one_where(source == start + plane * 8 + column), rows).astype(BF16)
            shift = (plane * 2 + column) * 32
            keep = (lane >= shift) & (lane < shift + 32)
            total = total + dot(picked, one_where((at + shift == lane + 32) & keep))
    out_ref[...] = jnp.broadcast_to(total.astype(BF16)[None], out_ref.shape)


def weight_kernel(after_ref, weight_ref, out_ref, token_ref):
    token_ref[...] = after_ref[...]
    out_ref[...] = jnp.zeros_like(out_ref)
    for q in range(8):
        for k in range(4):
            block = weight_ref[(k * 8 + q) * 32 : (k * 8 + q) * 32 + 32]
            for j in range(4):
                at = (q * 4 + k) * 128 + j * 32
                out_ref[at : at + 32, j * 128 : (j + 1) * 128] = block


def outer_kernel(
    half_ref, got_ref, right_in, pair_ref, came_ref, weight_hbm, out_ref, left, right, joined, update, weight, sem
):
    copy = pltpu.make_async_copy(weight_hbm, weight, sem)
    copy.start()
    row = iota((256, 1), 0)
    wanted = (((row >> 2) & 3) << 6) + (((row >> 4) & 1) << 5) + ((row & 3) << 3) + (row >> 5)
    turn = one_where(iota((256, 256), 1) == wanted)
    for g in range(8):
        part = dot(turn, got_ref[g * 4 : (g + 1) * 4, 0:64].reshape(256, 128)).astype(BF16)
        for q in range(8):
            for p in range(2):
                at = p * 128 + g * 16
                left[at : at + 16, q * 128 : (q + 1) * 128] = part[q * 32 + p * 16 : q * 32 + p * 16 + 16]
    low, _ = lane_masks(128)
    for t in range(8):
        a, b = right_in[2 * t].astype(F32), right_in[2 * t + 1].astype(F32)
        right[0:128, t * 128 : (t + 1) * 128] = jnp.where(low, a, pltpu.roll(b, 64, 1)).astype(BF16)
        right[128:256, t * 128 : (t + 1) * 128] = jnp.where(low, pltpu.roll(a, 64, 1), b).astype(BF16)
    for q in range(8):
        product = (dot(left[:, q * 128 : (q + 1) * 128], right[...], 0, 0) * (1.0 / 256.0)).astype(BF16)
        for t in range(8):
            for k in range(4):
                at = (q * 4 + k) * 128
                joined[t * 32 : (t + 1) * 32, at : at + 128] = product[
                    k * 32 : (k + 1) * 32, t * 128 : (t + 1) * 128
                ]
    copy.wait()
    rows = dot(joined[...], weight[...])
    for t in range(8):
        for j in range(4):
            update[:, t * 4 + j, :] = rows[t * 32 : (t + 1) * 32, j * 128 : (j + 1) * 128]
    out_ref[:, 0:32] = update[...].astype(BF16)

    first = iota((64, 16, 128), 1) // 8 == half_ref[0]
    kept, came = pair_ref[...].astype(F32), came_ref[144:656].reshape(64, 8, 128).astype(F32)
    pairs = jnp.where(first, jnp.concatenate([kept, kept], 1), jnp.concatenate([came, came], 1))
    out_ref[:, 32:64] = pairs.reshape(32, 32, 128).astype(BF16)


def attend_kernel(
    half_ref, got_ref, consts_ref, wq_ref, wk_ref, wv_ref, wg_ref, wo_ref, out_ref, q_s, k_s, v_s, mid_s, gate_s, done_s
):
    mine = half_ref[0] == 0
    factor = 32 ** (-0.5) * math.log2(math.e)
    head_of = iota((512, 128), 1) // 32
    zero, one = jnp.zeros((512, 128), BF16), jnp.ones((512, 128), BF16)
    row, source = iota((512, 1), 0), iota((512, 512), 1)
    wanted = (((row >> 4) & 3) << 7) + (((row >> 1) & 3) << 5) + (((row >> 3) & 1) << 4)
    turn = one_where(source == wanted + ((row >> 6) << 1) + (row & 1))
    shares = got_ref[:, 0:32].reshape(4, 2, 4, 32, 128)
    updates = jnp.concatenate([shares[:, p].reshape(512, 128) for p in range(2)], 1)
    updates = dot(turn, updates)
    for p in range(2):
        update = updates[:, p * 128 : (p + 1) * 128]
        pair = got_ref[:, 32:64].reshape(32, 2, 16, 128)[:, p].reshape(512, 128)
        pair_mid = update + pair.astype(F32) + consts_ref[0:1]
        pair_mid = pair_mid.astype(BF16).astype(F32)
        normed = layer_normalize(pair_mid, consts_ref[1:2])
        split = pair_mid.reshape(32, 2, 8, 128)
        mid_s[...] = jnp.where(mine, split[:, 0], split[:, 1]).reshape(256, 128)
        split = normed.reshape(32, 2, 8, 128)
        asking = jnp.where(mine, split[:, 0], split[:, 1]).reshape(256, 128).astype(BF16)
        normed = normed.astype(BF16)
        q_s[...] = dot(asking, wq_ref[...]).astype(BF16)
        gate_s[...] = dot(asking, wg_ref[...])
        k_s[...] = dot(normed, wk_ref[...]).astype(BF16)
        v_s[...] = dot(normed, wv_ref[...]).astype(BF16)
        keys, values = k_s[...], v_s[...]
        head_keys = [jnp.where(head_of == h, keys, zero) for h in range(PAIR_HEADS)]
        head_values = [
            jnp.concatenate(
                [jnp.where(head_of == h, values, zero), jnp.where(head_of == h, one, zero)], 1
            )
            for h in range(PAIR_HEADS)
        ]
        for c in range(2):
            at = slice(c * 128, (c + 1) * 128)
            queries = q_s[at, :]
            total = jnp.zeros((128, 256), F32)
            for h in range(PAIR_HEADS):
                scores = dot(queries, head_keys[h], 1, 1)
                top = jnp.max(scores, -1, keepdims=True)
                weights = jnp.exp2((scores - top) * factor).astype(BF16)
                total = total + dot(weights, head_values[h])
            attended = total[:, :128] / total[:, 128:] * jax.nn.sigmoid(gate_s[at, :])
            result = mid_s[at, :] + dot(attended.astype(BF16), wo_ref[...])
            done_s[c * 16 : (c + 1) * 16, p * 8 : (p + 1) * 8] = result.reshape(16, 8, 128)
    out_ref[...] = done_s[...].astype(BF16)


def node_kernel(
    count_ref, got_ref, index_ref, query_ref, nodes_ref, coords_ref, wo_ref, penalty_ref, step_ref, nodes_out, coords_out
):
    kv_table = got_ref[:, 64:80].reshape(512, 128)
    place_table = got_ref[:, 80:96].reshape(512, 128)
    local, slots = index_ref.shape
    width, dim = nodes_ref.shape[1], nodes_ref.shape[1] // NODE_HEADS
    lane = iota((1, slots), 1)
    spot = iota((1, local), 1)
    mixed = jnp.zeros((width, local), F32)
    moved = jnp.zeros((3, local), F32)
    for i in range(local):
        picked = one_where(iota((512, slots), 0) == index_ref[i : i + 1, :])
        near = dot(kv_table, picked, 0, 0)
        where = dot(place_table, picked, 0, 0)
        position = [
            where[3 * c : 3 * c + 1] + where[3 * c + 1 : 3 * c + 2] + where[3 * c + 2 : 3 * c + 3]
            for c in range(3)
        ]
        offsets = jnp.concatenate(position, 0) - coords_ref[:, i : i + 1]
        dist2 = jnp.sum(offsets * offsets, 0, keepdims=True)
        products = near[:width] * query_ref[:, i : i + 1]
        logits = jnp.sum(products.reshape(NODE_HEADS, dim, slots), 1) * dim ** (-0.5)
        logits = logits - penalty_ref[...] * dist2
        valid = lane < count_ref[i]
        logits = jnp.where(valid, logits, -1e30)
        powers = jnp.exp(logits - jnp.max(logits, -1, keepdims=True))
        weight = powers / jnp.sum(powers, -1, keepdims=True)
        weight = jnp.where(valid, weight, 0.0)
        low = weight.astype(BF16).astype(F32)
        spread = jnp.broadcast_to(low[:, None, :], (NODE_HEADS, dim, slots)).reshape(width, slots)
        column = jnp.sum(near[width:] * spread, -1, keepdims=True)
        mixed = mixed + jnp.where(spot == i, column, 0.0)
        pull = jnp.sum(weight * step_ref[...], 0, keepdims=True)
        moved = moved + jnp.where(spot == i, jnp.sum(offsets * pull, -1, keepdims=True), 0.0)
    out = nodes_ref[...].astype(F32) + dot(mixed.astype(BF16), wo_ref[...], 0, 0)
    nodes_out[...] = out.astype(BF16)
    coords_out[...] = coords_ref[...] + moved


def with_fetch(body, count):
    def kernel(*refs):
        sources, held, sems = refs[:count], refs[-count - 1 : -1], refs[-1]
        copies = [pltpu.make_async_copy(sources[i], held[i], sems.at[i]) for i in range(count)]
        for copy in copies:
            copy.start()
        for copy in copies:
            copy.wait()
        body(*held, *refs[count : -count - 1])

    return kernel


def call(body, out_shape, args, scratch=(), fetch=False, hbm=0):
    scratch, args = list(scratch), list(args)
    if fetch:
        body = with_fetch(body, len(args))
        scratch += [pltpu.VMEM(a.shape, a.dtype) for a in args] + [pltpu.SemaphoreType.DMA((len(args),))]
        hbm = len(args)
    first = len(args) - hbm
    args = args[:first] + [pltpu.with_memory_space_constraint(a, pltpu.HBM) for a in args[first:]]
    spaces = [pltpu.SMEM if a.ndim == 1 else pltpu.VMEM for a in args[:first]] + [pltpu.HBM] * hbm
    return pl.pallas_call(
        body,
        out_shape=out_shape,
        in_specs=[pl.BlockSpec(memory_space=s) for s in spaces],
        out_specs=jax.tree.map(lambda _: pl.BlockSpec(memory_space=pltpu.VMEM), out_shape),
        scratch_shapes=scratch,
        compiler_params=pltpu.CompilerParams(vmem_limit_bytes=VMEM_LIMIT),
    )(*args)


def shape(dims, kind=BF16):
    return jax.ShapeDtypeStruct(dims, kind)


def on_device(
    homolog_activations,
    alignment_token_ids,
    symbol_lookup_matrix,
    homolog_rescale_vector,
    first_operand_projection,
    second_operand_projection,
    outer_output_weight,
    outer_bias,
    pair,
    pair_norm_gain,
    pair_query_weight,
    pair_key_weight,
    pair_value_weight,
    pair_gate_weight,
    pair_output_weight,
    nodes,
    coords,
    neighbour_index,
    neighbour_count,
    node_norm_gain,
    node_query_weight,
    node_key_weight,
    node_value_weight,
    node_output_weight,
    distance_penalty,
    coordinate_step,
):
    half = lax.axis_index("zh").reshape(1).astype(jnp.int32)
    swap, node_query, consts, factors = call(
        first_kernel,
        (shape((656, 128)), shape((64, 8), F32), shape((8, 128), F32), shape((64, 64))),
        (
            homolog_activations,
            alignment_token_ids,
            symbol_lookup_matrix.T,
            homolog_rescale_vector.reshape(1, -1),
            nodes,
            coords,
            node_norm_gain.reshape(1, -1),
            node_query_weight,
            node_key_weight,
            node_value_weight,
            outer_bias.reshape(1, -1),
            pair_norm_gain.reshape(1, -1),
            pair.reshape(512, 128),
            first_operand_projection.T,
            second_operand_projection.T,
        ),
        fetch=True,
    )
    swapped = lax.ppermute(swap, "zh", [(0, 1), (1, 0)])
    weight, token = call(
        weight_kernel, (shape((4096, 512)), shape((8, 128), F32)), (consts, outer_output_weight)
    )
    spread = call(
        spread_kernel,
        shape((32, 96, 128)),
        (half, token, swap, swapped, factors),
    )
    got = lax.all_to_all(spread, PLANE, split_axis=0, concat_axis=0, tiled=True)
    right = call(right_kernel, shape((8, 128, 128)), (got,))
    right = lax.all_to_all(right, "row", split_axis=0, concat_axis=0, tiled=True)
    right = lax.all_gather(right, "core", axis=0, tiled=True)
    rows = call(
        outer_kernel,
        shape((32, 64, 128)),
        (half, got, right, pair, swapped, weight),
        scratch=(
            pltpu.VMEM((256, 1024), BF16),
            pltpu.VMEM((256, 1024), BF16),
            pltpu.VMEM((256, 4096), BF16),
            pltpu.VMEM((32, 32, 128), F32),
            pltpu.VMEM((4096, 512), BF16),
            pltpu.SemaphoreType.DMA,
        ),
        hbm=1,
    )
    rows = lax.all_to_all(rows, PLANE, split_axis=0, concat_axis=0, tiled=True)
    done = call(
        attend_kernel,
        shape((32, 16, 128)),
        (
            half,
            rows,
            consts,
            pair_query_weight,
            pair_key_weight,
            pair_value_weight,
            pair_gate_weight,
            pair_output_weight,
        ),
        scratch=(
            pltpu.VMEM((256, 128), BF16),
            pltpu.VMEM((512, 128), BF16),
            pltpu.VMEM((512, 128), BF16),
            pltpu.VMEM((256, 128), F32),
            pltpu.VMEM((256, 128), F32),
            pltpu.VMEM((32, 16, 128), F32),
        ),
    )
    done = lax.all_to_all(done, PLANE, split_axis=0, concat_axis=0, tiled=True)
    pair_out = done.reshape(pair.shape)
    nodes_out, coords_out = call(
        node_kernel,
        (shape(nodes.shape), shape(coords.shape, F32)),
        (
            neighbour_count,
            got,
            neighbour_index,
            node_query,
            nodes,
            coords,
            node_output_weight,
            distance_penalty.reshape(-1, 1),
            coordinate_step.reshape(-1, 1),
        ),
    )
    return (pair_out, nodes_out, coords_out)


def solution(mesh):
    fine = Mesh(mesh.devices.reshape(4, 2, 8, 4, 2), ("x", "core", "row", "y", "zh"))
    placed = (
        P(GROUP, "row", None),
        P(GROUP, "row"),
        P(),
        P(),
        P(),
        P(),
        P(),
        P(),
        P("row", GROUP, None),
        P(),
        P(),
        P(),
        P(),
        P(),
        P(),
        P(GROUP, None),
        P(None, GROUP),
        P(GROUP, None),
        P(GROUP),
        P(),
        P(),
        P(),
        P(),
        P(),
        P(),
        P(),
    )
    return jax.shard_map(
        on_device,
        mesh=fine,
        in_specs=placed,
        out_specs=(
            P("row", GROUP, None),
            P(GROUP, None),
            P(None, GROUP),
        ),
        check_vma=False,
    )
```

```python
import math

import jax
import jax.numpy as jnp
from jax import lax
from jax.experimental import pallas as pl
from jax.experimental.pallas import tpu as pltpu
from jax.sharding import Mesh, PartitionSpec as P

F32 = jnp.float32
BF16 = jnp.bfloat16
PAIR_HEADS = 4
NODE_HEADS = 4
PLANE = ("x", "core", "y")
GROUP = ("x", "core", "y", "zh")
VMEM_LIMIT = 24 * 1024 * 1024


def dot(a, b, ca=1, cb=0):
    return lax.dot_general(a, b, (((ca,), (cb,)), ((), ())), preferred_element_type=F32)


def iota(shape, dim):
    return lax.broadcasted_iota(jnp.int32, shape, dim)


def one_where(mask):
    return jnp.where(mask, 1.0, 0.0).astype(BF16)


def layer_normalize(values_in, gain):
    average = jnp.mean(values_in, -1, keepdims=True)
    centred = values_in - average
    variance = jnp.mean(centred * centred, -1, keepdims=True)
    return centred * lax.rsqrt(variance + 1e-05) * gain


def swap_lane_groups(v, low, even):
    t0 = jnp.where(low, v[0], pltpu.roll(v[2], 64, 1))
    t2 = jnp.where(low, pltpu.roll(v[0], 64, 1), v[2])
    t1 = jnp.where(low, v[1], pltpu.roll(v[3], 64, 1))
    t3 = jnp.where(low, pltpu.roll(v[1], 64, 1), v[3])
    return (
        jnp.where(even, t0, pltpu.roll(t1, 32, 1)),
        jnp.where(even, pltpu.roll(t0, 96, 1), t1),
        jnp.where(even, t2, pltpu.roll(t3, 32, 1)),
        jnp.where(even, pltpu.roll(t2, 96, 1), t3),
    )


def lane_masks(rows):
    lane = iota((rows, 128), 1)
    return lane < 64, (lane // 32) % 2 == 0


def first_kernel(
    act_ref,
    tok_ref,
    emb_ref,
    gain_ref,
    nodes_ref,
    coords_ref,
    node_gain_ref,
    wq_ref,
    wk_ref,
    wv_ref,
    bias_ref,
    pair_gain_ref,
    pair_ref,
    wl_ref,
    wr_ref,
    swap_ref,
    query_ref,
    consts_ref,
    factor_ref,
):
    swap_ref[144:656] = pair_ref[...]
    factor_ref[0:32] = wl_ref[...]
    factor_ref[32:64] = wr_ref[...]
    consts_ref[...] = jnp.where(iota((8, 128), 0) == 0, bias_ref[...], pair_gain_ref[...])
    seqs, length, _ = act_ref.shape
    kinds = emb_ref.shape[1]
    emb = emb_ref[...]
    rows = []
    for s in range(seqs):
        picked = one_where(iota((kinds, length), 0) == tok_ref[s : s + 1, :])
        rows.append(act_ref[s].astype(F32) + dot(picked, emb, 0, 1))
    normed = layer_normalize(jnp.concatenate(rows, 0), gain_ref[...]).astype(BF16)
    row, lane = iota((64, 128), 0), iota((64, 128), 1)
    packed = dot(normed[:128], one_where(lane == row)) + dot(normed[128:], one_where(lane == row + 64))
    swap_ref[0:128] = packed.astype(BF16)

    normed = layer_normalize(nodes_ref[...].astype(F32), node_gain_ref[...]).astype(BF16)
    query_ref[...] = dot(wq_ref[...], normed, 0, 1).astype(BF16).astype(F32)
    kv = dot(normed, dot(wk_ref[...], one_where(lane == row)).astype(BF16))
    kv = kv + dot(normed, dot(wv_ref[...], one_where(lane == row + 64)).astype(BF16))
    rest = coords_ref[...]
    placed = jnp.zeros((8, 128), F32)
    for part in range(3):
        piece = rest.astype(BF16)
        rest = rest - piece.astype(F32)
        spot = one_where(iota((3, 128), 1) == iota((3, 128), 0) * 3 + part)
        placed = placed + dot(piece, spot, 0, 0)
    swap_ref[128:144] = jnp.concatenate([kv, placed], 0).astype(BF16)


def spread_kernel(half_ref, own_ref, got_ref, factor_ref, out_ref):
    mine = half_ref[0] == 0
    own, came = own_ref[0:144].astype(F32), got_ref[0:144].astype(F32)
    one = jnp.where(mine, own, came)
    two = jnp.where(mine, came, own)
    row, lane = iota((128, 64), 0), iota((128, 64), 1)
    planes = []
    for block in (one, two):
        packed = block[:128].astype(BF16)
        parts = [dot(packed, one_where(row == lane)), dot(packed, one_where(row == lane + 64))]
        planes.append(jnp.concatenate(parts, 0).astype(BF16))

    row, source = iota((128, 1), 0), iota((128, 256), 1)
    low, even = lane_masks(8)
    for core in range(2):
        pick = one_where(source == ((row >> 5) << 6) + ((row & 31) << 1) + core)
        parts = []
        for p in range(2):
            rows = dot(pick, planes[p]).astype(BF16)
            left = dot(factor_ref[0:32], rows, 1, 1).astype(BF16).astype(F32)
            parts += swap_lane_groups([left[k * 8 : (k + 1) * 8] for k in range(4)], low, even)
        block = jnp.concatenate(parts, 0).astype(BF16)
        for to in range(32):
            if (to // 4) % 2 == core:
                out_ref[to, 0:64] = block

    kv = jnp.concatenate([one[128:136], two[128:136]], 0).astype(BF16)
    out_ref[:, 64:80] = jnp.broadcast_to(kv[None], (32, 16, 128))
    place = jnp.concatenate([one[136:144], two[136:144]], 0)
    widened = dot(factor_ref[32:64], one_where(iota((32, 128), 1) == iota((32, 128), 0) + 32), 0, 0).astype(BF16)
    both = jnp.concatenate(planes, 0)
    for g in range(4):
        row, source = iota((128, 1), 0) + g * 128, iota((128, 512), 1)
        wanted = (((row >> 3) & 1) << 8) + (((row >> 1) & 3) << 6) + ((row >> 4) << 1) + (row & 1)
        moved = dot(one_where(source == wanted), both).astype(BF16)
        right = dot(moved, widened).reshape(8, 16, 128) + place[None]
        out_ref[g * 8 : (g + 1) * 8, 80:96] = right.astype(BF16)


def right_kernel(got_ref, out_ref, token_ref):
    token_ref[...] = jnp.zeros_like(token_ref)
    rows = got_ref[:, 80:96].reshape(512, 128)
    row, source = iota((128, 1), 0), iota((128, 512), 1)
    start = ((row >> 2) << 4) + ((row & 3) << 1)
    at, lane = iota((128, 128), 0), iota((128, 128), 1)
    total = jnp.zeros((128, 128), F32)
    for plane in range(2):
        for column in range(2):
            picked = dot(one_where(source == start + plane * 8 + column), rows).astype(BF16)
            shift = (plane * 2 + column) * 32
            keep = (lane >= shift) & (lane < shift + 32)
            total = total + dot(picked, one_where((at + shift == lane + 32) & keep))
    out_ref[...] = jnp.broadcast_to(total.astype(BF16)[None], out_ref.shape)


def left_kernel(after_ref, got_ref, out_ref, left):
    row = iota((256, 1), 0)
    wanted = (((row >> 2) & 3) << 6) + (((row >> 4) & 1) << 5) + ((row & 3) << 3) + (row >> 5)
    turn = one_where(iota((256, 256), 1) == wanted)
    for g in range(8):
        part = dot(turn, got_ref[g * 4 : (g + 1) * 4, 0:64].reshape(256, 128))
        for q in range(8):
            for p in range(2):
                at = p * 128 + g * 16
                left[at : at + 16, q * 128 : (q + 1) * 128] = part[q * 32 + p * 16 : q * 32 + p * 16 + 16]
    for q in range(8):
        out_ref[q * 128 : (q + 1) * 128] = left[:, q * 128 : (q + 1) * 128].T.astype(BF16)


def outer_kernel(
    place_ref, own_ref, other_ref, right_in, pair_ref, came_ref, weight_ref, out_ref, right, joined, update, weight
):
    weight[...] = jnp.zeros_like(weight)
    for q in range(8):
        for k in range(4):
            block = weight_ref[(k * 8 + q) * 32 : (k * 8 + q) * 32 + 32]
            for j in range(4):
                at = (q * 4 + k) * 128 + j * 32
                weight[at : at + 32, j * 128 : (j + 1) * 128] = block
    low, _ = lane_masks(128)
    for t in range(4):
        a, b = right_in[2 * t].astype(F32), right_in[2 * t + 1].astype(F32)
        right[0:128, t * 128 : (t + 1) * 128] = jnp.where(low, a, pltpu.roll(b, 64, 1)).astype(BF16)
        right[128:256, t * 128 : (t + 1) * 128] = jnp.where(low, pltpu.roll(a, 64, 1), b).astype(BF16)
    for n, left in enumerate((own_ref, other_ref)):
        for q in range(8):
            product = (dot(left[q * 128 : (q + 1) * 128], right[...]) * (1.0 / 256.0)).astype(BF16)
            for t in range(4):
                for k in range(4):
                    at, to = (q * 4 + k) * 128, (n * 4 + t) * 32
                    joined[to : to + 32, at : at + 128] = product[
                        k * 32 : (k + 1) * 32, t * 128 : (t + 1) * 128
                    ]
    first = iota((64, 16, 128), 1) // 8 == place_ref[0]
    kept, came = pair_ref[...].astype(F32), came_ref[144:656].reshape(64, 8, 128).astype(F32)
    pairs = jnp.where(first, jnp.concatenate([kept, kept], 1), jnp.concatenate([came, came], 1))
    out_ref[:, 32:64] = pairs.reshape(32, 32, 128).astype(BF16)
    rows = dot(joined[...], weight[...])
    for t in range(8):
        for j in range(4):
            update[:, t * 4 + j, :] = rows[t * 32 : (t + 1) * 32, j * 128 : (j + 1) * 128]
    core = place_ref[1]
    out_ref[:, pl.ds(pl.multiple_of(core * 16, 16), 16)] = update[:, 0:16].astype(BF16)
    out_ref[:, pl.ds(pl.multiple_of((1 - core) * 16, 16), 16)] = update[:, 16:32].astype(BF16)


def attend_kernel(
    half_ref, got_ref, consts_ref, wq_ref, wk_ref, wv_ref, wg_ref, wo_ref, out_ref, q_s, k_s, v_s, mid_s, gate_s, done_s
):
    mine = half_ref[0] == 0
    factor = 32 ** (-0.5) * math.log2(math.e)
    head_of = iota((512, 128), 1) // 32
    zero, one = jnp.zeros((512, 128), BF16), jnp.ones((512, 128), BF16)
    row, source = iota((512, 1), 0), iota((512, 512), 1)
    turn = one_where(source == (((row >> 1) & 31) << 4) + ((row >> 6) << 1) + (row & 1))
    shares = got_ref[:, 0:32].reshape(32, 2, 16, 128)
    updates = jnp.concatenate([shares[:, p].reshape(512, 128) for p in range(2)], 1)
    updates = dot(turn, updates)
    for p in range(2):
        update = updates[:, p * 128 : (p + 1) * 128]
        pair = got_ref[:, 32:64].reshape(32, 2, 16, 128)[:, p].reshape(512, 128)
        pair_mid = update + pair.astype(F32) + consts_ref[0:1]
        pair_mid = pair_mid.astype(BF16).astype(F32)
        normed = layer_normalize(pair_mid, consts_ref[1:2])
        split = pair_mid.reshape(32, 2, 8, 128)
        mid_s[...] = jnp.where(mine, split[:, 0], split[:, 1]).reshape(256, 128)
        split = normed.reshape(32, 2, 8, 128)
        asking = jnp.where(mine, split[:, 0], split[:, 1]).reshape(256, 128).astype(BF16)
        normed = normed.astype(BF16)
        q_s[...] = dot(asking, wq_ref[...]).astype(BF16)
        gate_s[...] = dot(asking, wg_ref[...])
        k_s[...] = dot(normed, wk_ref[...]).astype(BF16)
        v_s[...] = dot(normed, wv_ref[...]).astype(BF16)
        keys, values = k_s[...], v_s[...]
        head_keys = [jnp.where(head_of == h, keys, zero) for h in range(PAIR_HEADS)]
        head_values = [
            jnp.concatenate(
                [jnp.where(head_of == h, values, zero), jnp.where(head_of == h, one, zero)], 1
            )
            for h in range(PAIR_HEADS)
        ]
        queries = q_s[...]
        total = jnp.zeros((256, 256), F32)
        for h in range(PAIR_HEADS):
            scores = dot(queries, head_keys[h], 1, 1)
            top = jnp.max(scores, -1, keepdims=True)
            weights = jnp.exp2((scores - top) * factor).astype(BF16)
            total = total + dot(weights, head_values[h])
        attended = total[:, :128] / total[:, 128:] * jax.nn.sigmoid(gate_s[...])
        result = mid_s[...] + dot(attended.astype(BF16), wo_ref[...])
        done_s[:, p * 8 : (p + 1) * 8] = result.reshape(32, 8, 128)
    out_ref[...] = done_s[...].astype(BF16)


def node_kernel(
    count_ref, got_ref, index_ref, query_ref, nodes_ref, coords_ref, wo_ref, penalty_ref, step_ref, nodes_out, coords_out
):
    kv_table = got_ref[:, 64:80].reshape(512, 128)
    place_table = got_ref[:, 80:96].reshape(512, 128)
    local, slots = index_ref.shape
    width, dim = nodes_ref.shape[1], nodes_ref.shape[1] // NODE_HEADS
    lane = iota((1, slots), 1)
    spot = iota((1, local), 1)
    mixed = jnp.zeros((width, local), F32)
    moved = jnp.zeros((3, local), F32)
    for i in range(local):
        picked = one_where(iota((512, slots), 0) == index_ref[i : i + 1, :])
        near = dot(kv_table, picked, 0, 0)
        where = dot(place_table, picked, 0, 0)
        position = [
            where[3 * c : 3 * c + 1] + where[3 * c + 1 : 3 * c + 2] + where[3 * c + 2 : 3 * c + 3]
            for c in range(3)
        ]
        offsets = jnp.concatenate(position, 0) - coords_ref[:, i : i + 1]
        dist2 = jnp.sum(offsets * offsets, 0, keepdims=True)
        products = near[:width] * query_ref[:, i : i + 1]
        logits = jnp.sum(products.reshape(NODE_HEADS, dim, slots), 1) * dim ** (-0.5)
        logits = logits - penalty_ref[...] * dist2
        valid = lane < count_ref[i]
        logits = jnp.where(valid, logits, -1e30)
        powers = jnp.exp(logits - jnp.max(logits, -1, keepdims=True))
        weight = powers / jnp.sum(powers, -1, keepdims=True)
        weight = jnp.where(valid, weight, 0.0)
        low = weight.astype(BF16).astype(F32)
        spread = jnp.broadcast_to(low[:, None, :], (NODE_HEADS, dim, slots)).reshape(width, slots)
        column = jnp.sum(near[width:] * spread, -1, keepdims=True)
        mixed = mixed + jnp.where(spot == i, column, 0.0)
        pull = jnp.sum(weight * step_ref[...], 0, keepdims=True)
        moved = moved + jnp.where(spot == i, jnp.sum(offsets * pull, -1, keepdims=True), 0.0)
    out = nodes_ref[...].astype(F32) + dot(mixed.astype(BF16), wo_ref[...], 0, 0)
    nodes_out[...] = out.astype(BF16)
    coords_out[...] = coords_ref[...] + moved


def with_fetch(body, count):
    def kernel(*refs):
        sources, held, sems = refs[:count], refs[-count - 1 : -1], refs[-1]
        copies = [pltpu.make_async_copy(sources[i], held[i], sems.at[i]) for i in range(count)]
        for copy in copies:
            copy.start()
        for copy in copies:
            copy.wait()
        body(*held, *refs[count : -count - 1])

    return kernel


def call(body, out_shape, args, scratch=(), fetch=False, hbm=0):
    scratch, args = list(scratch), list(args)
    if fetch:
        body = with_fetch(body, len(args))
        scratch += [pltpu.VMEM(a.shape, a.dtype) for a in args] + [pltpu.SemaphoreType.DMA((len(args),))]
        hbm = len(args)
    first = len(args) - hbm
    args = args[:first] + [pltpu.with_memory_space_constraint(a, pltpu.HBM) for a in args[first:]]
    spaces = [pltpu.SMEM if a.ndim == 1 else pltpu.VMEM for a in args[:first]] + [pltpu.HBM] * hbm
    return pl.pallas_call(
        body,
        out_shape=out_shape,
        in_specs=[pl.BlockSpec(memory_space=s) for s in spaces],
        out_specs=jax.tree.map(lambda _: pl.BlockSpec(memory_space=pltpu.VMEM), out_shape),
        scratch_shapes=scratch,
        compiler_params=pltpu.CompilerParams(vmem_limit_bytes=VMEM_LIMIT),
    )(*args)


def shape(dims, kind=BF16):
    return jax.ShapeDtypeStruct(dims, kind)


def on_device(
    homolog_activations,
    alignment_token_ids,
    symbol_lookup_matrix,
    homolog_rescale_vector,
    first_operand_projection,
    second_operand_projection,
    outer_output_weight,
    outer_bias,
    pair,
    pair_norm_gain,
    pair_query_weight,
    pair_key_weight,
    pair_value_weight,
    pair_gate_weight,
    pair_output_weight,
    nodes,
    coords,
    neighbour_index,
    neighbour_count,
    node_norm_gain,
    node_query_weight,
    node_key_weight,
    node_value_weight,
    node_output_weight,
    distance_penalty,
    coordinate_step,
):
    half = lax.axis_index("zh").reshape(1).astype(jnp.int32)
    swap, node_query, consts, factors = call(
        first_kernel,
        (shape((656, 128)), shape((64, 8), F32), shape((8, 128), F32), shape((64, 64))),
        (
            homolog_activations,
            alignment_token_ids,
            symbol_lookup_matrix.T,
            homolog_rescale_vector.reshape(1, -1),
            nodes,
            coords,
            node_norm_gain.reshape(1, -1),
            node_query_weight,
            node_key_weight,
            node_value_weight,
            outer_bias.reshape(1, -1),
            pair_norm_gain.reshape(1, -1),
            pair.reshape(512, 128),
            first_operand_projection.T,
            second_operand_projection.T,
        ),
        fetch=True,
    )
    swapped = lax.ppermute(swap, "zh", [(0, 1), (1, 0)])
    spread = call(
        spread_kernel,
        shape((32, 96, 128)),
        (half, swap, swapped, factors),
    )
    got = lax.all_to_all(spread, PLANE, split_axis=0, concat_axis=0, tiled=True)
    right, token = call(right_kernel, (shape((8, 128, 128)), shape((8, 128), F32)), (got,))
    right = lax.all_to_all(right, "row", split_axis=0, concat_axis=0, tiled=True)
    left = call(
        left_kernel, shape((1024, 256)), (token, got), scratch=(pltpu.VMEM((256, 1024), F32),)
    )
    other = lax.ppermute(left, "core", [(0, 1), (1, 0)])
    place = jnp.stack([lax.axis_index("zh"), lax.axis_index("core")]).astype(jnp.int32)
    rows = call(
        outer_kernel,
        shape((32, 64, 128)),
        (place, left, other, right, pair, swapped, outer_output_weight),
        scratch=(
            pltpu.VMEM((256, 512), BF16),
            pltpu.VMEM((256, 4096), BF16),
            pltpu.VMEM((32, 32, 128), F32),
            pltpu.VMEM((4096, 512), BF16),
        ),
    )
    rows = lax.all_to_all(rows, PLANE, split_axis=0, concat_axis=0, tiled=True)
    done = call(
        attend_kernel,
        shape((32, 16, 128)),
        (
            half,
            rows,
            consts,
            pair_query_weight,
            pair_key_weight,
            pair_value_weight,
            pair_gate_weight,
            pair_output_weight,
        ),
        scratch=(
            pltpu.VMEM((256, 128), BF16),
            pltpu.VMEM((512, 128), BF16),
            pltpu.VMEM((512, 128), BF16),
            pltpu.VMEM((256, 128), F32),
            pltpu.VMEM((256, 128), F32),
            pltpu.VMEM((32, 16, 128), F32),
        ),
    )
    done = lax.all_to_all(done, PLANE, split_axis=0, concat_axis=0, tiled=True)
    pair_out = done.reshape(pair.shape)
    nodes_out, coords_out = call(
        node_kernel,
        (shape(nodes.shape), shape(coords.shape, F32)),
        (
            neighbour_count,
            got,
            neighbour_index,
            node_query,
            nodes,
            coords,
            node_output_weight,
            distance_penalty.reshape(-1, 1),
            coordinate_step.reshape(-1, 1),
        ),
    )
    return (pair_out, nodes_out, coords_out)


def solution(mesh):
    fine = Mesh(mesh.devices.reshape(4, 2, 8, 4, 2), ("x", "core", "row", "y", "zh"))
    placed = (
        P(GROUP, "row", None),
        P(GROUP, "row"),
        P(),
        P(),
        P(),
        P(),
        P(),
        P(),
        P("row", GROUP, None),
        P(),
        P(),
        P(),
        P(),
        P(),
        P(),
        P(GROUP, None),
        P(None, GROUP),
        P(GROUP, None),
        P(GROUP),
        P(),
        P(),
        P(),
        P(),
        P(),
        P(),
        P(),
    )
    return jax.shard_map(
        on_device,
        mesh=fine,
        in_specs=placed,
        out_specs=(
            P("row", GROUP, None),
            P(GROUP, None),
            P(None, GROUP),
        ),
        check_vma=False,
    )
```

```python
import math

import jax
import jax.numpy as jnp
from jax import lax
from jax.experimental import pallas as pl
from jax.experimental.pallas import tpu as pltpu
from jax.sharding import Mesh, PartitionSpec as P

F32 = jnp.float32
BF16 = jnp.bfloat16
PAIR_HEADS = 4
NODE_HEADS = 4
PLANE = ("x", "core", "y")
GROUP = ("x", "core", "y", "zh")
VMEM_LIMIT = 24 * 1024 * 1024


def dot(a, b, ca=1, cb=0):
    return lax.dot_general(a, b, (((ca,), (cb,)), ((), ())), preferred_element_type=F32)


def iota(shape, dim):
    return lax.broadcasted_iota(jnp.int32, shape, dim)


def one_where(mask):
    return jnp.where(mask, 1.0, 0.0).astype(BF16)


def layer_normalize(values_in, gain):
    average = jnp.mean(values_in, -1, keepdims=True)
    centred = values_in - average
    variance = jnp.mean(centred * centred, -1, keepdims=True)
    return centred * lax.rsqrt(variance + 1e-05) * gain


def swap_lane_groups(v, low, even):
    t0 = jnp.where(low, v[0], pltpu.roll(v[2], 64, 1))
    t2 = jnp.where(low, pltpu.roll(v[0], 64, 1), v[2])
    t1 = jnp.where(low, v[1], pltpu.roll(v[3], 64, 1))
    t3 = jnp.where(low, pltpu.roll(v[1], 64, 1), v[3])
    return (
        jnp.where(even, t0, pltpu.roll(t1, 32, 1)),
        jnp.where(even, pltpu.roll(t0, 96, 1), t1),
        jnp.where(even, t2, pltpu.roll(t3, 32, 1)),
        jnp.where(even, pltpu.roll(t2, 96, 1), t3),
    )


def lane_masks(rows):
    lane = iota((rows, 128), 1)
    return lane < 64, (lane // 32) % 2 == 0


def first_kernel(
    act_ref,
    tok_ref,
    emb_ref,
    gain_ref,
    nodes_ref,
    coords_ref,
    node_gain_ref,
    wq_ref,
    wk_ref,
    wv_ref,
    bias_ref,
    pair_gain_ref,
    pair_ref,
    wl_ref,
    wr_ref,
    swap_ref,
    query_ref,
    consts_ref,
    factor_ref,
):
    swap_ref[144:656] = pair_ref[...]
    factor_ref[0:32] = wl_ref[...]
    factor_ref[32:64] = wr_ref[...]
    consts_ref[...] = jnp.where(iota((8, 128), 0) == 0, bias_ref[...], pair_gain_ref[...])
    seqs, length, _ = act_ref.shape
    kinds = emb_ref.shape[1]
    emb = emb_ref[...]
    rows = []
    for s in range(seqs):
        picked = one_where(iota((kinds, length), 0) == tok_ref[s : s + 1, :])
        rows.append(act_ref[s].astype(F32) + dot(picked, emb, 0, 1))
    normed = layer_normalize(jnp.concatenate(rows, 0), gain_ref[...]).astype(BF16)
    row, lane = iota((64, 128), 0), iota((64, 128), 1)
    packed = dot(normed[:128], one_where(lane == row)) + dot(normed[128:], one_where(lane == row + 64))
    swap_ref[0:128] = packed.astype(BF16)

    normed = layer_normalize(nodes_ref[...].astype(F32), node_gain_ref[...]).astype(BF16)
    query_ref[...] = dot(wq_ref[...], normed, 0, 1).astype(BF16).astype(F32)
    kv = dot(normed, dot(wk_ref[...], one_where(lane == row)).astype(BF16))
    kv = kv + dot(normed, dot(wv_ref[...], one_where(lane == row + 64)).astype(BF16))
    rest = coords_ref[...]
    placed = jnp.zeros((8, 128), F32)
    for part in range(3):
        piece = rest.astype(BF16)
        rest = rest - piece.astype(F32)
        spot = one_where(iota((3, 128), 1) == iota((3, 128), 0) * 3 + part)
        placed = placed + dot(piece, spot, 0, 0)
    swap_ref[128:144] = jnp.concatenate([kv, placed], 0).astype(BF16)


def spread_kernel(after_ref, block_ref, factor_ref, out_ref):
    packed = block_ref[0:128]
    row, lane = iota((128, 64), 0), iota((128, 64), 1)
    parts = [dot(packed, one_where(row == lane)), dot(packed, one_where(row == lane + 64))]
    plane = jnp.concatenate(parts, 0).astype(BF16)

    row, source = iota((128, 1), 0), iota((128, 256), 1)
    low, even = lane_masks(8)
    for core in range(2):
        pick = one_where(source == ((row >> 5) << 6) + ((row & 31) << 1) + core)
        rows = dot(pick, plane).astype(BF16)
        left = dot(factor_ref[0:32], rows, 1, 1).astype(BF16).astype(F32)
        parts = swap_lane_groups([left[k * 8 : (k + 1) * 8] for k in range(4)], low, even)
        block = jnp.concatenate(parts, 0).astype(BF16)
        for to in range(32):
            if (to // 4) % 2 == core:
                out_ref[to, 0:32] = block

    nodes = block_ref[128:144].astype(F32)
    widened = dot(factor_ref[32:64], one_where(iota((32, 128), 1) == iota((32, 128), 0) + 32), 0, 0).astype(BF16)
    row, source = iota((256, 1), 0), iota((256, 256), 1)
    wanted = (((row >> 1) & 3) << 6) + ((row >> 3) << 1) + (row & 1)
    moved = dot(one_where(source == wanted), plane).astype(BF16)
    right = dot(moved, widened).reshape(32, 8, 128) + nodes[None, 8:16]
    kv = jnp.broadcast_to(nodes[None, 0:8], (32, 8, 128))
    out_ref[:, 32:48] = jnp.concatenate([kv, right], 1).astype(BF16)


def right_kernel(own_ref, came_ref, out_ref, token_ref):
    token_ref[...] = jnp.zeros_like(token_ref)
    row, source = iota((128, 1), 0), iota((128, 512), 1)
    start = ((row >> 2) << 4) + ((row & 3) << 1) + 8
    at, lane = iota((128, 128), 0), iota((128, 128), 1)
    total = jnp.zeros((128, 128), F32)
    for plane, got_ref in enumerate((own_ref, came_ref)):
        rows = got_ref[:, 32:48].reshape(512, 128)
        for column in range(2):
            picked = dot(one_where(source == start + column), rows).astype(BF16)
            shift = (plane * 2 + column) * 32
            keep = (lane >= shift) & (lane < shift + 32)
            total = total + dot(picked, one_where((at + shift == lane + 32) & keep))
    out_ref[...] = jnp.broadcast_to(total.astype(BF16)[None], out_ref.shape)


def left_kernel(after_ref, own_ref, came_ref, out_ref, left):
    row = iota((256, 1), 0)
    wanted = (((row >> 2) & 7) << 5) + ((row & 3) << 3) + (row >> 5)
    turn = one_where(iota((256, 256), 1) == wanted)
    for p, got_ref in enumerate((own_ref, came_ref)):
        for g in range(4):
            part = dot(turn, got_ref[g * 8 : (g + 1) * 8, 0:32].reshape(256, 128))
            at = p * 128 + g * 32
            for q in range(8):
                left[at : at + 32, q * 128 : (q + 1) * 128] = part[q * 32 : (q + 1) * 32]
    for q in range(8):
        out_ref[q * 128 : (q + 1) * 128] = left[:, q * 128 : (q + 1) * 128].T.astype(BF16)


def outer_kernel(
    place_ref, own_ref, other_ref, right_in, pair_ref, came_ref, weight_ref, out_ref, right, joined, update, weight
):
    weight[...] = jnp.zeros_like(weight)
    for q in range(8):
        for k in range(4):
            block = weight_ref[(k * 8 + q) * 32 : (k * 8 + q) * 32 + 32]
            for j in range(4):
                at = (q * 4 + k) * 128 + j * 32
                weight[at : at + 32, j * 128 : (j + 1) * 128] = block
    low, _ = lane_masks(128)
    for t in range(4):
        a, b = right_in[2 * t].astype(F32), right_in[2 * t + 1].astype(F32)
        right[0:128, t * 128 : (t + 1) * 128] = jnp.where(low, a, pltpu.roll(b, 64, 1)).astype(BF16)
        right[128:256, t * 128 : (t + 1) * 128] = jnp.where(low, pltpu.roll(a, 64, 1), b).astype(BF16)
    for n, left in enumerate((own_ref, other_ref)):
        for q in range(8):
            product = (dot(left[q * 128 : (q + 1) * 128], right[...]) * (1.0 / 256.0)).astype(BF16)
            for t in range(4):
                for k in range(4):
                    at, to = (q * 4 + k) * 128, (n * 4 + t) * 32
                    joined[to : to + 32, at : at + 128] = product[
                        k * 32 : (k + 1) * 32, t * 128 : (t + 1) * 128
                    ]
    first = iota((64, 16, 128), 1) // 8 == place_ref[0]
    kept, came = pair_ref[...].astype(F32), came_ref[144:656].reshape(64, 8, 128).astype(F32)
    pairs = jnp.where(first, jnp.concatenate([kept, kept], 1), jnp.concatenate([came, came], 1))
    out_ref[:, 32:64] = pairs.reshape(32, 32, 128).astype(BF16)
    rows = dot(joined[...], weight[...])
    for t in range(8):
        for j in range(4):
            update[:, t * 4 + j, :] = rows[t * 32 : (t + 1) * 32, j * 128 : (j + 1) * 128]
    core = place_ref[1]
    out_ref[:, pl.ds(pl.multiple_of(core * 16, 16), 16)] = update[:, 0:16].astype(BF16)
    out_ref[:, pl.ds(pl.multiple_of((1 - core) * 16, 16), 16)] = update[:, 16:32].astype(BF16)


def attend_kernel(
    half_ref, got_ref, consts_ref, wq_ref, wk_ref, wv_ref, wg_ref, wo_ref, out_ref, q_s, k_s, v_s, mid_s, gate_s, done_s
):
    mine = half_ref[0] == 0
    factor = 32 ** (-0.5) * math.log2(math.e)
    head_of = iota((512, 128), 1) // 32
    zero, one = jnp.zeros((512, 128), BF16), jnp.ones((512, 128), BF16)
    row, source = iota((512, 1), 0), iota((512, 512), 1)
    turn = one_where(source == (((row >> 1) & 31) << 4) + ((row >> 6) << 1) + (row & 1))
    shares = got_ref[:, 0:32].reshape(32, 2, 16, 128)
    updates = jnp.concatenate([shares[:, p].reshape(512, 128) for p in range(2)], 1)
    updates = dot(turn, updates)
    for p in range(2):
        update = updates[:, p * 128 : (p + 1) * 128]
        pair = got_ref[:, 32:64].reshape(32, 2, 16, 128)[:, p].reshape(512, 128)
        pair_mid = update + pair.astype(F32) + consts_ref[0:1]
        pair_mid = pair_mid.astype(BF16).astype(F32)
        normed = layer_normalize(pair_mid, consts_ref[1:2])
        split = pair_mid.reshape(32, 2, 8, 128)
        mid_s[...] = jnp.where(mine, split[:, 0], split[:, 1]).reshape(256, 128)
        split = normed.reshape(32, 2, 8, 128)
        asking = jnp.where(mine, split[:, 0], split[:, 1]).reshape(256, 128).astype(BF16)
        normed = normed.astype(BF16)
        asked = dot(asking, jnp.concatenate([wq_ref[...], wg_ref[...]], 1))
        q_s[...] = asked[:, :128].astype(BF16)
        gate_s[...] = asked[:, 128:]
        given = dot(normed, jnp.concatenate([wk_ref[...], wv_ref[...]], 1)).astype(BF16)
        keys, values = given[:, :128], given[:, 128:]
        head_keys = [jnp.where(head_of == h, keys, zero) for h in range(PAIR_HEADS)]
        head_values = [
            jnp.concatenate(
                [jnp.where(head_of == h, values, zero), jnp.where(head_of == h, one, zero)], 1
            )
            for h in range(PAIR_HEADS)
        ]
        queries = q_s[...]
        total = jnp.zeros((256, 256), F32)
        for h in range(PAIR_HEADS):
            scores = dot(queries, head_keys[h], 1, 1)
            top = jnp.max(scores, -1, keepdims=True)
            weights = jnp.exp2((scores - top) * factor).astype(BF16)
            total = total + dot(weights, head_values[h])
        attended = total[:, :128] / total[:, 128:] * jax.nn.sigmoid(gate_s[...])
        result = mid_s[...] + dot(attended.astype(BF16), wo_ref[...])
        done_s[:, p * 8 : (p + 1) * 8] = result.reshape(32, 8, 128)
    out_ref[...] = done_s[...].astype(BF16)


def node_kernel(
    count_ref, half_ref, after_ref, own_ref, came_ref, index_ref, query_ref, nodes_ref, coords_ref, wo_ref, penalty_ref, step_ref, nodes_out, coords_out, token_ref
):
    token_ref[...] = after_ref[...]
    tables = [[], []]
    for got_ref in (own_ref, came_ref):
        both = got_ref[:, 32:48].reshape(32, 2, 8, 128)
        for n in range(2):
            tables[n].append(both[:, n].reshape(256, 128))
    kv_table, place_table = [jnp.concatenate(t, 0) for t in tables]
    index = index_ref[...]
    index = ((index >> 4) << 3) + (index & 7) + ((((index >> 3) & 1) ^ half_ref[0]) << 8)
    local, slots = index_ref.shape
    width, dim = nodes_ref.shape[1], nodes_ref.shape[1] // NODE_HEADS
    lane = iota((1, slots), 1)
    spot = iota((1, local), 1)
    mixed = jnp.zeros((width, local), F32)
    moved = jnp.zeros((3, local), F32)
    for i in range(local):
        picked = one_where(iota((512, slots), 0) == index[i : i + 1, :])
        near = dot(kv_table, picked, 0, 0)
        where = dot(place_table, picked, 0, 0)
        position = [
            where[3 * c : 3 * c + 1] + where[3 * c + 1 : 3 * c + 2] + where[3 * c + 2 : 3 * c + 3]
            for c in range(3)
        ]
        offsets = jnp.concatenate(position, 0) - coords_ref[:, i : i + 1]
        dist2 = jnp.sum(offsets * offsets, 0, keepdims=True)
        products = near[:width] * query_ref[:, i : i + 1]
        logits = jnp.sum(products.reshape(NODE_HEADS, dim, slots), 1) * dim ** (-0.5)
        logits = logits - penalty_ref[...] * dist2
        valid = lane < count_ref[i]
        logits = jnp.where(valid, logits, -1e30)
        powers = jnp.exp(logits - jnp.max(logits, -1, keepdims=True))
        weight = powers / jnp.sum(powers, -1, keepdims=True)
        weight = jnp.where(valid, weight, 0.0)
        low = weight.astype(BF16).astype(F32)
        spread = jnp.broadcast_to(low[:, None, :], (NODE_HEADS, dim, slots)).reshape(width, slots)
        column = jnp.sum(near[width:] * spread, -1, keepdims=True)
        mixed = mixed + jnp.where(spot == i, column, 0.0)
        pull = jnp.sum(weight * step_ref[...], 0, keepdims=True)
        moved = moved + jnp.where(spot == i, jnp.sum(offsets * pull, -1, keepdims=True), 0.0)
    out = nodes_ref[...].astype(F32) + dot(mixed.astype(BF16), wo_ref[...], 0, 0)
    nodes_out[...] = out.astype(BF16)
    coords_out[...] = coords_ref[...] + moved


def with_fetch(body, count):
    def kernel(*refs):
        sources, held, sems = refs[:count], refs[-count - 1 : -1], refs[-1]
        copies = [pltpu.make_async_copy(sources[i], held[i], sems.at[i]) for i in range(count)]
        for copy in copies:
            copy.start()
        for copy in copies:
            copy.wait()
        body(*held, *refs[count : -count - 1])

    return kernel


def call(body, out_shape, args, scratch=(), fetch=False, hbm=0, cost=None):
    scratch, args = list(scratch), list(args)
    if fetch:
        body = with_fetch(body, len(args))
        scratch += [pltpu.VMEM(a.shape, a.dtype) for a in args] + [pltpu.SemaphoreType.DMA((len(args),))]
        hbm = len(args)
    first = len(args) - hbm
    args = args[:first] + [pltpu.with_memory_space_constraint(a, pltpu.HBM) for a in args[first:]]
    spaces = [pltpu.SMEM if a.ndim == 1 else pltpu.VMEM for a in args[:first]] + [pltpu.HBM] * hbm
    return pl.pallas_call(
        body,
        out_shape=out_shape,
        in_specs=[pl.BlockSpec(memory_space=s) for s in spaces],
        out_specs=jax.tree.map(lambda _: pl.BlockSpec(memory_space=pltpu.VMEM), out_shape),
        scratch_shapes=scratch,
        compiler_params=pltpu.CompilerParams(vmem_limit_bytes=VMEM_LIMIT),
        cost_estimate=cost,
    )(*args)


def shape(dims, kind=BF16):
    return jax.ShapeDtypeStruct(dims, kind)


def on_device(
    homolog_activations,
    alignment_token_ids,
    symbol_lookup_matrix,
    homolog_rescale_vector,
    first_operand_projection,
    second_operand_projection,
    outer_output_weight,
    outer_bias,
    pair,
    pair_norm_gain,
    pair_query_weight,
    pair_key_weight,
    pair_value_weight,
    pair_gate_weight,
    pair_output_weight,
    nodes,
    coords,
    neighbour_index,
    neighbour_count,
    node_norm_gain,
    node_query_weight,
    node_key_weight,
    node_value_weight,
    node_output_weight,
    distance_penalty,
    coordinate_step,
):
    half = lax.axis_index("zh").reshape(1).astype(jnp.int32)
    swap, node_query, consts, factors = call(
        first_kernel,
        (shape((656, 128)), shape((64, 8), F32), shape((8, 128), F32), shape((64, 64))),
        (
            homolog_activations,
            alignment_token_ids,
            symbol_lookup_matrix.T,
            homolog_rescale_vector.reshape(1, -1),
            nodes,
            coords,
            node_norm_gain.reshape(1, -1),
            node_query_weight,
            node_key_weight,
            node_value_weight,
            outer_bias.reshape(1, -1),
            pair_norm_gain.reshape(1, -1),
            pair.reshape(512, 128),
            first_operand_projection.T,
            second_operand_projection.T,
        ),
        fetch=True,
    )
    swapped = lax.ppermute(swap, "zh", [(0, 1), (1, 0)])
    spread = call(spread_kernel, shape((32, 48, 128)), (consts, swap, factors))
    own = lax.all_to_all(spread, PLANE, split_axis=0, concat_axis=0, tiled=True)
    long = pl.CostEstimate(flops=1 << 36, bytes_accessed=1 << 28, transcendentals=0)
    spread = call(spread_kernel, shape((32, 48, 128)), (consts, swapped, factors), cost=long)
    got = lax.all_to_all(spread, PLANE, split_axis=0, concat_axis=0, tiled=True)
    right, token = call(right_kernel, (shape((8, 128, 128)), shape((8, 128), F32)), (own, got))
    right = lax.all_to_all(right, "row", split_axis=0, concat_axis=0, tiled=True)
    nodes_out, coords_out, token = call(
        node_kernel,
        (shape(nodes.shape), shape(coords.shape, F32), shape((8, 128), F32)),
        (
            neighbour_count,
            half,
            token,
            own,
            got,
            neighbour_index,
            node_query,
            nodes,
            coords,
            node_output_weight,
            distance_penalty.reshape(-1, 1),
            coordinate_step.reshape(-1, 1),
        ),
    )
    left = call(
        left_kernel, shape((1024, 256)), (token, own, got), scratch=(pltpu.VMEM((256, 1024), F32),)
    )
    other = lax.ppermute(left, "core", [(0, 1), (1, 0)])
    place = jnp.stack([lax.axis_index("zh"), lax.axis_index("core")]).astype(jnp.int32)
    rows = call(
        outer_kernel,
        shape((32, 64, 128)),
        (place, left, other, right, pair, swapped, outer_output_weight),
        scratch=(
            pltpu.VMEM((256, 512), BF16),
            pltpu.VMEM((256, 4096), BF16),
            pltpu.VMEM((32, 32, 128), F32),
            pltpu.VMEM((4096, 512), BF16),
        ),
    )
    rows = lax.all_to_all(rows, PLANE, split_axis=0, concat_axis=0, tiled=True)
    done = call(
        attend_kernel,
        shape((32, 16, 128)),
        (
            half,
            rows,
            consts,
            pair_query_weight,
            pair_key_weight,
            pair_value_weight,
            pair_gate_weight,
            pair_output_weight,
        ),
        scratch=(
            pltpu.VMEM((256, 128), BF16),
            pltpu.VMEM((512, 128), BF16),
            pltpu.VMEM((512, 128), BF16),
            pltpu.VMEM((256, 128), F32),
            pltpu.VMEM((256, 128), F32),
            pltpu.VMEM((32, 16, 128), F32),
        ),
    )
    done = lax.all_to_all(done, PLANE, split_axis=0, concat_axis=0, tiled=True)
    pair_out = done.reshape(pair.shape)
    return (pair_out, nodes_out, coords_out)


def solution(mesh):
    fine = Mesh(mesh.devices.reshape(4, 2, 8, 4, 2), ("x", "core", "row", "y", "zh"))
    placed = (
        P(GROUP, "row", None),
        P(GROUP, "row"),
        P(),
        P(),
        P(),
        P(),
        P(),
        P(),
        P("row", GROUP, None),
        P(),
        P(),
        P(),
        P(),
        P(),
        P(),
        P(GROUP, None),
        P(None, GROUP),
        P(GROUP, None),
        P(GROUP),
        P(),
        P(),
        P(),
        P(),
        P(),
        P(),
        P(),
    )
    return jax.shard_map(
        on_device,
        mesh=fine,
        in_specs=placed,
        out_specs=(
            P("row", GROUP, None),
            P(GROUP, None),
            P(None, GROUP),
        ),
        check_vma=False,
    )
```

```python
import math

import jax
import jax.numpy as jnp
from jax import lax
from jax.experimental import pallas as pl
from jax.experimental.pallas import tpu as pltpu
from jax.sharding import Mesh, PartitionSpec as P

F32 = jnp.float32
BF16 = jnp.bfloat16
PAIR_HEADS = 4
NODE_HEADS = 4
PLANE = ("x", "core", "y")
GROUP = ("x", "core", "y", "zh")
VMEM_LIMIT = 24 * 1024 * 1024


def dot(a, b, ca=1, cb=0):
    return lax.dot_general(a, b, (((ca,), (cb,)), ((), ())), preferred_element_type=F32)


def iota(shape, dim):
    return lax.broadcasted_iota(jnp.int32, shape, dim)


def one_where(mask):
    return jnp.where(mask, 1.0, 0.0).astype(BF16)


def layer_normalize(values_in, gain):
    average = jnp.mean(values_in, -1, keepdims=True)
    centred = values_in - average
    variance = jnp.mean(centred * centred, -1, keepdims=True)
    return centred * lax.rsqrt(variance + 1e-05) * gain


def swap_lane_groups(v, low, even):
    t0 = jnp.where(low, v[0], pltpu.roll(v[2], 64, 1))
    t2 = jnp.where(low, pltpu.roll(v[0], 64, 1), v[2])
    t1 = jnp.where(low, v[1], pltpu.roll(v[3], 64, 1))
    t3 = jnp.where(low, pltpu.roll(v[1], 64, 1), v[3])
    return (
        jnp.where(even, t0, pltpu.roll(t1, 32, 1)),
        jnp.where(even, pltpu.roll(t0, 96, 1), t1),
        jnp.where(even, t2, pltpu.roll(t3, 32, 1)),
        jnp.where(even, pltpu.roll(t2, 96, 1), t3),
    )


def lane_masks(rows):
    lane = iota((rows, 128), 1)
    return lane < 64, (lane // 32) % 2 == 0


def first_kernel(
    act_ref,
    tok_ref,
    emb_ref,
    gain_ref,
    nodes_ref,
    coords_ref,
    node_gain_ref,
    wq_ref,
    wk_ref,
    wv_ref,
    bias_ref,
    pair_gain_ref,
    pair_ref,
    wl_ref,
    wr_ref,
    swap_ref,
    query_ref,
    consts_ref,
    factor_ref,
):
    swap_ref[144:656] = pair_ref[...]
    factor_ref[0:32] = wl_ref[...]
    factor_ref[32:64] = wr_ref[...]
    consts_ref[...] = jnp.where(iota((8, 128), 0) == 0, bias_ref[...], pair_gain_ref[...])
    seqs, length, _ = act_ref.shape
    kinds = emb_ref.shape[1]
    emb = emb_ref[...]
    rows = []
    for s in range(seqs):
        picked = one_where(iota((kinds, length), 0) == tok_ref[s : s + 1, :])
        rows.append(act_ref[s].astype(F32) + dot(picked, emb, 0, 1))
    normed = layer_normalize(jnp.concatenate(rows, 0), gain_ref[...]).astype(BF16)
    row, lane = iota((64, 128), 0), iota((64, 128), 1)
    packed = dot(normed[:128], one_where(lane == row)) + dot(normed[128:], one_where(lane == row + 64))
    swap_ref[0:128] = packed.astype(BF16)

    normed = layer_normalize(nodes_ref[...].astype(F32), node_gain_ref[...]).astype(BF16)
    query_ref[...] = dot(wq_ref[...], normed, 0, 1).astype(BF16).astype(F32)
    kv = dot(normed, dot(wk_ref[...], one_where(lane == row)).astype(BF16))
    kv = kv + dot(normed, dot(wv_ref[...], one_where(lane == row + 64)).astype(BF16))
    rest = coords_ref[...]
    placed = jnp.zeros((8, 128), F32)
    for part in range(3):
        piece = rest.astype(BF16)
        rest = rest - piece.astype(F32)
        spot = one_where(iota((3, 128), 1) == iota((3, 128), 0) * 3 + part)
        placed = placed + dot(piece, spot, 0, 0)
    swap_ref[128:144] = jnp.concatenate([kv, placed], 0).astype(BF16)


def own_spread_kernel(pair_ref, block_ref, factor_ref, out_ref):
    out_ref[:, 48:64] = pair_ref[...]
    spread_kernel(block_ref, factor_ref, out_ref)


def spread_kernel(block_ref, factor_ref, out_ref):
    packed = block_ref[0:128]
    row, lane = iota((128, 64), 0), iota((128, 64), 1)
    parts = [dot(packed, one_where(row == lane)), dot(packed, one_where(row == lane + 64))]
    plane = jnp.concatenate(parts, 0).astype(BF16)

    row, source = iota((128, 1), 0), iota((128, 256), 1)
    low, even = lane_masks(8)
    for core in range(2):
        pick = one_where(source == ((row >> 5) << 6) + ((row & 31) << 1) + core)
        rows = dot(pick, plane).astype(BF16)
        left = dot(factor_ref[0:32], rows, 1, 1).astype(BF16).astype(F32)
        parts = swap_lane_groups([left[k * 8 : (k + 1) * 8] for k in range(4)], low, even)
        block = jnp.concatenate(parts, 0).astype(BF16)
        for to in range(32):
            if (to // 4) % 2 == core:
                out_ref[to, 0:32] = block

    nodes = block_ref[128:144].astype(F32)
    widened = dot(factor_ref[32:64], one_where(iota((32, 128), 1) == iota((32, 128), 0) + 32), 0, 0).astype(BF16)
    row, source = iota((256, 1), 0), iota((256, 256), 1)
    wanted = (((row >> 1) & 3) << 6) + ((row >> 3) << 1) + (row & 1)
    moved = dot(one_where(source == wanted), plane).astype(BF16)
    right = dot(moved, widened).reshape(32, 8, 128) + nodes[None, 8:16]
    kv = jnp.broadcast_to(nodes[None, 0:8], (32, 8, 128))
    out_ref[:, 32:48] = jnp.concatenate([kv, right], 1).astype(BF16)


def right_kernel(own_ref, came_ref, out_ref, token_ref):
    token_ref[...] = jnp.zeros_like(token_ref)
    row, source = iota((128, 1), 0), iota((128, 512), 1)
    start = ((row >> 2) << 4) + ((row & 3) << 1) + 8
    at, lane = iota((128, 128), 0), iota((128, 128), 1)
    total = jnp.zeros((128, 128), F32)
    for plane, got_ref in enumerate((own_ref, came_ref)):
        rows = got_ref[:, 32:48].reshape(512, 128)
        for column in range(2):
            picked = dot(one_where(source == start + column), rows).astype(BF16)
            shift = (plane * 2 + column) * 32
            keep = (lane >= shift) & (lane < shift + 32)
            total = total + dot(picked, one_where((at + shift == lane + 32) & keep))
    out_ref[...] = jnp.broadcast_to(total.astype(BF16)[None], out_ref.shape)


def left_kernel(after_ref, own_ref, came_ref, out_ref, left):
    row = iota((256, 1), 0)
    wanted = (((row >> 2) & 7) << 5) + ((row & 3) << 3) + (row >> 5)
    turn = one_where(iota((256, 256), 1) == wanted)
    for p, got_ref in enumerate((own_ref, came_ref)):
        for g in range(4):
            part = dot(turn, got_ref[g * 8 : (g + 1) * 8, 0:32].reshape(256, 128))
            at = p * 128 + g * 32
            for q in range(8):
                left[at : at + 32, q * 128 : (q + 1) * 128] = part[q * 32 : (q + 1) * 32]
    for q in range(8):
        out_ref[q * 128 : (q + 1) * 128] = left[:, q * 128 : (q + 1) * 128].T.astype(BF16)


def outer_kernel(
    place_ref, own_ref, other_ref, right_in, came_ref, weight_ref, out_ref, right, joined, update, weight
):
    weight[...] = jnp.zeros_like(weight)
    for q in range(8):
        for k in range(4):
            block = weight_ref[(k * 8 + q) * 32 : (k * 8 + q) * 32 + 32]
            for j in range(4):
                at = (q * 4 + k) * 128 + j * 32
                weight[at : at + 32, j * 128 : (j + 1) * 128] = block
    low, _ = lane_masks(128)
    for t in range(4):
        a, b = right_in[2 * t].astype(F32), right_in[2 * t + 1].astype(F32)
        right[0:128, t * 128 : (t + 1) * 128] = jnp.where(low, a, pltpu.roll(b, 64, 1)).astype(BF16)
        right[128:256, t * 128 : (t + 1) * 128] = jnp.where(low, pltpu.roll(a, 64, 1), b).astype(BF16)
    for n, left in enumerate((own_ref, other_ref)):
        for q in range(8):
            product = (dot(left[q * 128 : (q + 1) * 128], right[...]) * (1.0 / 256.0)).astype(BF16)
            for t in range(4):
                for k in range(4):
                    at, to = (q * 4 + k) * 128, (n * 4 + t) * 32
                    joined[to : to + 32, at : at + 128] = product[
                        k * 32 : (k + 1) * 32, t * 128 : (t + 1) * 128
                    ]
    out_ref[:, 32:48] = came_ref[144:656].reshape(32, 16, 128)
    rows = dot(joined[...], weight[...])
    for t in range(8):
        for j in range(4):
            update[:, t * 4 + j, :] = rows[t * 32 : (t + 1) * 32, j * 128 : (j + 1) * 128]
    core = place_ref[0]
    out_ref[:, pl.ds(pl.multiple_of(core * 16, 16), 16)] = update[:, 0:16].astype(BF16)
    out_ref[:, pl.ds(pl.multiple_of((1 - core) * 16, 16), 16)] = update[:, 16:32].astype(BF16)


def attend_kernel(
    half_ref, own_ref, got_ref, consts_ref, wq_ref, wk_ref, wv_ref, wg_ref, wo_ref, out_ref, q_s, k_s, v_s, mid_s, gate_s, done_s
):
    mine = half_ref[0] == 0
    factor = 32 ** (-0.5) * math.log2(math.e)
    head_of = iota((512, 128), 1) // 32
    zero, one = jnp.zeros((512, 128), BF16), jnp.ones((512, 128), BF16)
    row, source = iota((512, 1), 0), iota((512, 512), 1)
    turn = one_where(source == (((row >> 1) & 31) << 4) + ((row >> 6) << 1) + (row & 1))
    shares = got_ref[:, 0:32].reshape(32, 2, 16, 128)
    updates = jnp.concatenate([shares[:, p].reshape(512, 128) for p in range(2)], 1)
    updates = dot(turn, updates)
    for p in range(2):
        update = updates[:, p * 128 : (p + 1) * 128]
        own = own_ref[:, 48:64].reshape(32, 2, 8, 128)[:, p].astype(F32)
        came = got_ref[:, 32:48].reshape(32, 2, 8, 128)[:, p].astype(F32)
        pair = [jnp.where(mine, own, came)[:, None], jnp.where(mine, came, own)[:, None]]
        pair_mid = update + jnp.concatenate(pair, 1).reshape(512, 128) + consts_ref[0:1]
        pair_mid = pair_mid.astype(BF16).astype(F32)
        normed = layer_normalize(pair_mid, consts_ref[1:2])
        split = pair_mid.reshape(32, 2, 8, 128)
        mid_s[...] = jnp.where(mine, split[:, 0], split[:, 1]).reshape(256, 128)
        split = normed.reshape(32, 2, 8, 128)
        asking = jnp.where(mine, split[:, 0], split[:, 1]).reshape(256, 128).astype(BF16)
        normed = normed.astype(BF16)
        asked = dot(asking, jnp.concatenate([wq_ref[...], wg_ref[...]], 1))
        q_s[...] = asked[:, :128].astype(BF16)
        gate_s[...] = asked[:, 128:]
        given = dot(normed, jnp.concatenate([wk_ref[...], wv_ref[...]], 1)).astype(BF16)
        keys, values = given[:, :128], given[:, 128:]
        head_keys = [jnp.where(head_of == h, keys, zero) for h in range(PAIR_HEADS)]
        head_values = [
            jnp.concatenate(
                [jnp.where(head_of == h, values, zero), jnp.where(head_of == h, one, zero)], 1
            )
            for h in range(PAIR_HEADS)
        ]
        queries = q_s[...]
        total = jnp.zeros((256, 256), F32)
        for h in range(PAIR_HEADS):
            scores = dot(queries, head_keys[h], 1, 1)
            top = jnp.max(scores, -1, keepdims=True)
            weights = jnp.exp2((scores - top) * factor).astype(BF16)
            total = total + dot(weights, head_values[h])
        attended = total[:, :128] / total[:, 128:] * jax.nn.sigmoid(gate_s[...])
        result = mid_s[...] + dot(attended.astype(BF16), wo_ref[...])
        done_s[:, p * 8 : (p + 1) * 8] = result.reshape(32, 8, 128)
    out_ref[...] = done_s[...].astype(BF16)


def node_kernel(
    count_ref, half_ref, after_ref, own_ref, came_ref, index_ref, query_ref, nodes_ref, coords_ref, wo_ref, penalty_ref, step_ref, nodes_out, coords_out, token_ref
):
    token_ref[...] = after_ref[...]
    tables = [[], []]
    for got_ref in (own_ref, came_ref):
        both = got_ref[:, 32:48].reshape(32, 2, 8, 128)
        for n in range(2):
            tables[n].append(both[:, n].reshape(256, 128))
    kv_table, place_table = [jnp.concatenate(t, 0) for t in tables]
    index = index_ref[...]
    index = ((index >> 4) << 3) + (index & 7) + ((((index >> 3) & 1) ^ half_ref[0]) << 8)
    local, slots = index_ref.shape
    width, dim = nodes_ref.shape[1], nodes_ref.shape[1] // NODE_HEADS
    lane = iota((1, slots), 1)
    spot = iota((1, local), 1)
    mixed = jnp.zeros((width, local), F32)
    moved = jnp.zeros((3, local), F32)
    for i in range(local):
        picked = one_where(iota((512, slots), 0) == index[i : i + 1, :])
        near = dot(kv_table, picked, 0, 0)
        where = dot(place_table, picked, 0, 0)
        position = [
            where[3 * c : 3 * c + 1] + where[3 * c + 1 : 3 * c + 2] + where[3 * c + 2 : 3 * c + 3]
            for c in range(3)
        ]
        offsets = jnp.concatenate(position, 0) - coords_ref[:, i : i + 1]
        dist2 = jnp.sum(offsets * offsets, 0, keepdims=True)
        products = near[:width] * query_ref[:, i : i + 1]
        logits = jnp.sum(products.reshape(NODE_HEADS, dim, slots), 1) * dim ** (-0.5)
        logits = logits - penalty_ref[...] * dist2
        valid = lane < count_ref[i]
        logits = jnp.where(valid, logits, -1e30)
        powers = jnp.exp(logits - jnp.max(logits, -1, keepdims=True))
        weight = powers / jnp.sum(powers, -1, keepdims=True)
        weight = jnp.where(valid, weight, 0.0)
        low = weight.astype(BF16).astype(F32)
        spread = jnp.broadcast_to(low[:, None, :], (NODE_HEADS, dim, slots)).reshape(width, slots)
        column = jnp.sum(near[width:] * spread, -1, keepdims=True)
        mixed = mixed + jnp.where(spot == i, column, 0.0)
        pull = jnp.sum(weight * step_ref[...], 0, keepdims=True)
        moved = moved + jnp.where(spot == i, jnp.sum(offsets * pull, -1, keepdims=True), 0.0)
    out = nodes_ref[...].astype(F32) + dot(mixed.astype(BF16), wo_ref[...], 0, 0)
    nodes_out[...] = out.astype(BF16)
    coords_out[...] = coords_ref[...] + moved


def with_fetch(body, count):
    def kernel(*refs):
        sources, held, sems = refs[:count], refs[-count - 1 : -1], refs[-1]
        copies = [pltpu.make_async_copy(sources[i], held[i], sems.at[i]) for i in range(count)]
        for copy in copies:
            copy.start()
        for copy in copies:
            copy.wait()
        body(*held, *refs[count : -count - 1])

    return kernel


def call(body, out_shape, args, scratch=(), fetch=False, hbm=0, cost=None):
    scratch, args = list(scratch), list(args)
    if fetch:
        body = with_fetch(body, len(args))
        scratch += [pltpu.VMEM(a.shape, a.dtype) for a in args] + [pltpu.SemaphoreType.DMA((len(args),))]
        hbm = len(args)
    first = len(args) - hbm
    args = args[:first] + [pltpu.with_memory_space_constraint(a, pltpu.HBM) for a in args[first:]]
    spaces = [pltpu.SMEM if a.ndim == 1 else pltpu.VMEM for a in args[:first]] + [pltpu.HBM] * hbm
    return pl.pallas_call(
        body,
        out_shape=out_shape,
        in_specs=[pl.BlockSpec(memory_space=s) for s in spaces],
        out_specs=jax.tree.map(lambda _: pl.BlockSpec(memory_space=pltpu.VMEM), out_shape),
        scratch_shapes=scratch,
        compiler_params=pltpu.CompilerParams(vmem_limit_bytes=VMEM_LIMIT),
        cost_estimate=cost,
    )(*args)


def shape(dims, kind=BF16):
    return jax.ShapeDtypeStruct(dims, kind)


def on_device(
    homolog_activations,
    alignment_token_ids,
    symbol_lookup_matrix,
    homolog_rescale_vector,
    first_operand_projection,
    second_operand_projection,
    outer_output_weight,
    outer_bias,
    pair,
    pair_norm_gain,
    pair_query_weight,
    pair_key_weight,
    pair_value_weight,
    pair_gate_weight,
    pair_output_weight,
    nodes,
    coords,
    neighbour_index,
    neighbour_count,
    node_norm_gain,
    node_query_weight,
    node_key_weight,
    node_value_weight,
    node_output_weight,
    distance_penalty,
    coordinate_step,
):
    half = lax.axis_index("zh").reshape(1).astype(jnp.int32)
    swap, node_query, consts, factors = call(
        first_kernel,
        (shape((656, 128)), shape((64, 8), F32), shape((8, 128), F32), shape((64, 64))),
        (
            homolog_activations,
            alignment_token_ids,
            symbol_lookup_matrix.T,
            homolog_rescale_vector.reshape(1, -1),
            nodes,
            coords,
            node_norm_gain.reshape(1, -1),
            node_query_weight,
            node_key_weight,
            node_value_weight,
            outer_bias.reshape(1, -1),
            pair_norm_gain.reshape(1, -1),
            pair.reshape(512, 128),
            first_operand_projection.T,
            second_operand_projection.T,
        ),
        fetch=True,
    )
    swapped = lax.ppermute(swap, "zh", [(0, 1), (1, 0)])
    spread = call(own_spread_kernel, shape((32, 64, 128)), (pair.reshape(32, 16, 128), swap, factors))
    own = lax.all_to_all(spread, PLANE, split_axis=0, concat_axis=0, tiled=True)
    long = pl.CostEstimate(flops=1 << 36, bytes_accessed=1 << 28, transcendentals=0)
    spread = call(spread_kernel, shape((32, 48, 128)), (swapped, factors), cost=long)
    got = lax.all_to_all(spread, PLANE, split_axis=0, concat_axis=0, tiled=True)
    right, token = call(right_kernel, (shape((8, 128, 128)), shape((8, 128), F32)), (own, got))
    right = lax.all_to_all(right, "row", split_axis=0, concat_axis=0, tiled=True)
    nodes_out, coords_out, token = call(
        node_kernel,
        (shape(nodes.shape), shape(coords.shape, F32), shape((8, 128), F32)),
        (
            neighbour_count,
            half,
            token,
            own,
            got,
            neighbour_index,
            node_query,
            nodes,
            coords,
            node_output_weight,
            distance_penalty.reshape(-1, 1),
            coordinate_step.reshape(-1, 1),
        ),
    )
    left = call(
        left_kernel, shape((1024, 256)), (token, own, got), scratch=(pltpu.VMEM((256, 1024), F32),)
    )
    other = lax.ppermute(left, "core", [(0, 1), (1, 0)])
    place = lax.axis_index("core").reshape(1).astype(jnp.int32)
    rows = call(
        outer_kernel,
        shape((32, 48, 128)),
        (place, left, other, right, swapped, outer_output_weight),
        scratch=(
            pltpu.VMEM((256, 512), BF16),
            pltpu.VMEM((256, 4096), BF16),
            pltpu.VMEM((32, 32, 128), F32),
            pltpu.VMEM((4096, 512), BF16),
        ),
    )
    rows = lax.all_to_all(rows, PLANE, split_axis=0, concat_axis=0, tiled=True)
    done = call(
        attend_kernel,
        shape((32, 16, 128)),
        (
            half,
            own,
            rows,
            consts,
            pair_query_weight,
            pair_key_weight,
            pair_value_weight,
            pair_gate_weight,
            pair_output_weight,
        ),
        scratch=(
            pltpu.VMEM((256, 128), BF16),
            pltpu.VMEM((512, 128), BF16),
            pltpu.VMEM((512, 128), BF16),
            pltpu.VMEM((256, 128), F32),
            pltpu.VMEM((256, 128), F32),
            pltpu.VMEM((32, 16, 128), F32),
        ),
    )
    done = lax.all_to_all(done, PLANE, split_axis=0, concat_axis=0, tiled=True)
    pair_out = done.reshape(pair.shape)
    return (pair_out, nodes_out, coords_out)


def solution(mesh):
    fine = Mesh(mesh.devices.reshape(4, 2, 8, 4, 2), ("x", "core", "row", "y", "zh"))
    placed = (
        P(GROUP, "row", None),
        P(GROUP, "row"),
        P(),
        P(),
        P(),
        P(),
        P(),
        P(),
        P("row", GROUP, None),
        P(),
        P(),
        P(),
        P(),
        P(),
        P(),
        P(GROUP, None),
        P(None, GROUP),
        P(GROUP, None),
        P(GROUP),
        P(),
        P(),
        P(),
        P(),
        P(),
        P(),
        P(),
    )
    return jax.shard_map(
        on_device,
        mesh=fine,
        in_specs=placed,
        out_specs=(
            P("row", GROUP, None),
            P(GROUP, None),
            P(None, GROUP),
        ),
        check_vma=False,
    )
```

```python
import math

import jax
import jax.numpy as jnp
from jax import lax
from jax.experimental import pallas as pl
from jax.experimental.pallas import tpu as pltpu
from jax.sharding import Mesh, PartitionSpec as P

F32 = jnp.float32
BF16 = jnp.bfloat16
PAIR_HEADS = 4
NODE_HEADS = 4
PLANE = ("x", "core", "y")
GROUP = ("x", "core", "y", "zh")
VMEM_LIMIT = 24 * 1024 * 1024


def dot(a, b, ca=1, cb=0):
    return lax.dot_general(a, b, (((ca,), (cb,)), ((), ())), preferred_element_type=F32)


def iota(shape, dim):
    return lax.broadcasted_iota(jnp.int32, shape, dim)


def one_where(mask):
    return jnp.where(mask, 1.0, 0.0).astype(BF16)


def layer_normalize(values_in, gain):
    average = jnp.mean(values_in, -1, keepdims=True)
    centred = values_in - average
    variance = jnp.mean(centred * centred, -1, keepdims=True)
    return centred * lax.rsqrt(variance + 1e-05) * gain


def swap_lane_groups(v, low, even):
    t0 = jnp.where(low, v[0], pltpu.roll(v[2], 64, 1))
    t2 = jnp.where(low, pltpu.roll(v[0], 64, 1), v[2])
    t1 = jnp.where(low, v[1], pltpu.roll(v[3], 64, 1))
    t3 = jnp.where(low, pltpu.roll(v[1], 64, 1), v[3])
    return (
        jnp.where(even, t0, pltpu.roll(t1, 32, 1)),
        jnp.where(even, pltpu.roll(t0, 96, 1), t1),
        jnp.where(even, t2, pltpu.roll(t3, 32, 1)),
        jnp.where(even, pltpu.roll(t2, 96, 1), t3),
    )


def lane_masks(rows):
    lane = iota((rows, 128), 1)
    return lane < 64, (lane // 32) % 2 == 0


def first_kernel(
    act_ref,
    tok_ref,
    emb_ref,
    gain_ref,
    nodes_ref,
    coords_ref,
    node_gain_ref,
    wq_ref,
    wk_ref,
    wv_ref,
    bias_ref,
    pair_gain_ref,
    pair_ref,
    wl_ref,
    wr_ref,
    swap_ref,
    query_ref,
    consts_ref,
    factor_ref,
):
    swap_ref[144:656] = pair_ref[...]
    factor_ref[0:32] = wl_ref[...]
    factor_ref[32:64] = wr_ref[...]
    consts_ref[...] = jnp.where(iota((8, 128), 0) == 0, bias_ref[...], pair_gain_ref[...])
    seqs, length, _ = act_ref.shape
    kinds = emb_ref.shape[1]
    emb = emb_ref[...]
    rows = []
    for s in range(seqs):
        picked = one_where(iota((kinds, length), 0) == tok_ref[s : s + 1, :])
        rows.append(act_ref[s].astype(F32) + dot(picked, emb, 0, 1))
    normed = layer_normalize(jnp.concatenate(rows, 0), gain_ref[...]).astype(BF16)
    row, lane = iota((64, 128), 0), iota((64, 128), 1)
    packed = dot(normed[:128], one_where(lane == row)) + dot(normed[128:], one_where(lane == row + 64))
    swap_ref[0:128] = packed.astype(BF16)

    normed = layer_normalize(nodes_ref[...].astype(F32), node_gain_ref[...]).astype(BF16)
    query_ref[...] = dot(wq_ref[...], normed, 0, 1).astype(BF16).astype(F32)
    kv = dot(normed, dot(wk_ref[...], one_where(lane == row)).astype(BF16))
    kv = kv + dot(normed, dot(wv_ref[...], one_where(lane == row + 64)).astype(BF16))
    rest = coords_ref[...]
    placed = jnp.zeros((8, 128), F32)
    for part in range(3):
        piece = rest.astype(BF16)
        rest = rest - piece.astype(F32)
        spot = one_where(iota((3, 128), 1) == iota((3, 128), 0) * 3 + part)
        placed = placed + dot(piece, spot, 0, 0)
    swap_ref[128:144] = jnp.concatenate([kv, placed], 0).astype(BF16)


def own_spread_kernel(pair_ref, block_ref, factor_ref, out_ref):
    out_ref[:, 48:64] = pair_ref[...]
    spread_kernel(block_ref, factor_ref, out_ref)


def spread_kernel(block_ref, factor_ref, out_ref):
    packed = block_ref[0:128]
    row, lane = iota((128, 64), 0), iota((128, 64), 1)
    parts = [dot(packed, one_where(row == lane)), dot(packed, one_where(row == lane + 64))]
    plane = jnp.concatenate(parts, 0).astype(BF16)

    row, source = iota((128, 1), 0), iota((128, 256), 1)
    low, even = lane_masks(8)
    for core in range(2):
        pick = one_where(source == ((row >> 5) << 6) + ((row & 31) << 1) + core)
        rows = dot(pick, plane).astype(BF16)
        left = dot(factor_ref[0:32], rows, 1, 1).astype(BF16).astype(F32)
        parts = swap_lane_groups([left[k * 8 : (k + 1) * 8] for k in range(4)], low, even)
        block = jnp.concatenate(parts, 0).astype(BF16)
        for to in range(32):
            if (to // 4) % 2 == core:
                out_ref[to, 0:32] = block

    nodes = block_ref[128:144].astype(F32)
    widened = dot(factor_ref[32:64], one_where(iota((32, 128), 1) == iota((32, 128), 0) + 32), 0, 0).astype(BF16)
    row, source = iota((256, 1), 0), iota((256, 256), 1)
    wanted = (((row >> 1) & 3) << 6) + ((row >> 3) << 1) + (row & 1)
    moved = dot(one_where(source == wanted), plane).astype(BF16)
    right = dot(moved, widened).reshape(32, 8, 128) + nodes[None, 8:16]
    kv = jnp.broadcast_to(nodes[None, 0:8], (32, 8, 128))
    out_ref[:, 32:48] = jnp.concatenate([kv, right], 1).astype(BF16)


def right_kernel(own_ref, came_ref, out_ref, token_ref):
    token_ref[...] = jnp.zeros_like(token_ref)
    row, source = iota((64, 1), 0), iota((64, 128), 1)
    turn = one_where(source == (((row >> 2) & 7) << 4) + ((row & 3) << 1) + (row >> 5) + 8)
    at, lane = iota((128, 128), 0), iota((128, 128), 1)
    total = jnp.zeros((128, 128), F32)
    for plane, got_ref in enumerate((own_ref, came_ref)):
        rows = got_ref[:, 32:48].reshape(512, 128)
        parts = [dot(turn, rows[g * 128 : (g + 1) * 128]).astype(BF16) for g in range(4)]
        for column in range(2):
            picked = jnp.concatenate([part[column * 32 : column * 32 + 32] for part in parts], 0)
            shift = (plane * 2 + column) * 32
            keep = (lane >= shift) & (lane < shift + 32)
            total = total + dot(picked, one_where((at + shift == lane + 32) & keep))
    out_ref[...] = jnp.broadcast_to(total.astype(BF16)[None], out_ref.shape)


def left_kernel(after_ref, own_ref, came_ref, out_ref, left):
    row = iota((256, 1), 0)
    wanted = (((row >> 2) & 7) << 5) + ((row & 3) << 3) + (row >> 5)
    turn = one_where(iota((256, 256), 1) == wanted)
    for p, got_ref in enumerate((own_ref, came_ref)):
        for g in range(4):
            part = dot(turn, got_ref[g * 8 : (g + 1) * 8, 0:32].reshape(256, 128))
            at = p * 128 + g * 32
            for q in range(8):
                left[at : at + 32, q * 128 : (q + 1) * 128] = part[q * 32 : (q + 1) * 32]
    for q in range(8):
        out_ref[q * 128 : (q + 1) * 128] = left[:, q * 128 : (q + 1) * 128].T.astype(BF16)


def outer_kernel(
    place_ref, own_ref, other_ref, right_in, came_ref, weight_ref, out_ref, right, joined, update, weight
):
    weight[...] = jnp.zeros_like(weight)
    for q in range(8):
        for k in range(4):
            block = weight_ref[(k * 8 + q) * 32 : (k * 8 + q) * 32 + 32]
            for j in range(4):
                at = (q * 4 + k) * 128 + j * 32
                weight[at : at + 32, j * 128 : (j + 1) * 128] = block
    low, _ = lane_masks(128)
    for t in range(4):
        a, b = right_in[2 * t].astype(F32), right_in[2 * t + 1].astype(F32)
        right[0:128, t * 128 : (t + 1) * 128] = jnp.where(low, a, pltpu.roll(b, 64, 1)).astype(BF16)
        right[128:256, t * 128 : (t + 1) * 128] = jnp.where(low, pltpu.roll(a, 64, 1), b).astype(BF16)
    for n, left in enumerate((own_ref, other_ref)):
        for q in range(8):
            product = (dot(left[q * 128 : (q + 1) * 128], right[...]) * (1.0 / 256.0)).astype(BF16)
            for t in range(4):
                for k in range(4):
                    at, to = (q * 4 + k) * 128, (n * 4 + t) * 32
                    joined[to : to + 32, at : at + 128] = product[
                        k * 32 : (k + 1) * 32, t * 128 : (t + 1) * 128
                    ]
    out_ref[:, 32:48] = came_ref[144:656].reshape(32, 16, 128)
    rows = dot(joined[...], weight[...])
    for t in range(8):
        for j in range(4):
            update[:, t * 4 + j, :] = rows[t * 32 : (t + 1) * 32, j * 128 : (j + 1) * 128]
    core = place_ref[0]
    out_ref[:, pl.ds(pl.multiple_of(core * 16, 16), 16)] = update[:, 0:16].astype(BF16)
    out_ref[:, pl.ds(pl.multiple_of((1 - core) * 16, 16), 16)] = update[:, 16:32].astype(BF16)


def attend_kernel(
    half_ref, own_ref, got_ref, consts_ref, wq_ref, wk_ref, wv_ref, wg_ref, wo_ref, out_ref, q_s, k_s, v_s, mid_s, gate_s, done_s
):
    mine = half_ref[0] == 0
    factor = 32 ** (-0.5) * math.log2(math.e)
    head_of = iota((512, 128), 1) // 32
    zero, one = jnp.zeros((512, 128), BF16), jnp.ones((512, 128), BF16)
    row, source = iota((512, 1), 0), iota((512, 512), 1)
    turn = one_where(source == (((row >> 1) & 31) << 4) + ((row >> 6) << 1) + (row & 1))
    shares = got_ref[:, 0:32].reshape(32, 2, 16, 128)
    updates = jnp.concatenate([shares[:, p].reshape(512, 128) for p in range(2)], 1)
    updates = dot(turn, updates)
    for p in range(2):
        update = updates[:, p * 128 : (p + 1) * 128]
        own = own_ref[:, 48:64].reshape(32, 2, 8, 128)[:, p].astype(F32)
        came = got_ref[:, 32:48].reshape(32, 2, 8, 128)[:, p].astype(F32)
        pair = [jnp.where(mine, own, came)[:, None], jnp.where(mine, came, own)[:, None]]
        pair_mid = update + jnp.concatenate(pair, 1).reshape(512, 128) + consts_ref[0:1]
        pair_mid = pair_mid.astype(BF16).astype(F32)
        normed = layer_normalize(pair_mid, consts_ref[1:2])
        split = pair_mid.reshape(32, 2, 8, 128)
        mid_s[...] = jnp.where(mine, split[:, 0], split[:, 1]).reshape(256, 128)
        split = normed.reshape(32, 2, 8, 128)
        asking = jnp.where(mine, split[:, 0], split[:, 1]).reshape(256, 128).astype(BF16)
        normed = normed.astype(BF16)
        asked = dot(asking, jnp.concatenate([wq_ref[...], wg_ref[...]], 1))
        q_s[...] = asked[:, :128].astype(BF16)
        gate_s[...] = asked[:, 128:]
        given = dot(normed, jnp.concatenate([wk_ref[...], wv_ref[...]], 1)).astype(BF16)
        keys, values = given[:, :128], given[:, 128:]
        head_keys = [jnp.where(head_of == h, keys, zero) for h in range(PAIR_HEADS)]
        head_values = [
            jnp.concatenate(
                [jnp.where(head_of == h, values, zero), jnp.where(head_of == h, one, zero)], 1
            )
            for h in range(PAIR_HEADS)
        ]
        queries = q_s[...]
        total = jnp.zeros((256, 256), F32)
        for h in range(PAIR_HEADS):
            scores = dot(queries, head_keys[h], 1, 1)
            top = jnp.max(scores, -1, keepdims=True)
            weights = jnp.exp2((scores - top) * factor).astype(BF16)
            total = total + dot(weights, head_values[h])
        attended = total[:, :128] / total[:, 128:] * jax.nn.sigmoid(gate_s[...])
        result = mid_s[...] + dot(attended.astype(BF16), wo_ref[...])
        done_s[:, p * 8 : (p + 1) * 8] = result.reshape(32, 8, 128)
    out_ref[...] = done_s[...].astype(BF16)


def node_kernel(
    count_ref, half_ref, after_ref, own_ref, came_ref, index_ref, query_ref, nodes_ref, coords_ref, wo_ref, penalty_ref, step_ref, nodes_out, coords_out, token_ref
):
    token_ref[...] = after_ref[...]
    tables = [[], []]
    for got_ref in (own_ref, came_ref):
        both = got_ref[:, 32:48].reshape(32, 2, 8, 128)
        for n in range(2):
            tables[n].append(both[:, n].reshape(256, 128))
    kv_table, place_table = [jnp.concatenate(t, 0) for t in tables]
    index = index_ref[...]
    index = ((index >> 4) << 3) + (index & 7) + ((((index >> 3) & 1) ^ half_ref[0]) << 8)
    local, slots = index_ref.shape
    width, dim = nodes_ref.shape[1], nodes_ref.shape[1] // NODE_HEADS
    lane = iota((1, slots), 1)
    spot = iota((1, local), 1)
    mixed = jnp.zeros((width, local), F32)
    moved = jnp.zeros((3, local), F32)
    for i in range(local):
        picked = one_where(iota((512, slots), 0) == index[i : i + 1, :])
        near = dot(kv_table, picked, 0, 0)
        where = dot(place_table, picked, 0, 0)
        position = [
            where[3 * c : 3 * c + 1] + where[3 * c + 1 : 3 * c + 2] + where[3 * c + 2 : 3 * c + 3]
            for c in range(3)
        ]
        offsets = jnp.concatenate(position, 0) - coords_ref[:, i : i + 1]
        dist2 = jnp.sum(offsets * offsets, 0, keepdims=True)
        products = near[:width] * query_ref[:, i : i + 1]
        logits = jnp.sum(products.reshape(NODE_HEADS, dim, slots), 1) * dim ** (-0.5)
        logits = logits - penalty_ref[...] * dist2
        valid = lane < count_ref[i]
        logits = jnp.where(valid, logits, -1e30)
        powers = jnp.exp(logits - jnp.max(logits, -1, keepdims=True))
        weight = powers / jnp.sum(powers, -1, keepdims=True)
        weight = jnp.where(valid, weight, 0.0)
        low = weight.astype(BF16).astype(F32)
        spread = jnp.broadcast_to(low[:, None, :], (NODE_HEADS, dim, slots)).reshape(width, slots)
        column = jnp.sum(near[width:] * spread, -1, keepdims=True)
        mixed = mixed + jnp.where(spot == i, column, 0.0)
        pull = jnp.sum(weight * step_ref[...], 0, keepdims=True)
        moved = moved + jnp.where(spot == i, jnp.sum(offsets * pull, -1, keepdims=True), 0.0)
    out = nodes_ref[...].astype(F32) + dot(mixed.astype(BF16), wo_ref[...], 0, 0)
    nodes_out[...] = out.astype(BF16)
    coords_out[...] = coords_ref[...] + moved


def with_fetch(body, count):
    def kernel(*refs):
        sources, held, sems = refs[:count], refs[-count - 1 : -1], refs[-1]
        copies = [pltpu.make_async_copy(sources[i], held[i], sems.at[i]) for i in range(count)]
        for copy in copies:
            copy.start()
        for copy in copies:
            copy.wait()
        body(*held, *refs[count : -count - 1])

    return kernel


def call(body, out_shape, args, scratch=(), fetch=False, hbm=0, cost=None):
    scratch, args = list(scratch), list(args)
    if fetch:
        body = with_fetch(body, len(args))
        scratch += [pltpu.VMEM(a.shape, a.dtype) for a in args] + [pltpu.SemaphoreType.DMA((len(args),))]
        hbm = len(args)
    first = len(args) - hbm
    args = args[:first] + [pltpu.with_memory_space_constraint(a, pltpu.HBM) for a in args[first:]]
    spaces = [pltpu.SMEM if a.ndim == 1 else pltpu.VMEM for a in args[:first]] + [pltpu.HBM] * hbm
    return pl.pallas_call(
        body,
        out_shape=out_shape,
        in_specs=[pl.BlockSpec(memory_space=s) for s in spaces],
        out_specs=jax.tree.map(lambda _: pl.BlockSpec(memory_space=pltpu.VMEM), out_shape),
        scratch_shapes=scratch,
        compiler_params=pltpu.CompilerParams(vmem_limit_bytes=VMEM_LIMIT),
        cost_estimate=cost,
    )(*args)


def shape(dims, kind=BF16):
    return jax.ShapeDtypeStruct(dims, kind)


def on_device(
    homolog_activations,
    alignment_token_ids,
    symbol_lookup_matrix,
    homolog_rescale_vector,
    first_operand_projection,
    second_operand_projection,
    outer_output_weight,
    outer_bias,
    pair,
    pair_norm_gain,
    pair_query_weight,
    pair_key_weight,
    pair_value_weight,
    pair_gate_weight,
    pair_output_weight,
    nodes,
    coords,
    neighbour_index,
    neighbour_count,
    node_norm_gain,
    node_query_weight,
    node_key_weight,
    node_value_weight,
    node_output_weight,
    distance_penalty,
    coordinate_step,
):
    half = lax.axis_index("zh").reshape(1).astype(jnp.int32)
    swap, node_query, consts, factors = call(
        first_kernel,
        (shape((656, 128)), shape((64, 8), F32), shape((8, 128), F32), shape((64, 64))),
        (
            homolog_activations,
            alignment_token_ids,
            symbol_lookup_matrix.T,
            homolog_rescale_vector.reshape(1, -1),
            nodes,
            coords,
            node_norm_gain.reshape(1, -1),
            node_query_weight,
            node_key_weight,
            node_value_weight,
            outer_bias.reshape(1, -1),
            pair_norm_gain.reshape(1, -1),
            pair.reshape(512, 128),
            first_operand_projection.T,
            second_operand_projection.T,
        ),
        fetch=True,
    )
    swapped = lax.ppermute(swap, "zh", [(0, 1), (1, 0)])
    spread = call(own_spread_kernel, shape((32, 64, 128)), (pair.reshape(32, 16, 128), swap, factors))
    own = lax.all_to_all(spread, PLANE, split_axis=0, concat_axis=0, tiled=True)
    long = pl.CostEstimate(flops=1 << 36, bytes_accessed=1 << 28, transcendentals=0)
    spread = call(spread_kernel, shape((32, 48, 128)), (swapped, factors), cost=long)
    got = lax.all_to_all(spread, PLANE, split_axis=0, concat_axis=0, tiled=True)
    right, token = call(right_kernel, (shape((8, 128, 128)), shape((8, 128), F32)), (own, got))
    right = lax.all_to_all(right, "row", split_axis=0, concat_axis=0, tiled=True)
    nodes_out, coords_out, token = call(
        node_kernel,
        (shape(nodes.shape), shape(coords.shape, F32), shape((8, 128), F32)),
        (
            neighbour_count,
            half,
            token,
            own,
            got,
            neighbour_index,
            node_query,
            nodes,
            coords,
            node_output_weight,
            distance_penalty.reshape(-1, 1),
            coordinate_step.reshape(-1, 1),
        ),
    )
    left = call(
        left_kernel, shape((1024, 256)), (token, own, got), scratch=(pltpu.VMEM((256, 1024), F32),)
    )
    other = lax.ppermute(left, "core", [(0, 1), (1, 0)])
    place = lax.axis_index("core").reshape(1).astype(jnp.int32)
    rows = call(
        outer_kernel,
        shape((32, 48, 128)),
        (place, left, other, right, swapped, outer_output_weight),
        scratch=(
            pltpu.VMEM((256, 512), BF16),
            pltpu.VMEM((256, 4096), BF16),
            pltpu.VMEM((32, 32, 128), F32),
            pltpu.VMEM((4096, 512), BF16),
        ),
    )
    rows = lax.all_to_all(rows, PLANE, split_axis=0, concat_axis=0, tiled=True)
    done = call(
        attend_kernel,
        shape((32, 16, 128)),
        (
            half,
            own,
            rows,
            consts,
            pair_query_weight,
            pair_key_weight,
            pair_value_weight,
            pair_gate_weight,
            pair_output_weight,
        ),
        scratch=(
            pltpu.VMEM((256, 128), BF16),
            pltpu.VMEM((512, 128), BF16),
            pltpu.VMEM((512, 128), BF16),
            pltpu.VMEM((256, 128), F32),
            pltpu.VMEM((256, 128), F32),
            pltpu.VMEM((32, 16, 128), F32),
        ),
    )
    done = lax.all_to_all(done, PLANE, split_axis=0, concat_axis=0, tiled=True)
    pair_out = done.reshape(pair.shape)
    return (pair_out, nodes_out, coords_out)


def solution(mesh):
    fine = Mesh(mesh.devices.reshape(4, 2, 8, 4, 2), ("x", "core", "row", "y", "zh"))
    placed = (
        P(GROUP, "row", None),
        P(GROUP, "row"),
        P(),
        P(),
        P(),
        P(),
        P(),
        P(),
        P("row", GROUP, None),
        P(),
        P(),
        P(),
        P(),
        P(),
        P(),
        P(GROUP, None),
        P(None, GROUP),
        P(GROUP, None),
        P(GROUP),
        P(),
        P(),
        P(),
        P(),
        P(),
        P(),
        P(),
    )
    return jax.shard_map(
        on_device,
        mesh=fine,
        in_specs=placed,
        out_specs=(
            P("row", GROUP, None),
            P(GROUP, None),
            P(None, GROUP),
        ),
        check_vma=False,
    )
```
